32 devices in a mesh: replica: 4 (over z), shard: 8 (over y, x, core).
Axes of the slice: x: 2, y: 2, z: 4, core: 2. Of those that a mesh axis runs over, the one named last changes fastest.
Arguments:
- tokens: bfloat16 [16, 1024, 2048], P('replica', 'shard'), may hold values from -8 to 8
- segments: int32 [16, 1024], P('replica', 'shard'), may hold values from 0 to 6, as said below
- positions: int32 [16, 1024], P('replica', 'shard'), may hold values from 0 to 2047, as said below
- cotangent: bfloat16 [16, 1024, 2048], P('replica', 'shard'), may hold values from -6 to 6
- attention_gain: bfloat16 [2048], P('shard'), may hold values from 0.5 to 1.5
- query_weight: bfloat16 [2048, 2048], P('shard'), may hold values from -6 to 6
- key_weight: bfloat16 [2048, 512], P('shard'), may hold values from -6 to 6
- value_weight: bfloat16 [2048, 512], P('shard'), may hold values from -0.125 to 0.125
- output_weight: bfloat16 [2048, 2048], P('shard'), may hold values from -1.5 to 1.5
- mlp_gain: bfloat16 [2048], P('shard'), may hold values from 0.5 to 1.5
- gate_weight: bfloat16 [2048, 8192], P('shard'), may hold values from -0.125 to 0.125
- up_weight: bfloat16 [2048, 8192], P('shard'), may hold values from -0.125 to 0.125
- down_weight: bfloat16 [8192, 2048], P('shard'), may hold values from -0.0625 to 0.0625
Outputs:
- block_output: bfloat16 [16, 1024, 2048], P('replica', 'shard')
- token_grad: float32 [16, 1024, 2048], P('replica', 'shard')
- attention_gain_grad: float32 [2048], P('shard')
- query_grad: float32 [2048, 2048], P('shard')
- key_grad: float32 [2048, 512], P('shard')
- value_grad: float32 [2048, 512], P('shard')
- output_grad: float32 [2048, 2048], P('shard')
- mlp_gain_grad: float32 [2048], P('shard')
- gate_grad: float32 [2048, 8192], P('shard')
- up_grad: float32 [2048, 8192], P('shard')
- down_grad: float32 [8192, 2048], P('shard')
The draws below stay inside these ranges and needn't reach their ends.
Inputs may be any that keep to these rules, and one draw needn't show every extreme that they name: `segments`: ids never fall along a sequence, are 0 at its first token and rise by one at each document's first token; a document that begins and ends inside a sequence has 204 tokens or more. `positions`: a token's position within its document: it rises by one from token to token of a document and is 0 at a document's first token; a sequence's first document may have begun before the sequence.
All inputs are finite; a program needn't handle non-finite values.
Results may differ from the reference program's by a relative error of at most 0.023.
The reference program's roundings to bfloat16 on the way count: a program that leaves them out, or rounds other values in their place, can miss the bound.
Values may be sent and summed in bfloat16 or wider, within the bound.
A program may use at most 512 MiB of HBM per device.

```python
import math
import jax
import jax.numpy as jnp
from jax import lax

D = 2048
HEADS = 32
KV_HEADS = 8
HEAD_DIM = 64
FF = 8192
SEQ_LEN = 1024
SEQS = 16


def draw_tokens(key, part):
    base = jax.random.normal(jax.random.fold_in(key, 3), (SEQS, SEQ_LEN, D), jnp.float32)
    return jnp.clip(base, -8.0, 8.0).astype(jnp.bfloat16)


def query_and_key(key):
    group_share = HEADS // KV_HEADS
    key_part = jax.random.normal(jax.random.fold_in(key, 11), (D, KV_HEADS, 1, HEAD_DIM), jnp.float32) * D ** (-0.5)
    query_part = jax.random.normal(jax.random.fold_in(key, 12), (D, KV_HEADS, group_share, HEAD_DIM), jnp.float32) * D ** (-0.5)
    query_rows = jnp.clip(query_part, -6.0, 6.0).reshape(D, HEADS * HEAD_DIM)
    key_rows = jnp.clip(key_part, -6.0, 6.0).reshape(D, KV_HEADS * HEAD_DIM)
    return (query_rows, key_rows)


def draw_query_weight(key, part):
    return query_and_key(key)[0].astype(jnp.bfloat16)


def draw_key_weight(key, part):
    return query_and_key(key)[1].astype(jnp.bfloat16)


def documents(key):
    shortest = max(SEQ_LEN // 5, 1)
    doc_count = 10
    drawn_lengths = jax.random.randint(jax.random.fold_in(key, 21), (SEQS, doc_count), shortest, 2 * SEQ_LEN + 1)
    row_index = jnp.arange(SEQS, dtype=jnp.int32)[:, None]
    col_index = jnp.arange(doc_count, dtype=jnp.int32)[None, :]
    doc_lengths = jnp.where((row_index == 0) & (col_index == 0), 3 * SEQ_LEN, drawn_lengths)
    doc_lengths = jnp.where((row_index == 1) & (col_index > 0), shortest, doc_lengths)
    drawn_offset = jax.random.randint(jax.random.fold_in(key, 22), (SEQS, 1), 0, doc_lengths[:, :1])
    lead_offset = jnp.where(row_index == 0, SEQ_LEN, jnp.where(row_index == 1, doc_lengths[:, :1] - 1, drawn_offset))
    doc_ends = jnp.cumsum(doc_lengths, axis=1) - lead_offset
    doc_starts = doc_ends - doc_lengths
    token_index = jnp.arange(SEQ_LEN, dtype=jnp.int32)
    doc_number = jnp.sum((doc_ends[:, None, :] <= token_index[None, :, None]).astype(jnp.int32), -1)
    picked = doc_number[:, :, None] == jnp.arange(doc_count, dtype=jnp.int32)[None, None, :]
    start_at = jnp.sum(jnp.where(picked, doc_starts[:, None, :], 0), -1)
    return (doc_number.astype(jnp.int32), (token_index[None, :] - start_at).astype(jnp.int32))


def draw_segments(key, part):
    return documents(key)[0]


def draw_positions(key, part):
    return documents(key)[1]


def block_scale(own_key, extent, shards, least, top_value):
    level, own = 1.0, jax.random.fold_in(own_key, 6)
    for dim, shards_of in shards:
        draws = jnp.exp(jax.random.uniform(jax.random.fold_in(own, dim), (shards_of,), jnp.float32, least / len(shards), top_value / len(shards)))
        level = level * jnp.repeat(draws, extent[dim] // shards_of).reshape([-1 if axis == dim else 1 for axis in range(len(extent))])
    return level


def bell_draw(own_key, extent, width, bound, shards=(), held_as=jnp.bfloat16):
    drawn = jax.random.normal(own_key, extent, jnp.float32) * width
    if len(shards) > 0:
        drawn = block_scale(own_key, extent, shards, -0.22, 0.18) * drawn
    return jnp.clip(drawn, min=-bound, max=bound).astype(held_as)


def setup_inputs(seed: int = 0) -> dict:
    splits = jax.random.split(jax.random.key(seed), 14)
    return {
        "tokens": draw_tokens(jax.random.fold_in(splits[13], 71), 0),
        "segments": draw_segments(jax.random.fold_in(splits[13], 71), 0),
        "positions": draw_positions(jax.random.fold_in(splits[13], 71), 0),
        "cotangent": bell_draw(splits[3], (SEQS, SEQ_LEN, D), 1.0, 6.0, ((0, 4), (1, 8))),
        "attention_gain": jnp.clip(1.0 + 0.1 * jax.random.normal(splits[4], (D,), jnp.float32), 0.5, 1.5).astype(jnp.bfloat16),
        "query_weight": draw_query_weight(jax.random.fold_in(splits[13], 71), 0),
        "key_weight": draw_key_weight(jax.random.fold_in(splits[13], 71), 0),
        "value_weight": bell_draw(splits[7], (D, KV_HEADS * HEAD_DIM), D ** -0.5, 0.125, ((0, 8),)),
        "output_weight": bell_draw(splits[8], (HEADS * HEAD_DIM, D), (max(1, HEADS * HEAD_DIM // 128)) ** -0.5, 1.5, ((0, 8),)),
        "mlp_gain": jnp.clip(1.0 + 0.1 * jax.random.normal(splits[9], (D,), jnp.float32), 0.5, 1.5).astype(jnp.bfloat16),
        "gate_weight": bell_draw(splits[10], (D, FF), D ** -0.5, 0.125, ((0, 8),)),
        "up_weight": bell_draw(splits[11], (D, FF), D ** -0.5, 0.125, ((0, 8),)),
        "down_weight": bell_draw(splits[12], (FF, D), FF ** -0.5, 0.0625, ((0, 8),)),
    }


@jax.custom_vjp
def low(v):
    return lax.optimization_barrier(v.astype(jnp.bfloat16)).astype(jnp.float32)

@jax.custom_vjp
def low_back(v):
    return v

def low_keep(v):
    return (low(v), None)

def low_pass(kept, grad):
    return (grad,)

def back_keep(v):
    return (v, None)

def back_low(kept, grad):
    return (low(grad),)
low.defvjp(low_keep, low_pass)
low_back.defvjp(back_keep, back_low)
epsilon = 1e-05
rope_base = 500000.0
masked_score = -1e+30

def rotation(doc_positions):
    freq_index = jnp.arange(HEAD_DIM // 2, dtype=jnp.float32)
    inverse_freq = jnp.exp(freq_index * (-2.0 * math.log(rope_base) / HEAD_DIM))
    angle_all = doc_positions.astype(jnp.float32)[..., None] * inverse_freq
    return (jnp.cos(angle_all)[..., None, :], jnp.sin(angle_all)[..., None, :])

def rotate(values_in, cosine, sine_part):
    half_dim = values_in.shape[-1] // 2
    lower_half = values_in[..., :half_dim]
    upper_half = values_in[..., half_dim:]
    return jnp.concatenate([lower_half * cosine - upper_half * sine_part, upper_half * cosine + lower_half * sine_part], -1)

def matmul(left, right):
    return jnp.dot(left, right, precision=lax.Precision.HIGHEST)

def layer(inputs_f, attention_gain, query_weight, key_weight, value_weight, output_weight, mlp_gain, gate_weight, up_weight, down_weight, doc_ids, doc_positions):
    seq_rows = inputs_f.shape[0]
    group_share = HEADS // KV_HEADS
    scale_first = lax.rsqrt(lax.optimization_barrier(jnp.mean(inputs_f * inputs_f, -1, keepdims=True)) + epsilon)
    normed_first = low(inputs_f * scale_first * attention_gain)
    queries = low_back(matmul(normed_first, query_weight)).reshape(seq_rows, HEADS, HEAD_DIM)
    key_plain = low_back(matmul(normed_first, key_weight)).reshape(seq_rows, KV_HEADS, HEAD_DIM)
    value_rows = low(low_back(matmul(normed_first, value_weight))).reshape(seq_rows, KV_HEADS, HEAD_DIM)
    cosine, sine_part = rotation(doc_positions)
    query_turned = low(rotate(queries, cosine, sine_part)).reshape(seq_rows, KV_HEADS, group_share, HEAD_DIM)
    key_turned = low(rotate(key_plain, cosine, sine_part))
    token_index = jnp.arange(seq_rows, dtype=jnp.int32)
    allowed = (doc_ids[:, None] == doc_ids[None, :]) & (token_index[None, :] <= token_index[:, None])
    raw_scores = low_back(jnp.einsum('qhgd,khd->hgqk', query_turned, key_turned, precision=lax.Precision.HIGHEST) * HEAD_DIM ** (-0.5))
    scores = jnp.where(allowed[None, None], raw_scores, masked_score)
    row_top = lax.optimization_barrier(jnp.max(scores, -1, keepdims=True))
    lifted = jnp.exp(scores - row_top)
    softmax = lifted / lax.optimization_barrier(jnp.sum(lifted, -1, keepdims=True))
    attended = jnp.einsum('hgqk,khd->qhgd', low(softmax), value_rows, precision=lax.Precision.HIGHEST).reshape(seq_rows, HEADS * HEAD_DIM)
    attended = low(low_back(attended))
    hidden = inputs_f + low_back(matmul(attended, output_weight))
    scale_second = lax.rsqrt(lax.optimization_barrier(jnp.mean(hidden * hidden, -1, keepdims=True)) + epsilon)
    normed_second = low(hidden * scale_second * mlp_gain)
    gate_pre = low_back(matmul(normed_second, gate_weight))
    up_pre = low_back(matmul(normed_second, up_weight))
    mixed_low = low(gate_pre * jax.nn.sigmoid(gate_pre) * up_pre)
    return hidden + matmul(mixed_low, down_weight)

def reference(tokens, segments, positions, cotangent, attention_gain, query_weight, key_weight, value_weight, output_weight, mlp_gain, gate_weight, up_weight, down_weight):
    weights = tuple((array.astype(jnp.float32) for array in (attention_gain, query_weight, key_weight, value_weight, output_weight, mlp_gain, gate_weight, up_weight, down_weight)))

    def one_sequence(totals, sequence_item):
        inputs, grad_out, doc_ids, doc_positions = sequence_item

        def forward(inputs_f, *params):
            return layer(inputs_f, *params, doc_ids, doc_positions)
        block_out, pullback = jax.vjp(forward, inputs.astype(jnp.float32), *weights)
        gradients = pullback(grad_out.astype(jnp.float32))
        updated = tuple((total_part + grad_part for total_part, grad_part in zip(totals, gradients[1:])))
        return (updated, (block_out.astype(jnp.bfloat16), gradients[0]))
    zeros_init = tuple((jnp.zeros(array.shape, jnp.float32) for array in weights))
    final, (outputs, token_grads) = lax.scan(one_sequence, zeros_init, (tokens, cotangent, segments, positions))
    return (outputs, token_grads, final[0], final[1], final[2], final[3], final[4], final[5], final[6], final[7], final[8])
```

```python
import functools
import math

import jax
import jax.numpy as jnp
from jax import lax
from jax.experimental import pallas as pl
from jax.experimental.pallas import tpu as pltpu
from jax.sharding import PartitionSpec as P

HEADS = 32
KV_HEADS = 8
HEAD_DIM = 64

epsilon = 1e-05
rope_base = 500000.0
masked_score = -1e30
f32 = jnp.float32
bf16 = jnp.bfloat16


def angles(doc_positions):
    freq_index = jnp.arange(HEAD_DIM // 2, dtype=f32)
    inverse_freq = jnp.exp(freq_index * (-2.0 * math.log(rope_base) / HEAD_DIM))
    return doc_positions.astype(f32)[..., None] * inverse_freq


def outer_sum(left, right):
    return lax.dot_general(left, right, (((0,), (0,)), ((), ())), preferred_element_type=f32)


def dot_nt(left, right):
    return lax.dot_general(left, right, (((1,), (1,)), ((), ())), preferred_element_type=f32)


def dot_nn(left, right):
    return lax.dot_general(left, right, (((1,), (0,)), ((), ())), preferred_element_type=f32)


def score_bias(seg_col, seg_row, first, rows):
    last = first + rows
    key_at = lax.broadcasted_iota(jnp.int32, (last, rows), 0)
    query_at = lax.broadcasted_iota(jnp.int32, (last, rows), 1) + first
    allowed = (seg_col[:last] == seg_row[:, first:last]) & (key_at <= query_at)
    return jnp.where(allowed, 0.0, masked_score)


def forward_kernel(heads, rows, qkv_ref, seg_col_ref, seg_row_ref, out_ref, norm_ref):
    shards, _, span, _ = qkv_ref.shape
    length = shards * span
    wide = heads * HEAD_DIM
    seg_col, seg_row = seg_col_ref[0], seg_row_ref[0]
    keys = qkv_ref[:, 0, :, wide : wide + HEAD_DIM].reshape(length, HEAD_DIM)
    values = qkv_ref[:, 0, :, wide + HEAD_DIM :].reshape(length, HEAD_DIM)
    values_t = values.astype(f32).T.astype(bf16)
    for first in range(0, length, rows):
        last = first + rows
        bias = score_bias(seg_col, seg_row, first, rows)
        queries = (
            qkv_ref[first // span : last // span, 0, :, :wide].reshape(rows, wide)
            * HEAD_DIM ** (-0.5)
        )
        parts = []
        for head in range(heads):
            one = queries[:, head * HEAD_DIM : (head + 1) * HEAD_DIM]
            scores = dot_nt(keys[:last], one) + bias
            top = jnp.max(scores, 0, keepdims=True)
            lifted = jnp.exp(scores - top)
            total = jnp.sum(lifted, 0, keepdims=True)
            probs = (lifted * (1.0 / total)).astype(bf16)
            parts.append(dot_nn(values_t[:, :last], probs))
            norm_ref[0, head : head + 1, first:last] = top + jnp.log(total)
        out = jnp.concatenate(parts, 0).T.astype(bf16)
        out_ref[first // span : last // span, 0] = out.reshape(rows // span, span, wide)


def turn_back(part, cosine, sine):
    half = HEAD_DIM // 2
    lower, upper = part[:half], part[half:]
    return [lower * cosine + upper * sine, upper * cosine - lower * sine]


def backward_kernel(
    heads, rows, qkv_ref, grad_ref, norm_ref, seg_col_ref, seg_row_ref, cos_ref, sin_ref,
    out_ref, key_sum, value_sum,
):
    shards, _, span, _ = qkv_ref.shape
    length = shards * span
    wide = heads * HEAD_DIM
    seg_col, seg_row = seg_col_ref[0], seg_row_ref[0]
    keys = qkv_ref[:, 0, :, wide : wide + HEAD_DIM].reshape(length, HEAD_DIM)
    values = qkv_ref[:, 0, :, wide + HEAD_DIM :].reshape(length, HEAD_DIM)
    keys_t = keys.astype(f32).T.astype(bf16)
    key_sum[...] = jnp.zeros_like(key_sum)
    value_sum[...] = jnp.zeros_like(value_sum)
    for first in range(0, length, rows):
        last = first + rows
        at = slice(first // span, last // span)
        bias = score_bias(seg_col, seg_row, first, rows)
        queries = qkv_ref[at, 0, :, :wide].reshape(rows, wide) * HEAD_DIM ** (-0.5)
        grads = grad_ref[at, 0].reshape(rows, wide)
        cosine, sine = cos_ref[0, :, first:last], sin_ref[0, :, first:last]
        parts = []
        for head in range(heads):
            lanes = slice(head * HEAD_DIM, (head + 1) * HEAD_DIM)
            one, grad = queries[:, lanes], grads[:, lanes]
            scores = dot_nt(keys[:last], one) + bias
            probs = jnp.exp(scores - norm_ref[0, head : head + 1, first:last])
            grad_probs = dot_nt(values[:last], grad)
            level = jnp.sum(probs * grad_probs, 0, keepdims=True)
            grad_scores = (probs * (grad_probs - level)).astype(bf16)
            value_sum[:last] += dot_nn(probs.astype(bf16), grad)
            key_sum[:last] += dot_nn(grad_scores, one)
            turned = dot_nn(keys_t[:, :last], grad_scores) * HEAD_DIM ** (-0.5)
            parts.extend(turn_back(turned, cosine, sine))
        out = jnp.concatenate(parts, 0).T.astype(bf16)
        out_ref[at, 0, :, :wide] = out.reshape(rows // span, span, wide)
    key_parts = turn_back(key_sum[...].T, cos_ref[0], sin_ref[0])
    both = jnp.concatenate([jnp.concatenate(key_parts, 0).T, value_sum[...]], -1)
    out_ref[:, 0, :, wide:] = both.astype(bf16).reshape(shards, span, 2 * HEAD_DIM)


def by_sequence(shape, axis):
    block = tuple(1 if at == axis else size for at, size in enumerate(shape))
    return pl.BlockSpec(block, lambda i: tuple(i if at == axis else 0 for at in range(len(shape))))


def attention_forward(heads, qkv, seg_col, seg_row):
    shards, seqs, span, _ = qkv.shape
    length = shards * span
    out_shape = (
        jax.ShapeDtypeStruct((shards, seqs, span, heads * HEAD_DIM), bf16),
        jax.ShapeDtypeStruct((seqs, heads, length), f32),
    )
    return pl.pallas_call(
        functools.partial(forward_kernel, heads, 256),
        grid=(seqs,),
        in_specs=[
            by_sequence(qkv.shape, 1),
            by_sequence(seg_col.shape, 0),
            by_sequence(seg_row.shape, 0),
        ],
        out_specs=(by_sequence(out_shape[0].shape, 1), by_sequence(out_shape[1].shape, 0)),
        out_shape=out_shape,
        compiler_params=pltpu.CompilerParams(vmem_limit_bytes=48 * 2**20),
        cost_estimate=pl.CostEstimate(
            flops=4 * seqs * heads * length * length * HEAD_DIM,
            bytes_accessed=2 * qkv.size * 2,
            transcendentals=seqs * heads * length * length,
        ),
    )(qkv, seg_col, seg_row)


def attention_backward(heads, qkv, grads, norms, seg_col, seg_row, cosine, sine):
    shards, seqs, span, _ = qkv.shape
    length = shards * span
    args = (qkv, grads, norms, seg_col, seg_row, cosine, sine)
    return pl.pallas_call(
        functools.partial(backward_kernel, heads, 256),
        grid=(seqs,),
        in_specs=[by_sequence(a.shape, 1 if i < 2 else 0) for i, a in enumerate(args)],
        out_specs=by_sequence(qkv.shape, 1),
        out_shape=jax.ShapeDtypeStruct(qkv.shape, bf16),
        scratch_shapes=[pltpu.VMEM((length, HEAD_DIM), f32), pltpu.VMEM((length, HEAD_DIM), f32)],
        compiler_params=pltpu.CompilerParams(vmem_limit_bytes=48 * 2**20),
        cost_estimate=pl.CostEstimate(
            flops=10 * seqs * heads * length * length * HEAD_DIM,
            bytes_accessed=3 * qkv.size * 2,
            transcendentals=seqs * heads * length * length,
        ),
    )(*args)


def exchange(blocks):
    return lax.all_to_all(blocks, "shard", 0, 0, tiled=True)


def exchange_async(blocks):
    count = blocks.shape[0]
    me = lax.axis_index("shard")
    result = blocks
    for step in range(1, count):
        pairs = [(i, i ^ step) for i in range(count)]
        partner = me ^ step
        sent = lax.dynamic_index_in_dim(blocks, partner, 0, keepdims=True)
        got = lax.ppermute(sent, "shard", pairs)
        result = lax.dynamic_update_slice_in_dim(result, got, partner, 0)
    return result


def replica_sum(part):
    count = lax.axis_size("replica")
    if count != 4:
        return lax.psum(part.astype(bf16), "replica").astype(f32)
    me = lax.axis_index("replica")
    inner = (me == 1) | (me == 2)
    low = part.astype(bf16)
    inward = lax.ppermute(low, "replica", [(0, 1), (3, 2)])
    half = (part.astype(f32) + inward.astype(f32)).astype(bf16)
    other = lax.ppermute(half, "replica", [(1, 2), (2, 1)])
    whole = (half.astype(f32) + other.astype(f32)).astype(bf16)
    outward = lax.ppermute(whole, "replica", [(1, 0), (2, 3)])
    return jnp.where(inner, whole, outward).astype(f32)


def norm_back(grad_normed, unit_rows, scale_rows, gain_rows):
    scaled_grad = grad_normed * gain_rows
    return scale_rows * (
        scaled_grad - unit_rows * jnp.mean(scaled_grad * unit_rows, -1, keepdims=True)
    )


def gather(block):
    return lax.all_gather(block, "shard", axis=0, tiled=True)


def scatter(partial):
    return lax.psum_scatter(partial.astype(bf16), "shard", scatter_dimension=0, tiled=True).astype(
        f32
    )


def body(
    tokens,
    segments,
    positions,
    cotangent,
    attention_gain,
    query_weight,
    key_weight,
    value_weight,
    output_weight,
    mlp_gain,
    gate_weight,
    up_weight,
    down_weight,
):
    seqs, span, width = tokens.shape
    shards = lax.axis_size("shard")
    me = lax.axis_index("shard")
    rows = seqs * span
    length = shards * span
    owned = query_weight.shape[0]
    heads = HEADS // shards
    copies = max(1, shards // KV_HEADS)
    wide = heads * HEAD_DIM
    part = wide + 2 * HEAD_DIM
    hidden_share = down_weight.shape[0]

    def per_head(weight):
        return jnp.repeat(weight.reshape(owned, KV_HEADS, HEAD_DIM), copies, axis=1)

    qkv_owned = jnp.concatenate(
        [query_weight.reshape(owned, shards, wide), per_head(key_weight), per_head(value_weight)],
        -1,
    ).reshape(owned, shards * part)
    qkv_full = gather(qkv_owned)
    gains = lax.all_gather(jnp.stack([attention_gain, mlp_gain]), "shard", axis=1, tiled=True)
    gain_one, gain_two = gains[0].astype(f32), gains[1].astype(f32)
    places = lax.all_gather(jnp.stack([segments, positions]), "shard", axis=2, tiled=True)
    seg_row, seg_col = places[0][:, None, :], places[0][:, :, None]
    angle_all = jnp.swapaxes(angles(places[1]), 1, 2)
    cos_all, sin_all = jnp.cos(angle_all), jnp.sin(angle_all)
    output_full = gather(output_weight)

    x = tokens.reshape(rows, width).astype(f32)
    scale_one = lax.rsqrt(jnp.mean(x * x, -1, keepdims=True) + epsilon)
    unit_one = x * scale_one
    normed_one = (unit_one * gain_one).astype(bf16)
    projected = dot_nn(normed_one, qkv_full).reshape(rows, shards, part)
    angle = angles(positions).reshape(rows, 1, 1, HEAD_DIM // 2)
    cosine, sine = jnp.cos(angle), jnp.sin(angle)
    turning = projected[:, :, : wide + HEAD_DIM].reshape(rows, shards, heads + 1, HEAD_DIM)
    lower, upper = turning[..., : HEAD_DIM // 2], turning[..., HEAD_DIM // 2 :]
    turned = jnp.concatenate(
        [lower * cosine - upper * sine, upper * cosine + lower * sine], -1
    ).reshape(rows, shards, wide + HEAD_DIM)
    qkv_rows = jnp.concatenate([turned, projected[:, :, wide + HEAD_DIM :]], -1).astype(bf16)
    qkv = exchange(jnp.swapaxes(qkv_rows, 0, 1)).reshape(shards, seqs, span, part)

    attn_heads, norms = attention_forward(heads, qkv, seg_col, seg_row)
    attn = exchange(attn_heads.reshape(shards, rows, wide))
    attn = jnp.swapaxes(attn, 0, 1).reshape(rows, HEADS * HEAD_DIM)
    hidden = x + dot_nn(attn, output_full)
    scale_two = lax.rsqrt(jnp.mean(hidden * hidden, -1, keepdims=True) + epsilon)
    unit_two = hidden * scale_two
    normed_two = (unit_two * gain_two).astype(bf16)

    def to_columns(weight):
        blocks = jnp.swapaxes(weight.reshape(owned, shards, hidden_share), 0, 1)
        return exchange_async(blocks).reshape(shards * owned, hidden_share)

    gate_columns, up_columns = to_columns(gate_weight), to_columns(up_weight)
    cot_rows = cotangent.reshape(rows, width)
    cot_all = gather(cot_rows)
    normed_all = gather(normed_two)
    gate = dot_nn(normed_all, gate_columns)
    up = dot_nn(normed_all, up_columns)
    grad_mixed = dot_nt(cot_all, down_weight)
    sigmoid = jax.nn.sigmoid(gate)
    swish = gate * sigmoid
    mixed = (swish * up).astype(bf16)
    grad_gate = (grad_mixed * up * (sigmoid + swish * (1.0 - sigmoid))).astype(bf16)
    grad_up = (grad_mixed * swish).astype(bf16)
    grad_two = scatter(dot_nt(grad_gate, gate_columns) + dot_nt(grad_up, up_columns))
    down_grad = replica_sum(outer_sum(mixed, cot_all))

    def to_rows(grad):
        blocks = exchange_async(grad.astype(bf16).reshape(shards, owned, hidden_share))
        summed = replica_sum(blocks)
        return jnp.swapaxes(summed, 0, 1).reshape(owned, shards * hidden_share)

    gate_grad = to_rows(outer_sum(normed_all, grad_gate))
    up_grad = to_rows(outer_sum(normed_all, grad_up))
    block_out = (hidden + scatter(dot_nn(mixed, down_weight))).astype(bf16)

    second_grad = jnp.sum(grad_two * unit_two, 0)
    grad_hidden = cot_rows.astype(f32) + norm_back(grad_two, unit_two, scale_two, gain_two)
    branch = grad_hidden.astype(bf16)
    grad_attn = dot_nt(branch, output_full).astype(bf16).reshape(rows, shards, wide)
    grad_heads = exchange(jnp.swapaxes(grad_attn, 0, 1)).reshape(shards, seqs, span, wide)
    output_grad = replica_sum(scatter(outer_sum(attn, branch)))
    grad_qkv = attention_backward(
        heads, qkv, grad_heads, norms, seg_col, seg_row, cos_all, sin_all
    )
    grad_qkv = exchange(grad_qkv.reshape(shards, rows, part))
    grad_qkv = jnp.swapaxes(grad_qkv, 0, 1).reshape(rows, shards * part)
    grad_one = dot_nt(grad_qkv, qkv_full)
    qkv_grad = replica_sum(scatter(outer_sum(normed_one, grad_qkv)))
    qkv_grad = qkv_grad.reshape(owned, shards, part)

    def kv_grad(columns):
        return jnp.sum(columns.reshape(owned, KV_HEADS, copies, HEAD_DIM), 2).reshape(
            owned, KV_HEADS * HEAD_DIM
        )

    query_grad = qkv_grad[:, :, :wide].reshape(owned, HEADS * HEAD_DIM)
    key_grad = kv_grad(qkv_grad[:, :, wide : wide + HEAD_DIM])
    value_grad = kv_grad(qkv_grad[:, :, wide + HEAD_DIM :])
    first_grad = jnp.sum(grad_one * unit_one, 0)
    token_grad = grad_hidden + norm_back(grad_one, unit_one, scale_one, gain_one)
    gain_grads = lax.psum(jnp.stack([first_grad, second_grad]), ("replica", "shard"))
    gain_grads = lax.dynamic_slice_in_dim(gain_grads, me * owned, owned, 1)
    return (
        block_out.reshape(seqs, span, width),
        token_grad.reshape(seqs, span, width),
        gain_grads[0],
        query_grad,
        key_grad,
        value_grad,
        output_grad,
        gain_grads[1],
        gate_grad,
        up_grad,
        down_grad,
    )


def solution(mesh):
    rows = P("shard", None)
    blocks = P("replica", "shard", None)
    in_specs = (
        blocks, P("replica", "shard"), P("replica", "shard"), blocks, P("shard"),
        rows, rows, rows, rows, P("shard"), rows, rows, rows,
    )
    out_specs = (
        blocks, blocks, P("shard"), rows, rows, rows, rows, P("shard"), rows, rows, rows,
    )
    return jax.shard_map(body, mesh=mesh, in_specs=in_specs, out_specs=out_specs, check_vma=False)
```

```python
import functools
import math

import jax
import jax.numpy as jnp
from jax import lax
from jax.experimental import pallas as pl
from jax.experimental.pallas import tpu as pltpu
from jax.sharding import PartitionSpec as P

HEADS = 32
KV_HEADS = 8
HEAD_DIM = 64

epsilon = 1e-05
rope_base = 500000.0
masked_score = -1e30
f32 = jnp.float32
bf16 = jnp.bfloat16


def angles(doc_positions):
    freq_index = jnp.arange(HEAD_DIM // 2, dtype=f32)
    inverse_freq = jnp.exp(freq_index * (-2.0 * math.log(rope_base) / HEAD_DIM))
    return doc_positions.astype(f32)[..., None] * inverse_freq


def outer_sum(left, right):
    return lax.dot_general(left, right, (((0,), (0,)), ((), ())), preferred_element_type=f32)


def dot_nt(left, right):
    return lax.dot_general(left, right, (((1,), (1,)), ((), ())), preferred_element_type=f32)


def dot_nn(left, right):
    return lax.dot_general(left, right, (((1,), (0,)), ((), ())), preferred_element_type=f32)


def score_bias(seg_col, seg_row, first, rows):
    last = first + rows
    key_at = lax.broadcasted_iota(jnp.int32, (last, rows), 0)
    query_at = lax.broadcasted_iota(jnp.int32, (last, rows), 1) + first
    allowed = (seg_col[:last] == seg_row[:, first:last]) & (key_at <= query_at)
    return jnp.where(allowed, 0.0, masked_score)


def forward_kernel(heads, rows, qkv_ref, seg_col_ref, seg_row_ref, out_ref, norm_ref):
    shards, _, span, _ = qkv_ref.shape
    length = shards * span
    wide = heads * HEAD_DIM
    seg_col, seg_row = seg_col_ref[0], seg_row_ref[0]
    keys = qkv_ref[:, 0, :, wide : wide + HEAD_DIM].reshape(length, HEAD_DIM)
    values = qkv_ref[:, 0, :, wide + HEAD_DIM :].reshape(length, HEAD_DIM)
    values_t = values.astype(f32).T.astype(bf16)
    for first in range(0, length, rows):
        last = first + rows
        bias = score_bias(seg_col, seg_row, first, rows)
        queries = (
            qkv_ref[first // span : last // span, 0, :, :wide].reshape(rows, wide)
            * HEAD_DIM ** (-0.5)
        )
        parts = []
        for head in range(heads):
            one = queries[:, head * HEAD_DIM : (head + 1) * HEAD_DIM]
            scores = dot_nt(keys[:last], one) + bias
            top = jnp.max(scores, 0, keepdims=True)
            lifted = jnp.exp(scores - top)
            total = jnp.sum(lifted, 0, keepdims=True)
            probs = (lifted * (1.0 / total)).astype(bf16)
            parts.append(dot_nn(values_t[:, :last], probs))
            norm_ref[0, head : head + 1, first:last] = top + jnp.log(total)
        out = jnp.concatenate(parts, 0).T.astype(bf16)
        out_ref[first // span : last // span, 0] = out.reshape(rows // span, span, wide)


def turn_back(part, cosine, sine):
    half = HEAD_DIM // 2
    lower, upper = part[:half], part[half:]
    return [lower * cosine + upper * sine, upper * cosine - lower * sine]


def backward_kernel(
    heads, rows, qkv_ref, grad_ref, norm_ref, seg_col_ref, seg_row_ref, cos_ref, sin_ref,
    out_ref, key_sum, value_sum,
):
    shards, _, span, _ = qkv_ref.shape
    length = shards * span
    wide = heads * HEAD_DIM
    seg_col, seg_row = seg_col_ref[0], seg_row_ref[0]
    keys = qkv_ref[:, 0, :, wide : wide + HEAD_DIM].reshape(length, HEAD_DIM)
    values = qkv_ref[:, 0, :, wide + HEAD_DIM :].reshape(length, HEAD_DIM)
    keys_t = keys.astype(f32).T.astype(bf16)
    key_sum[...] = jnp.zeros_like(key_sum)
    value_sum[...] = jnp.zeros_like(value_sum)
    for first in range(0, length, rows):
        last = first + rows
        at = slice(first // span, last // span)
        bias = score_bias(seg_col, seg_row, first, rows)
        queries = qkv_ref[at, 0, :, :wide].reshape(rows, wide) * HEAD_DIM ** (-0.5)
        grads = grad_ref[at, 0].reshape(rows, wide)
        cosine, sine = cos_ref[0, :, first:last], sin_ref[0, :, first:last]
        parts = []
        for head in range(heads):
            lanes = slice(head * HEAD_DIM, (head + 1) * HEAD_DIM)
            one, grad = queries[:, lanes], grads[:, lanes]
            scores = dot_nt(keys[:last], one) + bias
            probs = jnp.exp(scores - norm_ref[0, head : head + 1, first:last])
            grad_probs = dot_nt(values[:last], grad)
            level = jnp.sum(probs * grad_probs, 0, keepdims=True)
            grad_scores = (probs * (grad_probs - level)).astype(bf16)
            value_sum[:last] += dot_nn(probs.astype(bf16), grad)
            key_sum[:last] += dot_nn(grad_scores, one)
            turned = dot_nn(keys_t[:, :last], grad_scores) * HEAD_DIM ** (-0.5)
            parts.extend(turn_back(turned, cosine, sine))
        out = jnp.concatenate(parts, 0).T.astype(bf16)
        out_ref[at, 0, :, :wide] = out.reshape(rows // span, span, wide)
    key_parts = turn_back(key_sum[...].T, cos_ref[0], sin_ref[0])
    both = jnp.concatenate([jnp.concatenate(key_parts, 0).T, value_sum[...]], -1)
    out_ref[:, 0, :, wide:] = both.astype(bf16).reshape(shards, span, 2 * HEAD_DIM)


def by_sequence(shape, axis):
    block = tuple(1 if at == axis else size for at, size in enumerate(shape))
    return pl.BlockSpec(block, lambda i: tuple(i if at == axis else 0 for at in range(len(shape))))


def attention_forward(heads, qkv, seg_col, seg_row):
    shards, seqs, span, _ = qkv.shape
    length = shards * span
    out_shape = (
        jax.ShapeDtypeStruct((shards, seqs, span, heads * HEAD_DIM), bf16),
        jax.ShapeDtypeStruct((seqs, heads, length), f32),
    )
    return pl.pallas_call(
        functools.partial(forward_kernel, heads, 256),
        grid=(seqs,),
        in_specs=[
            by_sequence(qkv.shape, 1),
            by_sequence(seg_col.shape, 0),
            by_sequence(seg_row.shape, 0),
        ],
        out_specs=(by_sequence(out_shape[0].shape, 1), by_sequence(out_shape[1].shape, 0)),
        out_shape=out_shape,
        compiler_params=pltpu.CompilerParams(vmem_limit_bytes=48 * 2**20),
        cost_estimate=pl.CostEstimate(
            flops=4 * seqs * heads * length * length * HEAD_DIM,
            bytes_accessed=2 * qkv.size * 2,
            transcendentals=seqs * heads * length * length,
        ),
    )(qkv, seg_col, seg_row)


def attention_backward(heads, qkv, grads, norms, seg_col, seg_row, cosine, sine):
    shards, seqs, span, _ = qkv.shape
    length = shards * span
    args = (qkv, grads, norms, seg_col, seg_row, cosine, sine)
    return pl.pallas_call(
        functools.partial(backward_kernel, heads, 256),
        grid=(seqs,),
        in_specs=[by_sequence(a.shape, 1 if i < 2 else 0) for i, a in enumerate(args)],
        out_specs=by_sequence(qkv.shape, 1),
        out_shape=jax.ShapeDtypeStruct(qkv.shape, bf16),
        scratch_shapes=[pltpu.VMEM((length, HEAD_DIM), f32), pltpu.VMEM((length, HEAD_DIM), f32)],
        compiler_params=pltpu.CompilerParams(vmem_limit_bytes=48 * 2**20),
        cost_estimate=pl.CostEstimate(
            flops=10 * seqs * heads * length * length * HEAD_DIM,
            bytes_accessed=3 * qkv.size * 2,
            transcendentals=seqs * heads * length * length,
        ),
    )(*args)


def chip_at(chip, distance):
    result, bit = chip, 1
    while bit <= distance:
        if distance & bit:
            result = result + bit * (1 - 2 * ((chip // bit) % 2))
        bit *= 2
    return result


def pieces_of(chips):
    if chips == 4:
        return [[(0, 0), (0, 1)], [(1, 0), (2, 0)], [(1, 1), (2, 1)], [(3, 0), (3, 1)]]
    return [[(d, 0), (d, 1)] for d in range(chips)]


def feed_kernel(
    normed_ref, cot_ref, own_ref, other_ref, down_own_ref, down_other_ref,
    partial_ref, out_ref, mixed_ref, gate_ref, up_ref,
    down_own_out, gate_own_out, up_own_out, down_got, gate_got, up_got,
    weights, normed, cot, inner, sent, out_stage,
    weight_sem, normed_send, normed_recv, cot_sem, inner_sem, sum_send, sum_recv, own_sem, out_sem,
    core_send, core_recv, core_sem, load_sem,
):
    chips, rows, width = normed.shape
    units = mixed_ref.shape[1]
    half_rows, half_units = rows // 2, units // 2
    replicas, _, _, share, _ = own_ref.shape
    me = lax.axis_index("shard")
    replica = lax.axis_index("replica")
    chip, core = me // 2, me % 2
    sibling = chip * 2 + (1 - core)
    partner = [chip_at(chip, d) * 2 + core for d in range(chips)]
    steps = pieces_of(chips)

    def remote(source, target, send, recv, shard):
        return pltpu.make_async_remote_copy(
            src_ref=source, dst_ref=target, send_sem=send, recv_sem=recv,
            device_id=(replica, shard), device_id_type=pl.DeviceIdType.MESH,
        )

    barrier = pltpu.get_barrier_semaphore()
    for shard in partner[1:] + [sibling]:
        pl.semaphore_signal(
            barrier, inc=1, device_id=(replica, shard), device_id_type=pl.DeviceIdType.MESH
        )
    pl.semaphore_wait(barrier, chips)

    def half(index):
        return pl.ds(index * half_rows, half_rows)

    def token_copy(distance, part, source, target):
        return remote(
            source, normed.at[distance, half(part)],
            normed_send.at[distance, part], normed_recv.at[distance, part], target,
        )

    relay = chips == 4
    direct = range(1, 3) if relay else range(1, chips)
    for part in range(2):
        for d in direct:
            token_copy(d, part, normed_ref.at[half(part)], partner[d]).start()
    own_copy = pltpu.make_async_copy(normed_ref, normed.at[0], own_sem.at[0])
    own_copy.start()

    def cot_copies(index):
        return [
            pltpu.make_async_copy(
                cot_ref.at[chip_at(chip, d), half(part)], cot.at[index % 2, half(at)],
                cot_sem.at[index % 2, at],
            )
            for at, (d, part) in enumerate(steps[index])
        ]

    for copy in cot_copies(0):
        copy.start()
    owned = share * replicas
    for which in range(2):
        for k in range(chips):
            for z in range(replicas):
                for ref, c in ((own_ref, core), (other_ref, 1 - core)):
                    pltpu.make_async_copy(
                        ref.at[z, which, k],
                        weights.at[which, pl.ds((2 * k + c) * owned + z * share, share), pl.ds(0, units)],
                        weight_sem.at[which],
                    ).start()
    down_own = pltpu.make_async_copy(
        down_own_ref, weights.at[2, pl.ds(core * half_units, half_units)], weight_sem.at[2]
    )
    down_other = pltpu.make_async_copy(
        down_other_ref, weights.at[2, pl.ds((1 - core) * half_units, half_units)], weight_sem.at[3]
    )
    down_own.start()
    down_other.start()
    own_copy.wait()
    for which in range(2):
        whole = weights.at[which, pl.ds(0, width), pl.ds(0, units)]
        pltpu.make_async_copy(whole, whole, weight_sem.at[which]).wait()
    down_own.wait()
    down_other.wait()

    def inner_copies(index):
        return [
            pltpu.make_async_copy(
                inner.at[which, half(at), pl.ds(0, units)],
                ref.at[pl.ds(d * rows + part * half_rows, half_rows)],
                inner_sem.at[which, at],
            )
            for at, (d, part) in enumerate(steps[index])
            for which, ref in enumerate((mixed_ref, gate_ref, up_ref))
        ]

    def out_copies(index):
        return [
            pltpu.make_async_copy(
                out_stage.at[half(at)], out_ref.at[chip_at(chip, d), half(part)], out_sem.at[at]
            )
            for at, (d, part) in enumerate(steps[index])
        ]

    def sum_copy(index, at):
        d, part = steps[index][at]
        return remote(
            sent.at[index % (chips - 1), half(at)], partial_ref.at[d, half(part)],
            sum_send.at[d, part], sum_recv.at[d, part], partner[d],
        )

    own_sums = [
        pltpu.make_async_copy(sent.at[0, half(at)], partial_ref.at[0, half(at)], own_sem.at[1 + at])
        for at in range(2)
    ]
    tile = min(512, units)
    for index in range(chips):
        parts = steps[index]
        for d, part in parts:
            if d > 0:
                if relay and d == 3:
                    source, way = (1, 2) if part == 0 else (2, 1)
                    copy = token_copy(3, part, normed.at[source, half(part)], partner[way])
                else:
                    copy = token_copy(d, part, normed_ref.at[half(part)], partner[d])
                copy.wait_recv()
        if relay and index in (1, 2):
            part, source, way = (0, 1, 2) if index == 1 else (1, 2, 1)
            token_copy(3, part, normed.at[source, half(part)], partner[way]).start()
        for copy in cot_copies(index):
            copy.wait()
        if index + 1 < chips:
            for copy in cot_copies(index + 1):
                copy.start()
        if index > 0:
            for copy in inner_copies(index - 1):
                copy.wait()
        (d0, p0), (d1, p1) = parts

        @pl.loop(0, units // tile)
        def _(j):
            columns = pl.ds(pl.multiple_of(j * tile, tile), tile)
            if d0 == d1:
                block = normed[d0]
            else:
                block = jnp.concatenate([normed[d0, half(p0)], normed[d1, half(p1)]], 0)
            gate = dot_nn(block, weights[0, :width, columns])
            up = dot_nn(block, weights[1, :width, columns])
            grad = dot_nt(cot[index % 2], weights[2, columns, :])
            sigmoid = jax.nn.sigmoid(gate)
            swish = gate * sigmoid
            inner[0, :, columns] = (swish * up).astype(bf16)
            inner[1, :, columns] = (grad * up * (sigmoid + swish * (1.0 - sigmoid))).astype(bf16)
            inner[2, :, columns] = (grad * swish).astype(bf16)

        for copy in inner_copies(index):
            copy.start()
        if index > 0:
            for copy in out_copies(index - 1):
                copy.wait()
        slot = index % (chips - 1)
        if index == chips - 1:
            for copy in own_sums:
                copy.wait()

        @pl.loop(0, width // 512)
        def _(j):
            columns = pl.ds(pl.multiple_of(j * 512, 512), 512)
            sent[slot, :, columns] = (
                dot_nt(inner[1, :, :units], weights[0, columns, :units])
                + dot_nt(inner[2, :, :units], weights[1, columns, :units])
            ).astype(bf16)

        if index == 0:
            for copy in own_sums:
                copy.start()
        else:
            for at in range(2):
                sum_copy(index, at).start()

        @pl.loop(0, width // 512)
        def _(j):
            columns = pl.ds(pl.multiple_of(j * 512, 512), 512)
            out_stage[:, columns] = dot_nn(
                inner[0, :, :units], weights[2, :units, columns]
            ).astype(bf16)

        for copy in out_copies(index):
            copy.start()

    for copy in inner_copies(chips - 1):
        copy.wait()
    for copy in out_copies(chips - 1):
        copy.wait()

    tokens = chips * rows

    def load(ref, which):
        return pltpu.make_async_copy(
            ref, weights.at[which, pl.ds(0, tokens), pl.ds(0, units)], load_sem.at[which]
        )

    loads = [load(mixed_ref, 0), load(gate_ref, 1)]
    cot_loads = [
        pltpu.make_async_copy(
            cot_ref.at[chip_at(chip, d)], weights.at[2, pl.ds(d * rows, rows)], load_sem.at[3 + d]
        )
        for d in range(chips)
    ]
    for copy in loads + cot_loads:
        copy.start()
    for copy in cot_loads + loads:
        copy.wait()
    tiles = width // rows
    per_slot = width // half_units

    def stage_copies(which, owner, stage, local, landing):
        result = []
        for t in range(tiles):
            if which == 0:
                if t >= half_units // rows:
                    break
                source, place = stage.at[t], (pl.ds(t * rows, rows),)
            else:
                source = stage.at[t // per_slot, :, pl.ds((t % per_slot) * half_units, half_units)]
                place = (pl.ds(t * rows, rows),)
            if owner == 0:
                result.append(
                    remote(
                        source, landing.at[place], core_send.at[which, t], core_recv.at[which, t],
                        sibling,
                    )
                )
            else:
                result.append(
                    pltpu.make_async_copy(source, local.at[place], core_sem.at[which, t])
                )
        return result

    outs = ((down_own_out, down_got), (gate_own_out, gate_got), (up_own_out, up_got))
    started = {}
    for which in range(3):
        if which == 2:
            copy = load(up_ref, 1)
            copy.start()
            copy.wait()
        for owner in range(2):
            stage = cot if owner == 0 else inner
            first = ((1 - core) if owner == 0 else core) * half_units
            copies = stage_copies(which, owner, stage, *outs[which])
            started[which, owner] = copies
            if which > 0:
                for copy in started[which - 1, owner]:
                    if owner == 0:
                        copy.wait_send()
                    else:
                        copy.wait()
            for t, copy in enumerate(copies):
                if which == 0:
                    left = weights[0, :tokens, pl.ds(pl.multiple_of(first + t * rows, rows), rows)]
                    for j in range(width // 1024):
                        columns = pl.ds(j * 1024, 1024)
                        stage[t, :, columns] = lax.dot_general(
                            left, weights[2, :tokens, columns], (((0,), (0,)), ((), ())),
                            preferred_element_type=f32,
                        ).astype(bf16)
                else:
                    left = normed[:, :, t * rows : (t + 1) * rows].reshape(tokens, rows)
                    right = weights[1, :tokens, pl.ds(pl.multiple_of(first, half_units), half_units)]
                    stage[t // per_slot, :, pl.ds((t % per_slot) * half_units, half_units)] = (
                        lax.dot_general(
                            left, right, (((0,), (0,)), ((), ())), preferred_element_type=f32
                        ).astype(bf16)
                    )
                copy.start()
    for owner in range(2):
        for copy in started[2, owner]:
            if owner == 0:
                copy.wait_send()
            else:
                copy.wait()
    for which in range(3):
        for copy in started[which, 0]:
            copy.wait_recv()
    for index in range(1, chips):
        for at in range(2):
            sum_copy(index, at).wait_send()
            sum_copy(index, at).wait_recv()
    for d in range(1, chips):
        for part in range(2):
            if relay and d == 3:
                source, way = (1, 2) if part == 0 else (2, 1)
                token_copy(3, part, normed.at[source, half(part)], partner[way]).wait_send()
            else:
                token_copy(d, part, normed_ref.at[half(part)], partner[d]).wait_send()


def feed_forward(normed, cot, own, other, down_own, down_other):
    chips, rows, width = cot.shape
    units = down_own.shape[0] * 2
    half = units // 2
    tokens = chips * rows
    tiles = width // rows
    hbm = pl.BlockSpec(memory_space=pl.ANY)
    dma = pltpu.SemaphoreType.DMA

    def low(*shape):
        return jax.ShapeDtypeStruct(shape, bf16)

    out_shape = (
        low(chips, rows, width), low(chips, rows, width),
        low(tokens, units), low(tokens, units), low(tokens, units),
        low(half, width), low(width, half), low(width, half),
        low(half, width), low(width, half), low(width, half),
    )
    depth = max(width, tokens)
    return pl.pallas_call(
        feed_kernel,
        in_specs=[hbm] * 6,
        out_specs=(hbm,) * len(out_shape),
        out_shape=out_shape,
        scratch_shapes=[
            pltpu.VMEM((3, depth, width), bf16),
            pltpu.VMEM((chips, rows, width), bf16),
            pltpu.VMEM((2, rows, width), bf16),
            pltpu.VMEM((3, rows, width), bf16),
            pltpu.VMEM((chips - 1, rows, width), bf16),
            pltpu.VMEM((rows, width), bf16),
            dma((4,)), dma((chips, 2)), dma((chips, 2)), dma((2, 2)), dma((3, 2)),
            dma((chips, 2)), dma((chips, 2)), dma((3,)), dma((2,)),
            dma((3, tiles)), dma((3, tiles)), dma((3, tiles)), dma((3 + chips,)),
        ],
        compiler_params=pltpu.CompilerParams(
            collective_id=0, has_side_effects=True, vmem_limit_bytes=63 * 2**20
        ),
        cost_estimate=pl.CostEstimate(
            flops=18 * tokens * units * width, bytes_accessed=2**27, transcendentals=tokens * units
        ),
    )(normed, cot, own, other, down_own, down_other)


def exchange(blocks):
    return lax.all_to_all(blocks, "shard", 0, 0, tiled=True)


def tie(*values):
    return lax.optimization_barrier(values)


def replica_sum(part):
    return lax.psum(part.astype(bf16), "replica").astype(f32)


def norm_back(grad_normed, unit_rows, scale_rows, gain_rows):
    scaled_grad = grad_normed * gain_rows
    return scale_rows * (
        scaled_grad - unit_rows * jnp.mean(scaled_grad * unit_rows, -1, keepdims=True)
    )


def gather(block):
    return lax.all_gather(block, "shard", axis=0, tiled=True)


def scatter(partial):
    return lax.psum_scatter(partial.astype(bf16), "shard", scatter_dimension=0, tiled=True).astype(
        f32
    )


def body(
    tokens,
    segments,
    positions,
    cotangent,
    attention_gain,
    query_weight,
    key_weight,
    value_weight,
    output_weight,
    mlp_gain,
    gate_weight,
    up_weight,
    down_weight,
):
    seqs, span, width = tokens.shape
    shards = lax.axis_size("shard")
    me = lax.axis_index("shard")
    rows = seqs * span
    length = shards * span
    owned = query_weight.shape[0]
    heads = HEADS // shards
    copies = max(1, shards // KV_HEADS)
    wide = heads * HEAD_DIM
    part = wide + 2 * HEAD_DIM
    hidden_share = down_weight.shape[0]

    def per_head(weight):
        return jnp.repeat(weight.reshape(owned, KV_HEADS, HEAD_DIM), copies, axis=1)

    qkv_owned = jnp.concatenate(
        [query_weight.reshape(owned, shards, wide), per_head(key_weight), per_head(value_weight)],
        -1,
    ).reshape(owned, shards * part)
    qkv_full = gather(qkv_owned)
    gains = lax.all_gather(jnp.stack([attention_gain, mlp_gain]), "shard", axis=1, tiled=True)
    gain_one, gain_two = gains[0].astype(f32), gains[1].astype(f32)
    places = lax.all_gather(jnp.stack([segments, positions]), "shard", axis=2, tiled=True)
    seg_row, seg_col = places[0][:, None, :], places[0][:, :, None]
    angle_all = jnp.swapaxes(angles(places[1]), 1, 2)
    cos_all, sin_all = jnp.cos(angle_all), jnp.sin(angle_all)
    output_full = gather(output_weight)

    x = tokens.reshape(rows, width).astype(f32)
    scale_one = lax.rsqrt(jnp.mean(x * x, -1, keepdims=True) + epsilon)
    unit_one = x * scale_one
    normed_one = (unit_one * gain_one).astype(bf16)
    projected = dot_nn(normed_one, qkv_full).reshape(rows, shards, part)
    angle = angles(positions).reshape(rows, 1, 1, HEAD_DIM // 2)
    cosine, sine = jnp.cos(angle), jnp.sin(angle)
    turning = projected[:, :, : wide + HEAD_DIM].reshape(rows, shards, heads + 1, HEAD_DIM)
    lower, upper = turning[..., : HEAD_DIM // 2], turning[..., HEAD_DIM // 2 :]
    turned = jnp.concatenate(
        [lower * cosine - upper * sine, upper * cosine + lower * sine], -1
    ).reshape(rows, shards, wide + HEAD_DIM)
    qkv_rows = jnp.concatenate([turned, projected[:, :, wide + HEAD_DIM :]], -1).astype(bf16)
    qkv = exchange(jnp.swapaxes(qkv_rows, 0, 1)).reshape(shards, seqs, span, part)

    chips = shards // 2
    same_core = [[2 * k + c for k in range(chips)] for c in range(2)]
    swap = [(i, i + 1 - 2 * (i % 2)) for i in range(shards)]
    units = 2 * hidden_share
    share = owned // lax.axis_size("replica")
    gate_up_own = lax.dynamic_slice_in_dim(
        jnp.stack([gate_weight, up_weight]), lax.axis_index("replica") * share, share, 1
    )
    gate_up_own = jnp.transpose(gate_up_own.reshape(2, share, chips, units), (0, 2, 1, 3))
    gate_up_part = lax.all_to_all(
        gate_up_own, "shard", 1, 1, axis_index_groups=same_core, tiled=True
    )
    gate_up = lax.all_gather(gate_up_part, "replica")
    gate_up_other = lax.ppermute(gate_up, "shard", swap)
    down_other = lax.ppermute(down_weight, "shard", swap)
    cot_rows = cotangent.reshape(rows, width)
    cot_all = lax.all_gather(cot_rows, "shard", axis_index_groups=same_core)

    attn_heads, norms = attention_forward(heads, qkv, seg_col, seg_row)
    attn = exchange(attn_heads.reshape(shards, rows, wide))
    attn = jnp.swapaxes(attn, 0, 1).reshape(rows, HEADS * HEAD_DIM)
    hidden = x + dot_nn(attn, output_full)
    scale_two = lax.rsqrt(jnp.mean(hidden * hidden, -1, keepdims=True) + epsilon)
    unit_two = hidden * scale_two
    normed_two = (unit_two * gain_two).astype(bf16)

    partials, outs, _, _, _, down_one, gate_one, up_one, down_two, gate_two, up_two = feed_forward(
        normed_two, cot_all, gate_up, gate_up_other, down_weight, down_other
    )
    grad_two = jnp.sum(partials.astype(f32), 0)
    out_sum = lax.psum_scatter(
        outs, "shard", scatter_dimension=0, axis_index_groups=same_core, tiled=False
    ).astype(f32)

    def added(one, two):
        return (one.astype(f32) + two.astype(f32)).astype(bf16)

    down_grad = lax.psum(added(down_one, down_two), "replica")
    gate_part = exchange(added(gate_one, gate_two).reshape(shards, owned, hidden_share))
    up_part = exchange(added(up_one, up_two).reshape(shards, owned, hidden_share))
    block_out = (hidden + out_sum).astype(bf16)

    def to_rows(summed):
        return jnp.swapaxes(summed, 0, 1).reshape(owned, shards * hidden_share).astype(f32)

    second_grad = jnp.sum(grad_two * unit_two, 0)
    grad_hidden = cot_rows.astype(f32) + norm_back(grad_two, unit_two, scale_two, gain_two)
    branch = grad_hidden.astype(bf16)
    grad_attn = dot_nt(branch, output_full).astype(bf16).reshape(rows, shards, wide)
    grad_heads = exchange(jnp.swapaxes(grad_attn, 0, 1)).reshape(shards, seqs, span, wide)
    output_sum = scatter(outer_sum(attn, branch))
    grad_heads, gate_part, up_part = tie(grad_heads, gate_part, up_part)
    gate_part, down_grad = tie(gate_part, down_grad)
    gate_sum = lax.psum(gate_part, "replica")
    up_part, gate_sum = tie(up_part, gate_sum)
    up_sum = lax.psum(up_part, "replica")
    grad_qkv = attention_backward(
        heads, qkv, grad_heads, norms, seg_col, seg_row, cos_all, sin_all
    )
    grad_qkv = exchange(grad_qkv.reshape(shards, rows, part))
    grad_qkv = jnp.swapaxes(grad_qkv, 0, 1).reshape(rows, shards * part)
    grad_one = dot_nt(grad_qkv, qkv_full)
    qkv_sum = scatter(outer_sum(normed_one, grad_qkv))
    qkv_sum, gate_sum, output_sum, up_sum = tie(qkv_sum, gate_sum, output_sum, up_sum)
    output_grad = replica_sum(output_sum)
    qkv_grad = replica_sum(qkv_sum)
    qkv_grad = qkv_grad.reshape(owned, shards, part)

    def kv_grad(columns):
        return jnp.sum(columns.reshape(owned, KV_HEADS, copies, HEAD_DIM), 2).reshape(
            owned, KV_HEADS * HEAD_DIM
        )

    query_grad = qkv_grad[:, :, :wide].reshape(owned, HEADS * HEAD_DIM)
    key_grad = kv_grad(qkv_grad[:, :, wide : wide + HEAD_DIM])
    value_grad = kv_grad(qkv_grad[:, :, wide + HEAD_DIM :])
    first_grad = jnp.sum(grad_one * unit_one, 0)
    token_grad = grad_hidden + norm_back(grad_one, unit_one, scale_one, gain_one)
    gain_grads = lax.psum(jnp.stack([first_grad, second_grad]), ("replica", "shard"))
    gain_grads = lax.dynamic_slice_in_dim(gain_grads, me * owned, owned, 1)
    return (
        block_out.reshape(seqs, span, width),
        token_grad.reshape(seqs, span, width),
        gain_grads[0],
        query_grad,
        key_grad,
        value_grad,
        output_grad,
        gain_grads[1],
        to_rows(gate_sum),
        to_rows(up_sum),
        down_grad.astype(f32),
    )


def solution(mesh):
    rows = P("shard", None)
    blocks = P("replica", "shard", None)
    in_specs = (
        blocks, P("replica", "shard"), P("replica", "shard"), blocks, P("shard"),
        rows, rows, rows, rows, P("shard"), rows, rows, rows,
    )
    out_specs = (
        blocks, blocks, P("shard"), rows, rows, rows, rows, P("shard"), rows, rows, rows,
    )
    return jax.shard_map(body, mesh=mesh, in_specs=in_specs, out_specs=out_specs, check_vma=False)
```

```python
import functools
import math

import jax
import jax.numpy as jnp
from jax import lax
from jax.experimental import pallas as pl
from jax.experimental.pallas import tpu as pltpu
from jax.sharding import PartitionSpec as P

HEADS = 32
KV_HEADS = 8
HEAD_DIM = 64

epsilon = 1e-05
rope_base = 500000.0
masked_score = -1e30
f32 = jnp.float32
bf16 = jnp.bfloat16


def angles(doc_positions):
    freq_index = jnp.arange(HEAD_DIM // 2, dtype=f32)
    inverse_freq = jnp.exp(freq_index * (-2.0 * math.log(rope_base) / HEAD_DIM))
    return doc_positions.astype(f32)[..., None] * inverse_freq


def outer_sum(left, right):
    return lax.dot_general(left, right, (((0,), (0,)), ((), ())), preferred_element_type=f32)


def dot_nt(left, right):
    return lax.dot_general(left, right, (((1,), (1,)), ((), ())), preferred_element_type=f32)


def dot_nn(left, right):
    return lax.dot_general(left, right, (((1,), (0,)), ((), ())), preferred_element_type=f32)


def score_bias(seg_col, seg_row, first, rows):
    last = first + rows
    key_at = lax.broadcasted_iota(jnp.int32, (last, rows), 0)
    query_at = lax.broadcasted_iota(jnp.int32, (last, rows), 1) + first
    allowed = (seg_col[:last] == seg_row[:, first:last]) & (key_at <= query_at)
    return jnp.where(allowed, 0.0, masked_score)


def forward_kernel(heads, rows, qkv_ref, seg_col_ref, seg_row_ref, out_ref, norm_ref):
    shards, _, span, _ = qkv_ref.shape
    length = shards * span
    wide = heads * HEAD_DIM
    seg_col, seg_row = seg_col_ref[0], seg_row_ref[0]
    keys = qkv_ref[:, 0, :, wide : wide + HEAD_DIM].reshape(length, HEAD_DIM)
    values = qkv_ref[:, 0, :, wide + HEAD_DIM :].reshape(length, HEAD_DIM)
    values_t = values.astype(f32).T.astype(bf16)
    for first in range(0, length, rows):
        last = first + rows
        bias = score_bias(seg_col, seg_row, first, rows)
        queries = (
            qkv_ref[first // span : last // span, 0, :, :wide].reshape(rows, wide)
            * HEAD_DIM ** (-0.5)
        )
        parts = []
        for head in range(heads):
            one = queries[:, head * HEAD_DIM : (head + 1) * HEAD_DIM]
            scores = dot_nt(keys[:last], one) + bias
            top = jnp.max(scores, 0, keepdims=True)
            lifted = jnp.exp(scores - top)
            total = jnp.sum(lifted, 0, keepdims=True)
            probs = (lifted * (1.0 / total)).astype(bf16)
            parts.append(dot_nn(values_t[:, :last], probs))
            norm_ref[0, head : head + 1, first:last] = top + jnp.log(total)
        out = jnp.concatenate(parts, 0).T.astype(bf16)
        out_ref[first // span : last // span, 0] = out.reshape(rows // span, span, wide)


def turn_back(part, cosine, sine):
    half = HEAD_DIM // 2
    lower, upper = part[:half], part[half:]
    return [lower * cosine + upper * sine, upper * cosine - lower * sine]


def attention_back(heads, rows, qkv_ref, grad_ref, norm, seg_col, seg_row, cos, sin, out_ref, sums):
    shards, span, _ = qkv_ref.shape
    length = shards * span
    wide = heads * HEAD_DIM
    keys = qkv_ref[:, :, wide : wide + HEAD_DIM].reshape(length, HEAD_DIM)
    values = qkv_ref[:, :, wide + HEAD_DIM :].reshape(length, HEAD_DIM)
    keys_t = keys.astype(f32).T.astype(bf16)
    sums[...] = jnp.zeros_like(sums)
    key_sum, value_sum = sums.at[0], sums.at[1]
    for first in range(0, length, rows):
        last = first + rows
        at = slice(first // span, last // span)
        bias = score_bias(seg_col, seg_row, first, rows)
        queries = qkv_ref[at, :, :wide].reshape(rows, wide) * HEAD_DIM ** (-0.5)
        grads = grad_ref[at].reshape(rows, wide)
        cosine, sine = cos[:, first:last], sin[:, first:last]
        parts = []
        for head in range(heads):
            lanes = slice(head * HEAD_DIM, (head + 1) * HEAD_DIM)
            one, grad = queries[:, lanes], grads[:, lanes]
            scores = dot_nt(keys[:last], one) + bias
            probs = jnp.exp(scores - norm[head : head + 1, first:last])
            grad_probs = dot_nt(values[:last], grad)
            level = jnp.sum(probs * grad_probs, 0, keepdims=True)
            grad_scores = (probs * (grad_probs - level)).astype(bf16)
            value_sum[:last] += dot_nn(probs.astype(bf16), grad)
            key_sum[:last] += dot_nn(grad_scores, one)
            turned = dot_nn(keys_t[:, :last], grad_scores) * HEAD_DIM ** (-0.5)
            parts.extend(turn_back(turned, cosine, sine))
        out = jnp.concatenate(parts, 0).T.astype(bf16)
        out_ref[at, :, :wide] = out.reshape(rows // span, span, wide)
    key_parts = turn_back(key_sum[...].T, cos[...], sin[...])
    both = jnp.concatenate([jnp.concatenate(key_parts, 0).T, value_sum[...]], -1)
    out_ref[:, :, wide:] = both.astype(bf16).reshape(shards, span, 2 * HEAD_DIM)


def by_sequence(shape, axis):
    block = tuple(1 if at == axis else size for at, size in enumerate(shape))
    return pl.BlockSpec(block, lambda i: tuple(i if at == axis else 0 for at in range(len(shape))))


def attention_forward(heads, qkv, seg_col, seg_row):
    shards, seqs, span, _ = qkv.shape
    length = shards * span
    out_shape = (
        jax.ShapeDtypeStruct((shards, seqs, span, heads * HEAD_DIM), bf16),
        jax.ShapeDtypeStruct((seqs, heads, length), f32),
    )
    return pl.pallas_call(
        functools.partial(forward_kernel, heads, 256),
        grid=(seqs,),
        in_specs=[
            by_sequence(qkv.shape, 1),
            by_sequence(seg_col.shape, 0),
            by_sequence(seg_row.shape, 0),
        ],
        out_specs=(by_sequence(out_shape[0].shape, 1), by_sequence(out_shape[1].shape, 0)),
        out_shape=out_shape,
        compiler_params=pltpu.CompilerParams(vmem_limit_bytes=48 * 2**20),
        cost_estimate=pl.CostEstimate(
            flops=4 * seqs * heads * length * length * HEAD_DIM,
            bytes_accessed=2 * qkv.size * 2,
            transcendentals=seqs * heads * length * length,
        ),
    )(qkv, seg_col, seg_row)


def chip_at(chip, distance):
    result, bit = chip, 1
    while bit <= distance:
        if distance & bit:
            result = result + bit * (1 - 2 * ((chip // bit) % 2))
        bit *= 2
    return result


def pieces_of(chips):
    if chips == 4:
        return [[(0, 0), (0, 1)], [(1, 0), (2, 0)], [(1, 1), (2, 1)], [(3, 0), (3, 1)]]
    return [[(d, 0), (d, 1)] for d in range(chips)]


def feed_kernel(
    normed_ref, cot_ref, own_ref, other_ref, down_own_ref, down_other_ref,
    partial_ref, out_ref, mixed_ref, gate_ref, up_ref,
    down_own_out, gate_own_out, up_own_out, down_got, gate_got, up_got,
    weights, normed, cot, inner, sent, out_stage,
    weight_sem, normed_send, normed_recv, cot_sem, inner_sem, sum_send, sum_recv, own_sem, out_sem,
    core_send, core_recv, core_sem, load_sem,
):
    chips, rows, width = normed.shape
    units = mixed_ref.shape[1]
    half_rows, half_units = rows // 2, units // 2
    replicas, _, _, share, _ = own_ref.shape
    me = lax.axis_index("shard")
    replica = lax.axis_index("replica")
    chip, core = me // 2, me % 2
    sibling = chip * 2 + (1 - core)
    partner = [chip_at(chip, d) * 2 + core for d in range(chips)]
    steps = pieces_of(chips)

    def remote(source, target, send, recv, shard):
        return pltpu.make_async_remote_copy(
            src_ref=source, dst_ref=target, send_sem=send, recv_sem=recv,
            device_id=(replica, shard), device_id_type=pl.DeviceIdType.MESH,
        )

    barrier = pltpu.get_barrier_semaphore()
    for shard in partner[1:] + [sibling]:
        pl.semaphore_signal(
            barrier, inc=1, device_id=(replica, shard), device_id_type=pl.DeviceIdType.MESH
        )
    pl.semaphore_wait(barrier, chips)

    def half(index):
        return pl.ds(index * half_rows, half_rows)

    def token_copy(distance, part, source, target):
        return remote(
            source, normed.at[distance, half(part)],
            normed_send.at[distance, part], normed_recv.at[distance, part], target,
        )

    relay = chips == 4
    direct = range(1, 3) if relay else range(1, chips)
    for part in range(2):
        for d in direct:
            token_copy(d, part, normed_ref.at[half(part)], partner[d]).start()
    own_copy = pltpu.make_async_copy(normed_ref, normed.at[0], own_sem.at[0])
    own_copy.start()

    def cot_copies(index):
        return [
            pltpu.make_async_copy(
                cot_ref.at[chip_at(chip, d), half(part)], cot.at[index % 2, half(at)],
                cot_sem.at[index % 2, at],
            )
            for at, (d, part) in enumerate(steps[index])
        ]

    for copy in cot_copies(0):
        copy.start()
    owned = share * replicas
    for which in range(2):
        for k in range(chips):
            for z in range(replicas):
                for ref, c in ((own_ref, core), (other_ref, 1 - core)):
                    pltpu.make_async_copy(
                        ref.at[z, which, k],
                        weights.at[which, pl.ds((2 * k + c) * owned + z * share, share), pl.ds(0, units)],
                        weight_sem.at[which],
                    ).start()
    down_own = pltpu.make_async_copy(
        down_own_ref, weights.at[2, pl.ds(core * half_units, half_units)], weight_sem.at[2]
    )
    down_other = pltpu.make_async_copy(
        down_other_ref, weights.at[2, pl.ds((1 - core) * half_units, half_units)], weight_sem.at[3]
    )
    down_own.start()
    down_other.start()
    own_copy.wait()
    for which in range(2):
        whole = weights.at[which, pl.ds(0, width), pl.ds(0, units)]
        pltpu.make_async_copy(whole, whole, weight_sem.at[which]).wait()
    down_own.wait()
    down_other.wait()

    def inner_copies(index):
        return [
            pltpu.make_async_copy(
                inner.at[which, half(at), pl.ds(0, units)],
                ref.at[pl.ds(d * rows + part * half_rows, half_rows)],
                inner_sem.at[which, at],
            )
            for at, (d, part) in enumerate(steps[index])
            for which, ref in enumerate((mixed_ref, gate_ref, up_ref))
        ]

    def out_copies(index):
        return [
            pltpu.make_async_copy(
                out_stage.at[half(at)], out_ref.at[chip_at(chip, d), half(part)], out_sem.at[at]
            )
            for at, (d, part) in enumerate(steps[index])
        ]

    def sum_copy(index, at):
        d, part = steps[index][at]
        return remote(
            sent.at[index % (chips - 1), half(at)], partial_ref.at[d, half(part)],
            sum_send.at[d, part], sum_recv.at[d, part], partner[d],
        )

    own_sums = [
        pltpu.make_async_copy(sent.at[0, half(at)], partial_ref.at[0, half(at)], own_sem.at[1 + at])
        for at in range(2)
    ]
    tile = min(512, units)
    for index in range(chips):
        parts = steps[index]
        for d, part in parts:
            if d > 0:
                if relay and d == 3:
                    source, way = (1, 2) if part == 0 else (2, 1)
                    copy = token_copy(3, part, normed.at[source, half(part)], partner[way])
                else:
                    copy = token_copy(d, part, normed_ref.at[half(part)], partner[d])
                copy.wait_recv()
        if relay and index in (1, 2):
            part, source, way = (0, 1, 2) if index == 1 else (1, 2, 1)
            token_copy(3, part, normed.at[source, half(part)], partner[way]).start()
        for copy in cot_copies(index):
            copy.wait()
        if index + 1 < chips:
            for copy in cot_copies(index + 1):
                copy.start()
        if index > 0:
            for copy in inner_copies(index - 1):
                copy.wait()
        (d0, p0), (d1, p1) = parts

        @pl.loop(0, units // tile)
        def _(j):
            columns = pl.ds(pl.multiple_of(j * tile, tile), tile)
            if d0 == d1:
                block = normed[d0]
            else:
                block = jnp.concatenate([normed[d0, half(p0)], normed[d1, half(p1)]], 0)
            gate = dot_nn(block, weights[0, :width, columns])
            up = dot_nn(block, weights[1, :width, columns])
            grad = dot_nt(cot[index % 2], weights[2, columns, :])
            sigmoid = jax.nn.sigmoid(gate)
            swish = gate * sigmoid
            inner[0, :, columns] = (swish * up).astype(bf16)
            inner[1, :, columns] = (grad * up * (sigmoid + swish * (1.0 - sigmoid))).astype(bf16)
            inner[2, :, columns] = (grad * swish).astype(bf16)

        for copy in inner_copies(index):
            copy.start()
        if index > 0:
            for copy in out_copies(index - 1):
                copy.wait()
        slot = index % (chips - 1)
        if index == chips - 1:
            for copy in own_sums:
                copy.wait()

        @pl.loop(0, width // 512)
        def _(j):
            columns = pl.ds(pl.multiple_of(j * 512, 512), 512)
            sent[slot, :, columns] = (
                dot_nt(inner[1, :, :units], weights[0, columns, :units])
                + dot_nt(inner[2, :, :units], weights[1, columns, :units])
            ).astype(bf16)

        if index == 0:
            for copy in own_sums:
                copy.start()
        else:
            for at in range(2):
                sum_copy(index, at).start()

        @pl.loop(0, width // 512)
        def _(j):
            columns = pl.ds(pl.multiple_of(j * 512, 512), 512)
            out_stage[:, columns] = dot_nn(
                inner[0, :, :units], weights[2, :units, columns]
            ).astype(bf16)

        for copy in out_copies(index):
            copy.start()

    for copy in inner_copies(chips - 1):
        copy.wait()
    for copy in out_copies(chips - 1):
        copy.wait()

    tokens = chips * rows

    def load(ref, which):
        return pltpu.make_async_copy(
            ref, weights.at[which, pl.ds(0, tokens), pl.ds(0, units)], load_sem.at[which]
        )

    loads = [load(mixed_ref, 0), load(gate_ref, 1)]
    cot_loads = [
        pltpu.make_async_copy(
            cot_ref.at[chip_at(chip, d)], weights.at[2, pl.ds(d * rows, rows)], load_sem.at[3 + d]
        )
        for d in range(chips)
    ]
    for copy in loads + cot_loads:
        copy.start()
    for copy in cot_loads + loads:
        copy.wait()
    tiles = width // rows
    per_slot = width // half_units

    def stage_copies(which, owner, stage, local, landing):
        result = []
        for t in range(tiles):
            if which == 0:
                if t >= half_units // rows:
                    break
                source, place = stage.at[t], (pl.ds(t * rows, rows),)
            else:
                source = stage.at[t // per_slot, :, pl.ds((t % per_slot) * half_units, half_units)]
                place = (pl.ds(t * rows, rows),)
            if owner == 0:
                result.append(
                    remote(
                        source, landing.at[place], core_send.at[which, t], core_recv.at[which, t],
                        sibling,
                    )
                )
            else:
                result.append(
                    pltpu.make_async_copy(source, local.at[place], core_sem.at[which, t])
                )
        return result

    outs = ((down_own_out, down_got), (gate_own_out, gate_got), (up_own_out, up_got))
    order = [(0, 0), (1, 0), (0, 1), (1, 1), (2, 0), (2, 1)]
    started = {}
    up_load = load(up_ref, 0)

    def finish(at):
        for copy in started[order[at]]:
            if order[at][1] == 0:
                copy.wait_send()
            else:
                copy.wait()

    for at, (which, owner) in enumerate(order):
        stage = cot if at % 2 == 0 else inner
        first = ((1 - core) if owner == 0 else core) * half_units
        copies = stage_copies(which, owner, stage, *outs[which])
        started[which, owner] = copies
        if at >= 2:
            finish(at - 2)
        if (which, owner) == (1, 1):
            up_load.start()
        if (which, owner) == (2, 0):
            up_load.wait()
        for t, copy in enumerate(copies):
            across = width if which == 0 else half_units
            got = None
            if owner == 1:
                started[which, 0][t].wait_recv()
                got = pltpu.make_async_copy(
                    outs[which][1].at[pl.ds(t * rows, rows)],
                    out_stage.at[:, pl.ds(0, across)],
                    core_sem.at[3, t],
                )
                got.start()
            if which == 0:
                left = weights[0, :tokens, pl.ds(pl.multiple_of(first + t * rows, rows), rows)]
                right = weights.at[2]
                slot, begin = t, 0
            else:
                left = normed[:, :, t * rows : (t + 1) * rows].reshape(tokens, rows)
                right = weights.at[1 if which == 1 else 0]
                slot, begin = t // per_slot, (t % per_slot) * half_units
            wide = min(1024, across)
            for j in range(across // wide):
                if which == 0:
                    columns = pl.ds(j * wide, wide)
                else:
                    columns = pl.ds(pl.multiple_of(first, half_units), half_units)
                product = outer_sum(left, right[:tokens, columns])
                if owner == 1:
                    if j == 0:
                        got.wait()
                    product = product + out_stage[:, j * wide : (j + 1) * wide].astype(f32)
                stage[slot, :, pl.ds(begin + j * wide, wide)] = product.astype(bf16)
            copy.start()
    finish(4)
    finish(5)
    for index in range(1, chips):
        for at in range(2):
            sum_copy(index, at).wait_send()
            sum_copy(index, at).wait_recv()
    for d in range(1, chips):
        for part in range(2):
            if relay and d == 3:
                source, way = (1, 2) if part == 0 else (2, 1)
                token_copy(3, part, normed.at[source, half(part)], partner[way]).wait_send()
            else:
                token_copy(d, part, normed_ref.at[half(part)], partner[d]).wait_send()


def feed_forward(normed, cot, own, other, down_own, down_other):
    chips, rows, width = cot.shape
    units = down_own.shape[0] * 2
    half = units // 2
    tokens = chips * rows
    tiles = width // rows
    hbm = pl.BlockSpec(memory_space=pl.ANY)
    dma = pltpu.SemaphoreType.DMA

    def low(*shape):
        return jax.ShapeDtypeStruct(shape, bf16)

    out_shape = (
        low(chips, rows, width), low(chips, rows, width),
        low(tokens, units), low(tokens, units), low(tokens, units),
        low(half, width), low(width, half), low(width, half),
        low(half, width), low(width, half), low(width, half),
    )
    depth = max(width, tokens)
    return pl.pallas_call(
        feed_kernel,
        in_specs=[hbm] * 6,
        out_specs=(hbm,) * len(out_shape),
        out_shape=out_shape,
        scratch_shapes=[
            pltpu.VMEM((3, depth, width), bf16),
            pltpu.VMEM((chips, rows, width), bf16),
            pltpu.VMEM((2, rows, width), bf16),
            pltpu.VMEM((3, rows, width), bf16),
            pltpu.VMEM((chips - 1, rows, width), bf16),
            pltpu.VMEM((rows, width), bf16),
            dma((4,)), dma((chips, 2)), dma((chips, 2)), dma((2, 2)), dma((3, 2)),
            dma((chips, 2)), dma((chips, 2)), dma((3,)), dma((2,)),
            dma((3, tiles)), dma((3, tiles)), dma((4, tiles)), dma((3 + chips,)),
        ],
        compiler_params=pltpu.CompilerParams(
            collective_id=0, has_side_effects=True, vmem_limit_bytes=63 * 2**20
        ),
        cost_estimate=pl.CostEstimate(
            flops=18 * tokens * units * width, bytes_accessed=2**27, transcendentals=tokens * units
        ),
    )(normed, cot, own, other, down_own, down_other)


def tail_kernel(
    heads,
    down_ref, gate_ref, up_ref, outs_ref, grad_ref, qkv_ref, normed_ref, attn_ref, branch_ref,
    norm_ref, seg_col_ref, seg_row_ref, cos_ref, sin_ref,
    inner_land, grad_land, turn_land, end_land, mid_land, out_land, total,
    down_result, gate_result, up_result, rest_result,
    qkv, grads, turned, sums, turned_all, normed, attn, branch, sent, core_land, sum_land,
    mine, theirs, half, whole,
    inner_send, inner_recv, grad_send, grad_recv, turn_send, turn_recv, core_send, core_recv,
    sum_send, sum_recv, part_send, part_recv, end_send, end_recv, mid_send, mid_recv, out_send, out_recv,
    self_sem, load_sem, seq_sem, tick_sem, whole_sem, total_sem,
):
    shards, seqs, span, part = qkv_ref.shape
    rows, width = normed_ref.shape
    _, owned, units = inner_land.shape[1:]
    chips = shards // 2
    chunks = end_land.shape[0]
    qkv_width = shards * part
    line = lax.axis_size("replica") == 4
    me, replica = lax.axis_index("shard"), lax.axis_index("replica")
    chip, core = me // 2, me % 2
    partner = [
        chip_at(chip, d // 2) * 2 + (core if d % 2 == 0 else 1 - core) for d in range(shards)
    ]
    is_inner = (replica == 1) | (replica == 2)
    inward = jnp.where(replica < 2, 1, 2)
    outward = jnp.where(replica < 2, 0, 3)

    def remote(source, target, send, recv, shard, to=None):
        return pltpu.make_async_remote_copy(
            src_ref=source, dst_ref=target, send_sem=send, recv_sem=recv,
            device_id=(replica if to is None else to, shard),
            device_id_type=pl.DeviceIdType.MESH,
        )

    barrier = pltpu.get_barrier_semaphore()

    def greet(to, shard):
        pl.semaphore_signal(
            barrier, inc=1, device_id=(to, shard), device_id_type=pl.DeviceIdType.MESH
        )

    for d in range(1, shards):
        greet(replica, partner[d])
    if line:

        @pl.when(is_inner)
        def _():
            greet(outward, me)
            greet(3 - replica, me)
            pl.semaphore_wait(barrier, shards + 1)

        @pl.when(jnp.logical_not(is_inner))
        def _():
            greet(inward, me)
            pl.semaphore_wait(barrier, shards)

    else:
        pl.semaphore_wait(barrier, shards - 1)

    def grad_copy(d, s):
        at = pl.ds(pl.multiple_of(s * span, span), span)
        return remote(
            grad_ref.at[partner[d], at], grad_land.at[me, at],
            grad_send.at[d, s], grad_recv.at[d, s], partner[d],
        )

    def inner_copy(which, d):
        source = (gate_ref, up_ref)[which]
        return remote(
            source.at[pl.ds(pl.multiple_of(partner[d] * owned, owned), owned)],
            inner_land.at[which, me],
            inner_send.at[which, d], inner_recv.at[which, d], partner[d],
        )

    own_grad = pltpu.make_async_copy(grad_ref.at[me], grad_land.at[me], self_sem.at[0])
    own_grad.start()
    for s in range(seqs):
        for d in range(1, shards):
            grad_copy(d, s).start()
    own_inner = [
        pltpu.make_async_copy(
            ref.at[pl.ds(pl.multiple_of(me * owned, owned), owned)],
            inner_land.at[which, me], self_sem.at[1 + which],
        )
        for which, ref in enumerate((gate_ref, up_ref))
    ]

    def start_inner(which):
        own_inner[which].start()
        for d in range(1, shards):
            inner_copy(which, d).start()

    loads = [
        pltpu.make_async_copy(ref, target, load_sem.at[i])
        for i, (ref, target) in enumerate(
            ((normed_ref, normed), (attn_ref, attn), (branch_ref, branch))
        )
    ]
    for copy in loads:
        copy.start()

    down_across = width // units
    down_chunks = down_ref.shape[0] // owned * down_across
    last_inner = down_chunks + 2 * shards

    def block(ref, row, column):
        return ref.at[
            pl.ds(pl.multiple_of(row * owned, owned), owned),
            pl.ds(pl.multiple_of(column * units, units), units),
        ]

    def source_of(c):
        if not isinstance(c, int) or c < down_chunks:
            return block(down_ref, c // down_across, c % down_across)
        if c < last_inner:
            which, d = divmod(c - down_chunks, shards)
            return inner_land.at[which, partner[d]]
        return total.at[c - last_inner]

    def place_of(c):
        if not isinstance(c, int) or c < down_chunks:
            return block(down_result, c // down_across, c % down_across)
        if c < last_inner:
            which, d = divmod(c - down_chunks, shards)
            return block((gate_result, up_result)[which], 0, partner[d])
        return block(rest_result, 0, c - last_inner)

    def end_copy(c):
        return remote(
            source_of(c), end_land.at[c], end_send.at[c], end_recv.at[c], me, inward
        )

    def mid_copy(c):
        return remote(
            half.at[c % 2], mid_land.at[c], mid_send.at[c], mid_recv.at[c], me, 3 - replica
        )

    def out_copy(c):
        return remote(
            whole.at[c % 2], place_of(c), out_send.at[c], out_recv.at[c], me, outward
        )

    def keep_copy(c):
        return pltpu.make_async_copy(whole.at[c % 2], place_of(c), whole_sem.at[c % 2])

    def from_end(c):
        @pl.when(jnp.logical_not(is_inner))
        def _():
            end_copy(c).start()

    def settle(c):
        which, d = divmod(c - down_chunks, shards)
        if d == 0:
            own_inner[which].wait()
        else:
            inner_copy(which, d).wait_recv()

    def middle(c):
        later = not isinstance(c, int)

        @pl.when(is_inner)
        def _():
            one = pltpu.make_async_copy(source_of(c), mine, tick_sem.at[0])
            one.start()
            end_copy(c).wait_recv()
            two = pltpu.make_async_copy(end_land.at[c], theirs.at[0], tick_sem.at[1])
            two.start()
            one.wait()
            two.wait()
            if later or c >= 2:
                mid_copy(c - 2).wait_send()
            half[c % 2] = (mine[...].astype(f32) + theirs[0].astype(f32)).astype(bf16)
            mid_copy(c).start()
            if later or c >= 1:
                finish(c - 1)

    def finish(c):
        mid_copy(c).wait_recv()
        two = pltpu.make_async_copy(mid_land.at[c], theirs.at[1], tick_sem.at[2])
        two.start()
        two.wait()
        if not isinstance(c, int) or c >= 2:
            out_copy(c - 2).wait_send()
            keep_copy(c - 2).wait()
        whole[c % 2] = (half[c % 2].astype(f32) + theirs[1].astype(f32)).astype(bf16)
        out_copy(c).start()
        keep_copy(c).start()

    lead = 4
    position = [0]

    def ticks(count):
        for _ in range(count):
            c = position[0]
            if c >= last_inner:
                return
            position[0] += 1
            ahead = c + lead
            if down_chunks <= ahead < last_inner:
                settle(ahead)
                if line:
                    from_end(ahead)
            if line:
                middle(c)

    if line:
        for c in range(down_chunks):
            from_end(c)
    own_grad.wait()
    ticks(3)
    start_inner(0)

    def seq_loads(s):
        at = pl.ds(pl.multiple_of(s * span, span), span)
        return [
            pltpu.make_async_copy(qkv_ref.at[:, s], qkv, seq_sem.at[0]),
            pltpu.make_async_copy(grad_land.at[:, at], grads, seq_sem.at[1]),
        ]

    def turn_copy(d, s):
        at = pl.ds(pl.multiple_of(s * span, span), span)
        return remote(
            turned.at[s, partner[d]], turn_land.at[me, at],
            turn_send.at[d, s], turn_recv.at[d, s], partner[d],
        )

    def own_turn(s):
        at = pl.ds(pl.multiple_of(s * span, span), span)
        return pltpu.make_async_copy(turned.at[s, me], turn_land.at[me, at], seq_sem.at[2 + s])

    @pl.loop(0, seqs)
    def _(s):
        for d in range(1, shards):
            grad_copy(d, s).wait_recv()
        for copy in seq_loads(s):
            copy.start()
        for copy in seq_loads(s):
            copy.wait()
        attention_back(
            heads, 256, qkv, grads, norm_ref.at[s], seg_col_ref[s], seg_row_ref[s],
            cos_ref.at[s], sin_ref.at[s], turned.at[s], sums,
        )
        own_turn(s).start()
        for d in range(1, shards):
            turn_copy(d, s).start()
        if line:
            middle(3 + s)

    if line:
        position[0] = 3 + seqs
        for c in range(down_chunks, 3 + seqs + lead):
            settle(c)
            from_end(c)
    start_inner(1)
    for s in range(seqs):
        own_turn(s).wait()
        for d in range(1, shards):
            turn_copy(d, s).wait_recv()
    take = pltpu.make_async_copy(turn_land, turned_all, load_sem.at[3])
    take.start()
    ticks(1)
    for copy in loads:
        copy.wait()
    take.wait()

    def block_of(owner, target, more=None):
        columns = pl.ds(pl.multiple_of(owner * owned, owned), owned)
        left, left_out = normed[:, columns], attn[:, columns]
        for k in range(shards + width // units):
            if k < shards:
                value = outer_sum(left, turned_all[k])
                place = slice(k * part, (k + 1) * part)
            else:
                at = (k - shards) * units
                value = outer_sum(left_out, branch[:, at : at + units])
                place = slice(qkv_width + at, qkv_width + at + units)
            if more is not None:
                value = value + more[:, place].astype(f32)
            target[:, place] = value.astype(bf16)

    def core_copy(d):
        return remote(
            sent.at[d], core_land.at[d], core_send.at[d], core_recv.at[d], partner[1]
        )

    def sum_copy(d):
        return remote(
            core_land.at[d], sum_land.at[d], sum_send.at[d], sum_recv.at[d], partner[2 * d]
        )

    def part_copy(d):
        return remote(
            outs_ref.at[chip_at(chip, d)], out_land.at[d],
            part_send.at[d], part_recv.at[d], partner[2 * d],
        )

    order = list(range(chips - 1, -1, -1))
    for d in order:
        block_of(chip_at(chip, d) * 2 + 1 - core, sent.at[d])
        core_copy(d).start()
        if d % 2 == 0:
            ticks(1)
    for d in order:
        core_copy(d).wait_recv()
        block_of(chip_at(chip, d) * 2 + core, core_land.at[d], core_land.at[d])
        if d > 0:
            sum_copy(d).start()
        if d % 2 == 0:
            ticks(1)
    for d in order[:-1]:
        part_copy(d).start()
    ticks(last_inner)
    for d in range(1, chips):
        sum_copy(d).wait_recv()
    across = total.shape[0]
    puts = []
    core_copy(0).wait_send()
    for k in range(across):
        columns = pl.ds(k * units, units)
        value = core_land[0, :, columns].astype(f32)
        for d in range(1, chips):
            value = value + sum_land[d, :, columns].astype(f32)
        sent[0, :, columns] = value.astype(bf16)
    for k in range(across):
        put = pltpu.make_async_copy(
            sent.at[0, :, pl.ds(k * units, units)], total.at[k], total_sem.at[k]
        )
        put.start()
        puts.append(put)
    for k in range(across):
        puts[k].wait()
        if line:
            from_end(last_inner + k)
    if line:
        for k in range(across):
            middle(last_inner + k)

        @pl.when(is_inner)
        def _():
            finish(chunks - 1)

    for s in range(seqs):
        for d in range(1, shards):
            grad_copy(d, s).wait_send()
            turn_copy(d, s).wait_send()
    for which in range(2):
        for d in range(1, shards):
            inner_copy(which, d).wait_send()
    for d in range(chips):
        if d > 0:
            core_copy(d).wait_send()
            sum_copy(d).wait_send()
            part_copy(d).wait_send()
            part_copy(d).wait_recv()
    if line:

        @pl.when(is_inner)
        def _():
            for c in (chunks - 2, chunks - 1):
                mid_copy(c).wait_send()
                out_copy(c).wait_send()
                keep_copy(c).wait()

        @pl.when(jnp.logical_not(is_inner))
        def _():
            for c in range(chunks):
                end_copy(c).wait_send()
                out_copy(c).wait_recv()


def tail(heads, down, gate, up, outs, grads, qkv, normed, attn, branch, norms, *tables):
    shards, seqs, span, part = qkv.shape
    rows, width = normed.shape
    units = gate.shape[1]
    owned = width // shards
    chips = shards // 2
    full = shards * part + width
    across = full // units
    chunks = (down.shape[0] // owned) * (width // units) + 2 * shards + across
    hbm = pl.BlockSpec(memory_space=pl.ANY)
    vmem = pl.BlockSpec(memory_space=pltpu.VMEM)
    dma = pltpu.SemaphoreType.DMA

    def low(*shape):
        return jax.ShapeDtypeStruct(shape, bf16)

    out_shape = (
        low(2, shards, owned, units), low(*grads.shape), low(shards, rows, part),
        low(chunks, owned, units), low(chunks, owned, units), low(*outs.shape),
        low(across, owned, units),
        low(*down.shape), low(owned, shards * units), low(owned, shards * units), low(owned, full),
    )
    length = shards * span
    wide = grads.shape[2]
    return pl.pallas_call(
        functools.partial(tail_kernel, heads),
        in_specs=[hbm] * 9 + [vmem] * 5,
        out_specs=(hbm,) * len(out_shape),
        out_shape=out_shape,
        scratch_shapes=[
            pltpu.VMEM((shards, span, part), bf16),
            pltpu.VMEM((shards, span, wide), bf16),
            pltpu.VMEM((seqs, shards, span, part), bf16),
            pltpu.VMEM((2, length, HEAD_DIM), f32),
            pltpu.VMEM((shards, rows, part), bf16),
            pltpu.VMEM((rows, width), bf16),
            pltpu.VMEM((rows, width), bf16),
            pltpu.VMEM((rows, width), bf16),
            pltpu.VMEM((chips, owned, full), bf16),
            pltpu.VMEM((chips, owned, full), bf16),
            pltpu.VMEM((chips, owned, full), bf16),
            pltpu.VMEM((owned, units), bf16),
            pltpu.VMEM((2, owned, units), bf16),
            pltpu.VMEM((2, owned, units), bf16),
            pltpu.VMEM((2, owned, units), bf16),
            dma((2, shards)), dma((2, shards)), dma((shards, seqs)), dma((shards, seqs)),
            dma((shards, seqs)), dma((shards, seqs)), dma((chips,)), dma((chips,)),
            dma((chips,)), dma((chips,)), dma((chips,)), dma((chips,)), dma((chunks,)), dma((chunks,)),
            dma((chunks,)), dma((chunks,)), dma((chunks,)), dma((chunks,)),
            dma((3,)), dma((4,)), dma((2 + seqs,)), dma((3,)), dma((2,)), dma((across,)),
        ],
        compiler_params=pltpu.CompilerParams(
            collective_id=1, has_side_effects=True, vmem_limit_bytes=62 * 2**20
        ),
        cost_estimate=pl.CostEstimate(
            flops=10 * seqs * heads * length * length * HEAD_DIM,
            bytes_accessed=2**29,
            transcendentals=seqs * heads * length * length,
        ),
    )(down, gate, up, outs, grads, qkv, normed, attn, branch, norms, *tables)


def exchange(blocks):
    return lax.all_to_all(blocks, "shard", 0, 0, tiled=True)


def tie(*values):
    return lax.optimization_barrier(values)


def norm_back(grad_normed, unit_rows, scale_rows, gain_rows):
    scaled_grad = grad_normed * gain_rows
    return scale_rows * (
        scaled_grad - unit_rows * jnp.mean(scaled_grad * unit_rows, -1, keepdims=True)
    )


def gather(block):
    return lax.all_gather(block, "shard", axis=0, tiled=True)


def body(
    tokens,
    segments,
    positions,
    cotangent,
    attention_gain,
    query_weight,
    key_weight,
    value_weight,
    output_weight,
    mlp_gain,
    gate_weight,
    up_weight,
    down_weight,
):
    seqs, span, width = tokens.shape
    shards = lax.axis_size("shard")
    me = lax.axis_index("shard")
    rows = seqs * span
    length = shards * span
    owned = query_weight.shape[0]
    heads = HEADS // shards
    copies = max(1, shards // KV_HEADS)
    wide = heads * HEAD_DIM
    part = wide + 2 * HEAD_DIM
    hidden_share = down_weight.shape[0]

    chips = shards // 2
    same_core = [[2 * k + c for k in range(chips)] for c in range(2)]
    swap = [(i, i + 1 - 2 * (i % 2)) for i in range(shards)]
    units = 2 * hidden_share
    share = owned // lax.axis_size("replica")
    gate_up_own = lax.dynamic_slice_in_dim(
        jnp.stack([gate_weight, up_weight]), lax.axis_index("replica") * share, share, 1
    )
    gate_up_own = jnp.transpose(gate_up_own.reshape(2, share, chips, units), (0, 2, 1, 3))
    gate_up_part = lax.all_to_all(
        gate_up_own, "shard", 1, 1, axis_index_groups=same_core, tiled=True
    )
    replicas = lax.axis_size("replica")
    replica = lax.axis_index("replica")

    def line_step(step, right, left):
        up_pairs = [(i, i + 1) for i in range(step - 1, replicas - 1)]
        down_pairs = [(replicas - 1 - i, replicas - 1 - j) for i, j in up_pairs]
        return lax.ppermute(right, "replica", up_pairs), lax.ppermute(left, "replica", down_pairs)

    rights, lefts = [gate_up_part], [gate_up_part]

    def advance():
        right, left = line_step(len(rights), rights[-1], lefts[-1])
        rights.append(right)
        lefts.append(left)

    advance()
    down_other = lax.ppermute(down_weight, "shard", swap)
    cot_rows = cotangent.reshape(rows, width)
    cot_all = lax.all_gather(cot_rows, "shard", axis_index_groups=same_core)

    def per_head(weight):
        return jnp.repeat(weight.reshape(owned, KV_HEADS, HEAD_DIM), copies, axis=1)

    qkv_owned = jnp.concatenate(
        [query_weight.reshape(owned, shards, wide), per_head(key_weight), per_head(value_weight)],
        -1,
    ).reshape(owned, shards * part)
    qkv_full = gather(qkv_owned)
    gains = lax.all_gather(jnp.stack([attention_gain, mlp_gain]), "shard", axis=1, tiled=True)
    gain_one, gain_two = gains[0].astype(f32), gains[1].astype(f32)
    places = lax.all_gather(jnp.stack([segments, positions]), "shard", axis=2, tiled=True)
    seg_row, seg_col = places[0][:, None, :], places[0][:, :, None]
    angle_all = jnp.swapaxes(angles(places[1]), 1, 2)
    cos_all, sin_all = jnp.cos(angle_all), jnp.sin(angle_all)
    output_full = gather(output_weight)

    x = tokens.reshape(rows, width).astype(f32)
    scale_one = lax.rsqrt(jnp.mean(x * x, -1, keepdims=True) + epsilon)
    unit_one = x * scale_one
    normed_one = (unit_one * gain_one).astype(bf16)
    projected = dot_nn(normed_one, qkv_full).reshape(rows, shards, part)
    angle = angles(positions).reshape(rows, 1, 1, HEAD_DIM // 2)
    cosine, sine = jnp.cos(angle), jnp.sin(angle)
    turning = projected[:, :, : wide + HEAD_DIM].reshape(rows, shards, heads + 1, HEAD_DIM)
    lower, upper = turning[..., : HEAD_DIM // 2], turning[..., HEAD_DIM // 2 :]
    turned = jnp.concatenate(
        [lower * cosine - upper * sine, upper * cosine + lower * sine], -1
    ).reshape(rows, shards, wide + HEAD_DIM)
    qkv_rows = jnp.concatenate([turned, projected[:, :, wide + HEAD_DIM :]], -1).astype(bf16)
    qkv_rows, rights[-1], lefts[-1] = tie(qkv_rows, rights[-1], lefts[-1])
    advance()
    qkv = exchange(jnp.swapaxes(qkv_rows, 0, 1)).reshape(shards, seqs, span, part)

    attn_heads, norms = attention_forward(heads, qkv, seg_col, seg_row)
    attn_heads, rights[-1], lefts[-1] = tie(attn_heads, rights[-1], lefts[-1])
    while len(rights) < replicas:
        advance()
    attn = exchange(attn_heads.reshape(shards, rows, wide))
    attn = jnp.swapaxes(attn, 0, 1).reshape(rows, HEADS * HEAD_DIM)
    hidden = x + dot_nn(attn, output_full)
    scale_two = lax.rsqrt(jnp.mean(hidden * hidden, -1, keepdims=True) + epsilon)
    unit_two = hidden * scale_two
    normed_two = (unit_two * gain_two).astype(bf16)

    gate_up = jnp.zeros((replicas,) + gate_up_part.shape, bf16)
    gate_up = lax.dynamic_update_index_in_dim(gate_up, gate_up_part, replica, 0)
    for step in range(1, replicas):
        block = jnp.where(replica >= step, rights[step], lefts[replicas - step])
        gate_up = lax.dynamic_update_index_in_dim(gate_up, block, (replica - step) % replicas, 0)
    gate_up_other = lax.ppermute(gate_up, "shard", swap)
    partials, outs, _, _, _, down_part, gate_part, up_part, _, _, _ = feed_forward(
        normed_two, cot_all, gate_up, gate_up_other, down_weight, down_other
    )
    grad_two = jnp.sum(partials.astype(f32), 0)
    grad_hidden = cot_rows.astype(f32) + norm_back(grad_two, unit_two, scale_two, gain_two)
    branch = grad_hidden.astype(bf16)
    grad_attn = dot_nt(branch, output_full).astype(bf16).reshape(rows, shards, wide)
    inner_blocks, _, grad_qkv, _, _, out_land, total, *summed = tail(
        heads, down_part, gate_part, up_part, outs, jnp.swapaxes(grad_attn, 0, 1), qkv, normed_one,
        attn, branch, norms, seg_col, seg_row, cos_all, sin_all,
    )
    out_sum = lax.dynamic_index_in_dim(outs, me // 2, 0, keepdims=False).astype(f32)
    out_sum = out_sum + jnp.sum(out_land[1:].astype(f32), 0)
    block_out = (hidden + out_sum).astype(bf16)
    grad_qkv = jnp.swapaxes(grad_qkv, 0, 1).reshape(rows, shards * part)
    grad_one = dot_nt(grad_qkv, qkv_full)
    if replicas != 4:

        def side_by_side(some):
            return jnp.swapaxes(some, 0, 1).reshape(owned, some.shape[0] * hidden_share)

        summed = lax.psum(
            (
                down_part, side_by_side(inner_blocks[0]), side_by_side(inner_blocks[1]),
                side_by_side(total),
            ),
            "replica",
        )
    down_grad, gate_grad, up_grad, rest = [some.astype(f32) for some in summed]
    qkv_grad = rest[:, : shards * part].reshape(owned, shards, part)
    output_grad = rest[:, shards * part :]

    own_one, own_two = attention_gain.astype(f32), mlp_gain.astype(f32)
    gain_one_grad = jnp.sum(qkv_owned.astype(f32) * rest[:, : shards * part], 1) / own_one
    gain_two_grad = (
        jnp.sum(gate_weight.astype(f32) * gate_grad + up_weight.astype(f32) * up_grad, 1) / own_two
    )

    def kv_grad(columns):
        return jnp.sum(columns.reshape(owned, KV_HEADS, copies, HEAD_DIM), 2).reshape(
            owned, KV_HEADS * HEAD_DIM
        )

    query_grad = qkv_grad[:, :, :wide].reshape(owned, HEADS * HEAD_DIM)
    key_grad = kv_grad(qkv_grad[:, :, wide : wide + HEAD_DIM])
    value_grad = kv_grad(qkv_grad[:, :, wide + HEAD_DIM :])
    token_grad = grad_hidden + norm_back(grad_one, unit_one, scale_one, gain_one)
    return (
        block_out.reshape(seqs, span, width),
        token_grad.reshape(seqs, span, width),
        gain_one_grad,
        query_grad,
        key_grad,
        value_grad,
        output_grad,
        gain_two_grad,
        gate_grad,
        up_grad,
        down_grad,
    )


def solution(mesh):
    rows = P("shard", None)
    blocks = P("replica", "shard", None)
    in_specs = (
        blocks, P("replica", "shard"), P("replica", "shard"), blocks, P("shard"),
        rows, rows, rows, rows, P("shard"), rows, rows, rows,
    )
    out_specs = (
        blocks, blocks, P("shard"), rows, rows, rows, rows, P("shard"), rows, rows, rows,
    )
    return jax.shard_map(body, mesh=mesh, in_specs=in_specs, out_specs=out_specs, check_vma=False)
```

```python
import functools
import math

import jax
import jax.numpy as jnp
from jax import lax
from jax.experimental import pallas as pl
from jax.experimental.pallas import tpu as pltpu
from jax.sharding import PartitionSpec as P

HEADS = 32
KV_HEADS = 8
HEAD_DIM = 64

epsilon = 1e-05
rope_base = 500000.0
masked_score = -1e30
f32 = jnp.float32
bf16 = jnp.bfloat16


def angles(doc_positions):
    freq_index = jnp.arange(HEAD_DIM // 2, dtype=f32)
    inverse_freq = jnp.exp(freq_index * (-2.0 * math.log(rope_base) / HEAD_DIM))
    return doc_positions.astype(f32)[..., None] * inverse_freq


def outer_sum(left, right):
    return lax.dot_general(left, right, (((0,), (0,)), ((), ())), preferred_element_type=f32)


def dot_nt(left, right):
    return lax.dot_general(left, right, (((1,), (1,)), ((), ())), preferred_element_type=f32)


def dot_nn(left, right):
    return lax.dot_general(left, right, (((1,), (0,)), ((), ())), preferred_element_type=f32)


def score_bias(seg_col, seg_row, first, rows):
    last = first + rows
    key_at = lax.broadcasted_iota(jnp.int32, (last, rows), 0)
    query_at = lax.broadcasted_iota(jnp.int32, (last, rows), 1) + first
    allowed = (seg_col[:last] == seg_row[:, first:last]) & (key_at <= query_at)
    return jnp.where(allowed, 0.0, masked_score)


def attention_fore(heads, rows, qkv_ref, seg_col, seg_row, out_ref, norm_ref):
    shards, span, _ = qkv_ref.shape
    length = shards * span
    wide = heads * HEAD_DIM
    keys = qkv_ref[:, :, wide : wide + HEAD_DIM].reshape(length, HEAD_DIM)
    values = qkv_ref[:, :, wide + HEAD_DIM :].reshape(length, HEAD_DIM)
    values_t = values.astype(f32).T.astype(bf16)
    for first in range(0, length, rows):
        last = first + rows
        at = slice(first // span, last // span)
        bias = score_bias(seg_col, seg_row, first, rows)
        queries = qkv_ref[at, :, :wide].reshape(rows, wide) * HEAD_DIM ** (-0.5)
        parts = []
        for head in range(heads):
            one = queries[:, head * HEAD_DIM : (head + 1) * HEAD_DIM]
            scores = dot_nt(keys[:last], one) + bias
            top = jnp.max(scores, 0, keepdims=True)
            lifted = jnp.exp(scores - top)
            total = jnp.sum(lifted, 0, keepdims=True)
            probs = (lifted * (1.0 / total)).astype(bf16)
            parts.append(dot_nn(values_t[:, :last], probs))
            norm_ref[head : head + 1, first:last] = top + jnp.log(total)
        out = jnp.concatenate(parts, 0).T.astype(bf16)
        out_ref[at] = out.reshape(rows // span, span, wide)


def turn_back(part, cosine, sine):
    half = HEAD_DIM // 2
    lower, upper = part[:half], part[half:]
    return [lower * cosine + upper * sine, upper * cosine - lower * sine]


def attention_back(heads, rows, qkv_ref, grad_ref, norm, seg_col, seg_row, cos, sin, out_ref, sums):
    shards, span, _ = qkv_ref.shape
    length = shards * span
    wide = heads * HEAD_DIM
    keys = qkv_ref[:, :, wide : wide + HEAD_DIM].reshape(length, HEAD_DIM)
    values = qkv_ref[:, :, wide + HEAD_DIM :].reshape(length, HEAD_DIM)
    keys_t = keys.astype(f32).T.astype(bf16)
    sums[...] = jnp.zeros_like(sums)
    key_sum, value_sum = sums.at[0], sums.at[1]
    for first in range(0, length, rows):
        last = first + rows
        at = slice(first // span, last // span)
        bias = score_bias(seg_col, seg_row, first, rows)
        queries = qkv_ref[at, :, :wide].reshape(rows, wide) * HEAD_DIM ** (-0.5)
        grads = grad_ref[at].reshape(rows, wide)
        cosine, sine = cos[:, first:last], sin[:, first:last]
        parts = []
        for head in range(heads):
            lanes = slice(head * HEAD_DIM, (head + 1) * HEAD_DIM)
            one, grad = queries[:, lanes], grads[:, lanes]
            scores = dot_nt(keys[:last], one) + bias
            probs = jnp.exp(scores - norm[head : head + 1, first:last])
            grad_probs = dot_nt(values[:last], grad)
            level = jnp.sum(probs * grad_probs, 0, keepdims=True)
            grad_scores = (probs * (grad_probs - level)).astype(bf16)
            value_sum[:last] += dot_nn(probs.astype(bf16), grad)
            key_sum[:last] += dot_nn(grad_scores, one)
            turned = dot_nn(keys_t[:, :last], grad_scores) * HEAD_DIM ** (-0.5)
            parts.extend(turn_back(turned, cosine, sine))
        out = jnp.concatenate(parts, 0).T.astype(bf16)
        out_ref[at, :, :wide] = out.reshape(rows // span, span, wide)
    key_parts = turn_back(key_sum[...].T, cos[...], sin[...])
    both = jnp.concatenate([jnp.concatenate(key_parts, 0).T, value_sum[...]], -1)
    out_ref[:, :, wide:] = both.astype(bf16).reshape(shards, span, 2 * HEAD_DIM)


def chip_at(chip, distance):
    result, bit = chip, 1
    while bit <= distance:
        if distance & bit:
            result = result + bit * (1 - 2 * ((chip // bit) % 2))
        bit *= 2
    return result


def head_kernel(
    heads,
    share_ref, weight_ref, output_ref, normed_ref, cos_ref, sin_ref, seg_col_ref, seg_row_ref,
    share_land, weight_out, output_land, qkv_land, attn_land, norm_ref,
    weights, normed, made, qkv, attended,
    share_send, share_recv, line_send, line_recv, swap_send, swap_recv,
    weight_send, weight_recv, near_send, near_recv, output_send, output_recv, close_send, close_recv,
    qkv_send, qkv_recv, attn_send, attn_recv, self_sem, load_sem,
):
    shards, owned, columns = weights.shape
    chips = shards // 2
    rows, width = normed_ref.shape
    _, seqs, span, part = qkv_land.shape
    wide = heads * HEAD_DIM
    replicas = lax.axis_size("replica")
    me, replica = lax.axis_index("shard"), lax.axis_index("replica")
    chip, core = me // 2, me % 2
    partner = [
        chip_at(chip, d // 2) * 2 + (core if d % 2 == 0 else 1 - core) for d in range(shards)
    ]
    relay = chips == 4
    half_owned = owned // 2

    def remote(source, target, send, recv, shard, to=None):
        return pltpu.make_async_remote_copy(
            src_ref=source, dst_ref=target, send_sem=send, recv_sem=recv,
            device_id=(replica if to is None else to, shard),
            device_id_type=pl.DeviceIdType.MESH,
        )

    barrier = pltpu.get_barrier_semaphore()

    def greet(to, shard):
        pl.semaphore_signal(
            barrier, inc=1, device_id=(to, shard), device_id_type=pl.DeviceIdType.MESH
        )

    for d in range(1, shards):
        greet(replica, partner[d])
    has_left, has_right = replica > 0, replica < replicas - 1

    @pl.when(has_left)
    def _():
        greet(replica - 1, me)

    @pl.when(has_right)
    def _():
        greet(replica + 1, me)

    @pl.when(has_left & has_right)
    def _():
        pl.semaphore_wait(barrier, shards + 1)

    @pl.when(jnp.logical_not(has_left & has_right))
    def _():
        pl.semaphore_wait(barrier, shards)

    def share_copy(d):
        return remote(
            share_ref.at[chip_at(chip, d)], share_land.at[core, replica, chip],
            share_send.at[d], share_recv.at[d], partner[2 * d],
        )

    own_share = pltpu.make_async_copy(
        share_ref.at[chip], share_land.at[core, replica, chip], self_sem.at[0]
    )
    own_share.start()
    for d in range(1, chips):
        share_copy(d).start()

    def rows_copies(ref, land, far_send, far_recv, side_send, side_recv):
        def half(index):
            return pl.ds(index * half_owned, half_owned)

        def far(d, index):
            if relay and d == 3:
                origin, way = (1, 2) if index == 0 else (2, 1)
                at = partner[2 * origin]
                return remote(
                    land.at[at, half(index)], land.at[at, half(index)],
                    far_send.at[d, index], far_recv.at[d, index], partner[2 * way],
                )
            return remote(
                ref.at[half(index)], land.at[me, half(index)],
                far_send.at[d, index], far_recv.at[d, index], partner[2 * d],
            )

        def near(d, index):
            at = partner[2 * d]
            source = ref.at[half(index)] if d == 0 else land.at[at, half(index)]
            return remote(
                source, land.at[at, half(index)],
                side_send.at[d, index], side_recv.at[d, index], partner[1],
            )

        return far, near

    def start_rows(far, near):
        for index in range(2):
            for d in range(1, chips):
                if not (relay and d == 3):
                    far(d, index).start()
        for index in range(2):
            near(0, index).start()

    def pass_rows(far, near):
        if relay:
            for index in range(2):
                for d in (1, 2):
                    far(d, index).wait_recv()
                far(3, index).start()
                for d in (1, 2):
                    near(d, index).start()
            for index in range(2):
                far(3, index).wait_recv()
                near(3, index).start()
        else:
            for d in range(1, chips):
                for index in range(2):
                    far(d, index).wait_recv()
                    near(d, index).start()

    def end_rows(far, near):
        for d in range(chips):
            for index in range(2):
                near(d, index).wait_recv()

    def sent_rows(far, near):
        for d in range(chips):
            for index in range(2):
                near(d, index).wait_send()
                if d > 0:
                    far(d, index).wait_send()

    weight_rows = rows_copies(
        weight_ref, weights, weight_send, weight_recv, near_send, near_recv
    )
    output_rows = rows_copies(
        output_ref, output_land, output_send, output_recv, close_send, close_recv
    )
    start_rows(*weight_rows)
    own_weight = pltpu.make_async_copy(weight_ref, weights.at[me], self_sem.at[1])
    own_weight.start()
    own_output = pltpu.make_async_copy(output_ref, output_land.at[me], self_sem.at[2])
    own_output.start()
    take_normed = pltpu.make_async_copy(normed_ref, normed, load_sem.at[0])
    take_normed.start()

    def right_copy(step):
        at = share_land.at[core, replica - step]
        return remote(at, at, line_send.at[0, step], line_recv.at[0, step], me, replica + 1)

    def left_copy(step):
        at = share_land.at[core, replica + step]
        return remote(at, at, line_send.at[1, step], line_recv.at[1, step], me, replica - 1)

    def came(way, step):
        at = share_land.at[core, replica - step - 1 if way == 0 else replica + step + 1]
        return remote(at, at, line_send.at[way, step], line_recv.at[way, step], me)

    def swap_copy(way, step):
        at = share_land.at[core, replica - step if way == 0 else replica + step]
        return remote(at, at, swap_send.at[way, step], swap_recv.at[way, step], partner[1])

    def line_step(step):
        if step == 0:
            own_share.wait()
            for d in range(1, chips):
                share_copy(d).wait_recv()
            swap_copy(0, 0).start()
        for way in range(2):
            room = replica - step >= 0 if way == 0 else replica + step < replicas
            onward = has_right if way == 0 else has_left
            if step > 0:

                @pl.when(room)
                def _():
                    came(way, step - 1).wait_recv()
                    swap_copy(way, step).start()

            if step < replicas - 1:

                @pl.when(room & onward)
                def _():
                    (right_copy if way == 0 else left_copy)(step).start()

    line_step(0)
    pass_rows(*weight_rows)
    own_weight.wait()
    take_normed.wait()
    end_rows(*weight_rows)
    keep_weight = pltpu.make_async_copy(weights, weight_out, self_sem.at[1])
    keep_weight.start()

    lane = lax.broadcasted_iota(jnp.int32, (rows, part), 1)
    lower = lane % HEAD_DIM < HEAD_DIM // 2

    def project(owner):
        at = pl.ds(pl.multiple_of(owner * part, part), part)
        value = dot_nn(normed[...], weights[:, :, at].reshape(width, part))
        swapped = jnp.where(
            lower,
            pltpu.roll(value, part - HEAD_DIM // 2, 1),
            pltpu.roll(value, HEAD_DIM // 2, 1),
        )
        turned = value * cos_ref[...] + swapped * sin_ref[...]
        made[owner] = turned.astype(bf16)

    @pl.loop(0, shards)
    def _(k):
        project(k)

    def at_seq(s):
        return pl.ds(pl.multiple_of(s * span, span), span)

    def qkv_copy(d, s):
        return remote(
            made.at[partner[d], at_seq(s)], qkv_land.at[me, s],
            qkv_send.at[d, s], qkv_recv.at[d, s], partner[d],
        )

    def own_qkv(s):
        return pltpu.make_async_copy(made.at[me, at_seq(s)], qkv_land.at[me, s], load_sem.at[1 + s])

    for s in range(seqs):
        own_qkv(s).start()
        for d in range(shards - 1, 0, -1):
            qkv_copy(d, s).start()
    start_rows(*output_rows)
    if replicas > 2:
        line_step(1)

    def attn_copy(d, s):
        return remote(
            attended.at[s, partner[d]],
            attn_land.at[at_seq(s), pl.ds(pl.multiple_of(me * wide, wide), wide)],
            attn_send.at[d, s], attn_recv.at[d, s], partner[d],
        )

    def own_attn(s):
        return pltpu.make_async_copy(
            attended.at[s, me],
            attn_land.at[at_seq(s), pl.ds(pl.multiple_of(me * wide, wide), wide)],
            load_sem.at[1 + s],
        )

    @pl.loop(0, seqs)
    def _(s):
        own_qkv(s).wait()
        for d in range(1, shards):
            qkv_copy(d, s).wait_recv()
        take = pltpu.make_async_copy(qkv_land.at[:, s], qkv, load_sem.at[0])
        take.start()
        take.wait()
        attention_fore(
            heads, 256, qkv, seg_col_ref[s], seg_row_ref[s], attended.at[s], norm_ref.at[s]
        )
        own_attn(s).start()
        for d in range(1, shards):
            attn_copy(d, s).start()

    for step in range(2 if replicas > 2 else 1, replicas - 1):
        line_step(step)
    pass_rows(*output_rows)
    for s in range(seqs):
        own_attn(s).wait()
        for d in range(1, shards):
            attn_copy(d, s).wait_recv()
    line_step(replicas - 1)

    end_rows(*output_rows)
    own_output.wait()
    keep_weight.wait()
    sent_rows(*weight_rows)
    sent_rows(*output_rows)
    for d in range(1, chips):
        share_copy(d).wait_send()
    for s in range(seqs):
        for d in range(1, shards):
            qkv_copy(d, s).wait_send()
            attn_copy(d, s).wait_send()
    swap_copy(0, 0).wait_send()
    swap_copy(0, 0).wait_recv()
    for way in range(2):
        for step in range(replicas):
            room = replica - step >= 0 if way == 0 else replica + step < replicas
            onward = has_right if way == 0 else has_left
            if step > 0:

                @pl.when(room)
                def _():
                    swap_copy(way, step).wait_send()
                    swap_copy(way, step).wait_recv()

            if step < replicas - 1:

                @pl.when(room & onward)
                def _():
                    (right_copy if way == 0 else left_copy)(step).wait_send()


def head(heads, seqs, share, weight, output, normed, cosine, sine, seg_col, seg_row):
    chips = share.shape[0]
    shards = 2 * chips
    rows, width = normed.shape
    span = rows // seqs
    owned, columns = weight.shape
    part = columns // shards
    wide = heads * HEAD_DIM
    length = shards * span
    replicas = lax.axis_size("replica")
    hbm = pl.BlockSpec(memory_space=pl.ANY)
    vmem = pl.BlockSpec(memory_space=pltpu.VMEM)
    dma = pltpu.SemaphoreType.DMA

    def low(*shape):
        return jax.ShapeDtypeStruct(shape, bf16)

    out_shape = (
        low(2, replicas, *share.shape), low(shards, owned, columns), low(shards, owned, width),
        low(shards, seqs, span, part), low(rows, shards * wide),
        jax.ShapeDtypeStruct((seqs, heads, length), f32),
    )
    return pl.pallas_call(
        functools.partial(head_kernel, heads),
        in_specs=[hbm] * 4 + [vmem] * 4,
        out_specs=(hbm,) * 5 + (vmem,),
        out_shape=out_shape,
        scratch_shapes=[
            pltpu.VMEM((shards, owned, columns), bf16),
            pltpu.VMEM((rows, width), bf16),
            pltpu.VMEM((shards, rows, part), bf16),
            pltpu.VMEM((shards, span, part), bf16),
            pltpu.VMEM((seqs, shards, span, wide), bf16),
            dma((chips,)), dma((chips,)), dma((2, replicas)), dma((2, replicas)),
            dma((2, replicas)), dma((2, replicas)),
            dma((chips, 2)), dma((chips, 2)), dma((chips, 2)), dma((chips, 2)),
            dma((chips, 2)), dma((chips, 2)), dma((chips, 2)), dma((chips, 2)),
            dma((shards, seqs)), dma((shards, seqs)), dma((shards, seqs)), dma((shards, seqs)),
            dma((3,)), dma((1 + seqs,)),
        ],
        compiler_params=pltpu.CompilerParams(
            collective_id=2, has_side_effects=True, vmem_limit_bytes=56 * 2**20
        ),
        cost_estimate=pl.CostEstimate(
            flops=4 * seqs * heads * length * length * HEAD_DIM,
            bytes_accessed=2**28,
            transcendentals=seqs * heads * length * length,
        ),
    )(share, weight, output, normed, cosine, sine, seg_col, seg_row)


def pieces_of(chips):
    if chips == 4:
        return [[(0, 0), (0, 1)], [(1, 0), (2, 0)], [(1, 1), (2, 1)], [(3, 0), (3, 1)]]
    return [[(d, 0), (d, 1)] for d in range(chips)]


def feed_kernel(
    normed_ref, cot_own_ref, share_ref, down_own_ref, down_other_ref,
    cot_ref, partial_ref, out_ref, mixed_ref, gate_ref, up_ref,
    down_own_out, gate_own_out, up_own_out, down_got, gate_got, up_got,
    weights, normed, cot, inner, sent, out_stage,
    weight_sem, normed_send, normed_recv, far_send, far_recv, cot_sem, inner_sem, sum_send, sum_recv, own_sem, out_sem,
    core_send, core_recv, core_sem, load_sem,
):
    chips, rows, width = normed.shape
    units = mixed_ref.shape[1]
    half_rows, half_units = rows // 2, units // 2
    _, replicas, _, _, share, _ = share_ref.shape
    me = lax.axis_index("shard")
    replica = lax.axis_index("replica")
    chip, core = me // 2, me % 2
    sibling = chip * 2 + (1 - core)
    partner = [chip_at(chip, d) * 2 + core for d in range(chips)]
    steps = pieces_of(chips)

    def remote(source, target, send, recv, shard):
        return pltpu.make_async_remote_copy(
            src_ref=source, dst_ref=target, send_sem=send, recv_sem=recv,
            device_id=(replica, shard), device_id_type=pl.DeviceIdType.MESH,
        )

    barrier = pltpu.get_barrier_semaphore()
    for shard in partner[1:] + [sibling]:
        pl.semaphore_signal(
            barrier, inc=1, device_id=(replica, shard), device_id_type=pl.DeviceIdType.MESH
        )
    pl.semaphore_wait(barrier, chips)

    def half(index):
        return pl.ds(index * half_rows, half_rows)

    def token_copy(distance, part, source, target):
        return remote(
            source, normed.at[distance, half(part)],
            normed_send.at[distance, part], normed_recv.at[distance, part], target,
        )

    def far_copy(distance, part, source, target):
        return remote(
            source, cot_ref.at[distance, half(part)],
            far_send.at[distance, part], far_recv.at[distance, part], target,
        )

    relay = chips == 4
    direct = range(1, 3) if relay else range(1, chips)
    for part in range(2):
        for d in direct:
            token_copy(d, part, normed_ref.at[half(part)], partner[d]).start()
        for d in direct:
            far_copy(d, part, cot_own_ref.at[half(part)], partner[d]).start()
    own_copy = pltpu.make_async_copy(normed_ref, normed.at[0], own_sem.at[0])
    own_copy.start()
    own_cot = pltpu.make_async_copy(cot_own_ref, cot_ref.at[0], own_sem.at[3])
    own_cot.start()

    def cot_copies(index):
        return [
            pltpu.make_async_copy(
                (cot_own_ref if d == 0 else cot_ref.at[d]).at[half(part)],
                cot.at[index % 2, half(at)], cot_sem.at[index % 2, at],
            )
            for at, (d, part) in enumerate(steps[index])
        ]

    for copy in cot_copies(0):
        copy.start()
    owned = share * replicas
    for which in range(2):
        for k in range(chips):
            for z in range(replicas):
                for c in range(2):
                    pltpu.make_async_copy(
                        share_ref.at[c, z, k, which],
                        weights.at[which, pl.ds((2 * k + c) * owned + z * share, share), pl.ds(0, units)],
                        weight_sem.at[which],
                    ).start()
    down_own = pltpu.make_async_copy(
        down_own_ref, weights.at[2, pl.ds(core * half_units, half_units)], weight_sem.at[2]
    )
    down_other = pltpu.make_async_copy(
        down_other_ref, weights.at[2, pl.ds((1 - core) * half_units, half_units)], weight_sem.at[3]
    )
    down_own.start()
    down_other.start()
    own_copy.wait()
    for which in range(2):
        whole = weights.at[which, pl.ds(0, width), pl.ds(0, units)]
        pltpu.make_async_copy(whole, whole, weight_sem.at[which]).wait()
    down_own.wait()
    down_other.wait()

    def inner_copies(index):
        return [
            pltpu.make_async_copy(
                inner.at[which, half(at), pl.ds(0, units)],
                ref.at[pl.ds(d * rows + part * half_rows, half_rows)],
                inner_sem.at[which, at],
            )
            for at, (d, part) in enumerate(steps[index])
            for which, ref in enumerate((mixed_ref, gate_ref, up_ref))
        ]

    def out_copies(index):
        return [
            pltpu.make_async_copy(
                out_stage.at[half(at)], out_ref.at[chip_at(chip, d), half(part)], out_sem.at[at]
            )
            for at, (d, part) in enumerate(steps[index])
        ]

    def sum_copy(index, at):
        d, part = steps[index][at]
        return remote(
            sent.at[index % (chips - 1), half(at)], partial_ref.at[d, half(part)],
            sum_send.at[d, part], sum_recv.at[d, part], partner[d],
        )

    own_sums = [
        pltpu.make_async_copy(sent.at[0, half(at)], partial_ref.at[0, half(at)], own_sem.at[1 + at])
        for at in range(2)
    ]
    tile = min(512, units)
    for index in range(chips):
        parts = steps[index]
        for d, part in parts:
            if d > 0:
                for arrive, block, own in (
                    (token_copy, normed, normed_ref), (far_copy, cot_ref, cot_own_ref)
                ):
                    if relay and d == 3:
                        origin, way = (1, 2) if part == 0 else (2, 1)
                        copy = arrive(3, part, block.at[origin, half(part)], partner[way])
                    else:
                        copy = arrive(d, part, own.at[half(part)], partner[d])
                    copy.wait_recv()
        if relay and index in (1, 2):
            part, origin, way = (0, 1, 2) if index == 1 else (1, 2, 1)
            token_copy(3, part, normed.at[origin, half(part)], partner[way]).start()
            far_copy(3, part, cot_ref.at[origin, half(part)], partner[way]).start()
        if index > 0:
            for copy in cot_copies(index):
                copy.start()
        for copy in cot_copies(index):
            copy.wait()
        if index > 0:
            for copy in inner_copies(index - 1):
                copy.wait()
        (d0, p0), (d1, p1) = parts

        @pl.loop(0, units // tile)
        def _(j):
            columns = pl.ds(pl.multiple_of(j * tile, tile), tile)
            if d0 == d1:
                block = normed[d0]
            else:
                block = jnp.concatenate([normed[d0, half(p0)], normed[d1, half(p1)]], 0)
            gate = dot_nn(block, weights[0, :width, columns])
            up = dot_nn(block, weights[1, :width, columns])
            grad = dot_nt(cot[index % 2], weights[2, columns, :])
            sigmoid = jax.nn.sigmoid(gate)
            swish = gate * sigmoid
            inner[0, :, columns] = (swish * up).astype(bf16)
            inner[1, :, columns] = (grad * up * (sigmoid + swish * (1.0 - sigmoid))).astype(bf16)
            inner[2, :, columns] = (grad * swish).astype(bf16)

        for copy in inner_copies(index):
            copy.start()
        if index > 0:
            for copy in out_copies(index - 1):
                copy.wait()
        slot = index % (chips - 1)
        if index == chips - 1:
            for copy in own_sums:
                copy.wait()

        @pl.loop(0, width // 512)
        def _(j):
            columns = pl.ds(pl.multiple_of(j * 512, 512), 512)
            sent[slot, :, columns] = (
                dot_nt(inner[1, :, :units], weights[0, columns, :units])
                + dot_nt(inner[2, :, :units], weights[1, columns, :units])
            ).astype(bf16)

        if index == 0:
            for copy in own_sums:
                copy.start()
        else:
            for at in range(2):
                sum_copy(index, at).start()

        @pl.loop(0, width // 512)
        def _(j):
            columns = pl.ds(pl.multiple_of(j * 512, 512), 512)
            out_stage[:, columns] = dot_nn(
                inner[0, :, :units], weights[2, :units, columns]
            ).astype(bf16)

        for copy in out_copies(index):
            copy.start()

    for copy in inner_copies(chips - 1):
        copy.wait()
    for copy in out_copies(chips - 1):
        copy.wait()

    tokens = chips * rows

    def load(ref, which):
        return pltpu.make_async_copy(
            ref, weights.at[which, pl.ds(0, tokens), pl.ds(0, units)], load_sem.at[which]
        )

    own_cot.wait()
    loads = [load(mixed_ref, 0), load(gate_ref, 1)]
    cot_loads = [
        pltpu.make_async_copy(
            cot_ref.at[d], weights.at[2, pl.ds(d * rows, rows)], load_sem.at[3 + d]
        )
        for d in range(chips)
    ]
    for copy in loads + cot_loads:
        copy.start()
    for copy in cot_loads + loads:
        copy.wait()
    tiles = width // rows
    per_slot = width // half_units

    def stage_copies(which, owner, stage, local, landing):
        result = []
        for t in range(tiles):
            if which == 0:
                if t >= half_units // rows:
                    break
                source, place = stage.at[t], (pl.ds(t * rows, rows),)
            else:
                source = stage.at[t // per_slot, :, pl.ds((t % per_slot) * half_units, half_units)]
                place = (pl.ds(t * rows, rows),)
            if owner == 0:
                result.append(
                    remote(
                        source, landing.at[place], core_send.at[which, t], core_recv.at[which, t],
                        sibling,
                    )
                )
            else:
                result.append(
                    pltpu.make_async_copy(source, local.at[place], core_sem.at[which, t])
                )
        return result

    outs = ((down_own_out, down_got), (gate_own_out, gate_got), (up_own_out, up_got))
    order = [(0, 0), (1, 0), (0, 1), (1, 1), (2, 0), (2, 1)]
    started = {}
    up_load = load(up_ref, 0)

    def finish(at):
        for copy in started[order[at]]:
            if order[at][1] == 0:
                copy.wait_send()
            else:
                copy.wait()

    for at, (which, owner) in enumerate(order):
        stage = cot if at % 2 == 0 else inner
        first = ((1 - core) if owner == 0 else core) * half_units
        copies = stage_copies(which, owner, stage, *outs[which])
        started[which, owner] = copies
        if at >= 2:
            finish(at - 2)
        if (which, owner) == (1, 1):
            up_load.start()
        if (which, owner) == (2, 0):
            up_load.wait()
        for t, copy in enumerate(copies):
            across = width if which == 0 else half_units
            got = None
            if owner == 1:
                started[which, 0][t].wait_recv()
                got = pltpu.make_async_copy(
                    outs[which][1].at[pl.ds(t * rows, rows)],
                    out_stage.at[:, pl.ds(0, across)],
                    core_sem.at[3, t],
                )
                got.start()
            if which == 0:
                left = weights[0, :tokens, pl.ds(pl.multiple_of(first + t * rows, rows), rows)]
                right = weights.at[2]
                slot, begin = t, 0
            else:
                left = normed[:, :, t * rows : (t + 1) * rows].reshape(tokens, rows)
                right = weights.at[1 if which == 1 else 0]
                slot, begin = t // per_slot, (t % per_slot) * half_units
            wide = min(1024, across)
            for j in range(across // wide):
                if which == 0:
                    columns = pl.ds(j * wide, wide)
                else:
                    columns = pl.ds(pl.multiple_of(first, half_units), half_units)
                product = outer_sum(left, right[:tokens, columns])
                if owner == 1:
                    if j == 0:
                        got.wait()
                    product = product + out_stage[:, j * wide : (j + 1) * wide].astype(f32)
                stage[slot, :, pl.ds(begin + j * wide, wide)] = product.astype(bf16)
            copy.start()
    finish(4)
    finish(5)
    for index in range(1, chips):
        for at in range(2):
            sum_copy(index, at).wait_send()
            sum_copy(index, at).wait_recv()
    for d in range(1, chips):
        for part in range(2):
            if relay and d == 3:
                origin, way = (1, 2) if part == 0 else (2, 1)
                token_copy(3, part, normed.at[origin, half(part)], partner[way]).wait_send()
                far_copy(3, part, cot_ref.at[origin, half(part)], partner[way]).wait_send()
            else:
                token_copy(d, part, normed_ref.at[half(part)], partner[d]).wait_send()
                far_copy(d, part, cot_own_ref.at[half(part)], partner[d]).wait_send()


def feed_forward(normed, cot, share, down_own, down_other):
    chips = share.shape[2]
    rows, width = normed.shape
    units = down_own.shape[0] * 2
    half = units // 2
    tokens = chips * rows
    tiles = width // rows
    hbm = pl.BlockSpec(memory_space=pl.ANY)
    dma = pltpu.SemaphoreType.DMA

    def low(*shape):
        return jax.ShapeDtypeStruct(shape, bf16)

    out_shape = (
        low(chips, rows, width), low(chips, rows, width), low(chips, rows, width),
        low(tokens, units), low(tokens, units), low(tokens, units),
        low(half, width), low(width, half), low(width, half),
        low(half, width), low(width, half), low(width, half),
    )
    depth = max(width, tokens)
    return pl.pallas_call(
        feed_kernel,
        in_specs=[hbm] * 5,
        out_specs=(hbm,) * len(out_shape),
        out_shape=out_shape,
        scratch_shapes=[
            pltpu.VMEM((3, depth, width), bf16),
            pltpu.VMEM((chips, rows, width), bf16),
            pltpu.VMEM((2, rows, width), bf16),
            pltpu.VMEM((3, rows, width), bf16),
            pltpu.VMEM((chips - 1, rows, width), bf16),
            pltpu.VMEM((rows, width), bf16),
            dma((4,)), dma((chips, 2)), dma((chips, 2)), dma((chips, 2)), dma((chips, 2)),
            dma((2, 2)), dma((3, 2)), dma((chips, 2)), dma((chips, 2)), dma((4,)), dma((2,)),
            dma((3, tiles)), dma((3, tiles)), dma((4, tiles)), dma((3 + chips,)),
        ],
        compiler_params=pltpu.CompilerParams(
            collective_id=0, has_side_effects=True, vmem_limit_bytes=63 * 2**20
        ),
        cost_estimate=pl.CostEstimate(
            flops=18 * tokens * units * width, bytes_accessed=2**27, transcendentals=tokens * units
        ),
    )(normed, cot, share, down_own, down_other)


def tail_kernel(
    heads,
    down_ref, gate_ref, up_ref, outs_ref, grad_ref, qkv_ref, normed_ref, attn_ref, branch_ref,
    norm_ref, seg_col_ref, seg_row_ref, cos_ref, sin_ref,
    inner_land, grad_land, turn_land, end_land, mid_land, out_land, total,
    down_result, gate_result, up_result, rest_result,
    qkv, grads, turned, sums, turned_all, normed, attn, branch, sent, core_land, sum_land,
    mine, theirs, half, whole,
    inner_send, inner_recv, grad_send, grad_recv, turn_send, turn_recv, core_send, core_recv,
    sum_send, sum_recv, part_send, part_recv, end_send, end_recv, mid_send, mid_recv, out_send, out_recv,
    self_sem, load_sem, seq_sem, tick_sem, whole_sem, total_sem,
):
    shards, seqs, span, part = qkv_ref.shape
    rows, width = normed_ref.shape
    _, owned, units = inner_land.shape[1:]
    chips = shards // 2
    chunks = end_land.shape[0]
    qkv_width = shards * part
    line = lax.axis_size("replica") == 4
    me, replica = lax.axis_index("shard"), lax.axis_index("replica")
    chip, core = me // 2, me % 2
    partner = [
        chip_at(chip, d // 2) * 2 + (core if d % 2 == 0 else 1 - core) for d in range(shards)
    ]
    is_inner = (replica == 1) | (replica == 2)
    inward = jnp.where(replica < 2, 1, 2)
    outward = jnp.where(replica < 2, 0, 3)

    def remote(source, target, send, recv, shard, to=None):
        return pltpu.make_async_remote_copy(
            src_ref=source, dst_ref=target, send_sem=send, recv_sem=recv,
            device_id=(replica if to is None else to, shard),
            device_id_type=pl.DeviceIdType.MESH,
        )

    barrier = pltpu.get_barrier_semaphore()

    def greet(to, shard):
        pl.semaphore_signal(
            barrier, inc=1, device_id=(to, shard), device_id_type=pl.DeviceIdType.MESH
        )

    for d in range(1, shards):
        greet(replica, partner[d])
    if line:

        @pl.when(is_inner)
        def _():
            greet(outward, me)
            greet(3 - replica, me)
            pl.semaphore_wait(barrier, shards + 1)

        @pl.when(jnp.logical_not(is_inner))
        def _():
            greet(inward, me)
            pl.semaphore_wait(barrier, shards)

    else:
        pl.semaphore_wait(barrier, shards - 1)

    def grad_copy(d, s):
        at = pl.ds(pl.multiple_of(s * span, span), span)
        return remote(
            grad_ref.at[partner[d], at], grad_land.at[me, at],
            grad_send.at[d, s], grad_recv.at[d, s], partner[d],
        )

    def inner_copy(which, d):
        source = (gate_ref, up_ref)[which]
        return remote(
            source.at[pl.ds(pl.multiple_of(partner[d] * owned, owned), owned)],
            inner_land.at[which, me],
            inner_send.at[which, d], inner_recv.at[which, d], partner[d],
        )

    own_grad = pltpu.make_async_copy(grad_ref.at[me], grad_land.at[me], self_sem.at[0])
    own_grad.start()
    for s in range(seqs):
        for d in range(1, shards):
            grad_copy(d, s).start()
    own_inner = [
        pltpu.make_async_copy(
            ref.at[pl.ds(pl.multiple_of(me * owned, owned), owned)],
            inner_land.at[which, me], self_sem.at[1 + which],
        )
        for which, ref in enumerate((gate_ref, up_ref))
    ]

    def start_inner(which):
        own_inner[which].start()
        for d in range(1, shards):
            inner_copy(which, d).start()

    loads = [
        pltpu.make_async_copy(ref, target, load_sem.at[i])
        for i, (ref, target) in enumerate(
            ((normed_ref, normed), (attn_ref, attn), (branch_ref, branch))
        )
    ]
    for copy in loads:
        copy.start()

    down_across = width // units
    down_chunks = down_ref.shape[0] // owned * down_across
    last_inner = down_chunks + 2 * shards

    def block(ref, row, column):
        return ref.at[
            pl.ds(pl.multiple_of(row * owned, owned), owned),
            pl.ds(pl.multiple_of(column * units, units), units),
        ]

    def source_of(c):
        if not isinstance(c, int) or c < down_chunks:
            return block(down_ref, c // down_across, c % down_across)
        if c < last_inner:
            which, d = divmod(c - down_chunks, shards)
            return inner_land.at[which, partner[d]]
        return total.at[c - last_inner]

    def place_of(c):
        if not isinstance(c, int) or c < down_chunks:
            return block(down_result, c // down_across, c % down_across)
        if c < last_inner:
            which, d = divmod(c - down_chunks, shards)
            return block((gate_result, up_result)[which], 0, partner[d])
        return block(rest_result, 0, c - last_inner)

    def end_copy(c):
        return remote(
            source_of(c), end_land.at[c], end_send.at[c], end_recv.at[c], me, inward
        )

    def mid_copy(c):
        return remote(
            half.at[c % 2], mid_land.at[c], mid_send.at[c], mid_recv.at[c], me, 3 - replica
        )

    def out_copy(c):
        return remote(
            whole.at[c % 2], place_of(c), out_send.at[c], out_recv.at[c], me, outward
        )

    def keep_copy(c):
        return pltpu.make_async_copy(whole.at[c % 2], place_of(c), whole_sem.at[c % 2])

    def from_end(c):
        @pl.when(jnp.logical_not(is_inner))
        def _():
            end_copy(c).start()

    def settle(c):
        which, d = divmod(c - down_chunks, shards)
        if d == 0:
            own_inner[which].wait()
        else:
            inner_copy(which, d).wait_recv()

    def middle(c):
        later = not isinstance(c, int)

        @pl.when(is_inner)
        def _():
            one = pltpu.make_async_copy(source_of(c), mine, tick_sem.at[0])
            one.start()
            end_copy(c).wait_recv()
            two = pltpu.make_async_copy(end_land.at[c], theirs.at[0], tick_sem.at[1])
            two.start()
            one.wait()
            two.wait()
            if later or c >= 2:
                mid_copy(c - 2).wait_send()
            half[c % 2] = (mine[...].astype(f32) + theirs[0].astype(f32)).astype(bf16)
            mid_copy(c).start()
            if later or c >= 1:
                finish(c - 1)

    def finish(c):
        mid_copy(c).wait_recv()
        two = pltpu.make_async_copy(mid_land.at[c], theirs.at[1], tick_sem.at[2])
        two.start()
        two.wait()
        if not isinstance(c, int) or c >= 2:
            out_copy(c - 2).wait_send()
            keep_copy(c - 2).wait()
        whole[c % 2] = (half[c % 2].astype(f32) + theirs[1].astype(f32)).astype(bf16)
        out_copy(c).start()
        keep_copy(c).start()

    lead = 4
    position = [0]

    def ticks(count):
        for _ in range(count):
            c = position[0]
            if c >= last_inner:
                return
            position[0] += 1
            ahead = c + lead
            if down_chunks <= ahead < last_inner:
                settle(ahead)
                if line:
                    from_end(ahead)
            if line:
                middle(c)

    if line:
        for c in range(down_chunks):
            from_end(c)
    own_grad.wait()
    ticks(3)
    start_inner(0)

    def seq_loads(s):
        at = pl.ds(pl.multiple_of(s * span, span), span)
        return [
            pltpu.make_async_copy(qkv_ref.at[:, s], qkv, seq_sem.at[0]),
            pltpu.make_async_copy(grad_land.at[:, at], grads, seq_sem.at[1]),
        ]

    def turn_copy(d, s):
        at = pl.ds(pl.multiple_of(s * span, span), span)
        return remote(
            turned.at[s, partner[d]], turn_land.at[me, at],
            turn_send.at[d, s], turn_recv.at[d, s], partner[d],
        )

    def own_turn(s):
        at = pl.ds(pl.multiple_of(s * span, span), span)
        return pltpu.make_async_copy(turned.at[s, me], turn_land.at[me, at], seq_sem.at[2 + s])

    @pl.loop(0, seqs)
    def _(s):
        for d in range(1, shards):
            grad_copy(d, s).wait_recv()
        for copy in seq_loads(s):
            copy.start()
        for copy in seq_loads(s):
            copy.wait()
        attention_back(
            heads, 256, qkv, grads, norm_ref.at[s], seg_col_ref[s], seg_row_ref[s],
            cos_ref.at[s], sin_ref.at[s], turned.at[s], sums,
        )
        own_turn(s).start()
        for d in range(1, shards):
            turn_copy(d, s).start()
        if line:
            middle(3 + s)

    if line:
        position[0] = 3 + seqs
        for c in range(down_chunks, 3 + seqs + lead):
            settle(c)
            from_end(c)
    start_inner(1)
    for s in range(seqs):
        own_turn(s).wait()
        for d in range(1, shards):
            turn_copy(d, s).wait_recv()
    take = pltpu.make_async_copy(turn_land, turned_all, load_sem.at[3])
    take.start()
    ticks(1)
    for copy in loads:
        copy.wait()
    take.wait()

    def block_of(owner, target, more=None):
        columns = pl.ds(pl.multiple_of(owner * owned, owned), owned)
        left, left_out = normed[:, columns], attn[:, columns]
        for k in range(shards + width // units):
            if k < shards:
                value = outer_sum(left, turned_all[k])
                place = slice(k * part, (k + 1) * part)
            else:
                at = (k - shards) * units
                value = outer_sum(left_out, branch[:, at : at + units])
                place = slice(qkv_width + at, qkv_width + at + units)
            if more is not None:
                value = value + more[:, place].astype(f32)
            target[:, place] = value.astype(bf16)

    def core_copy(d):
        return remote(
            sent.at[d], core_land.at[d], core_send.at[d], core_recv.at[d], partner[1]
        )

    def sum_copy(d):
        return remote(
            core_land.at[d], sum_land.at[d], sum_send.at[d], sum_recv.at[d], partner[2 * d]
        )

    def part_copy(d):
        return remote(
            outs_ref.at[chip_at(chip, d)], out_land.at[d],
            part_send.at[d], part_recv.at[d], partner[2 * d],
        )

    order = list(range(chips - 1, -1, -1))
    for d in order:
        block_of(chip_at(chip, d) * 2 + 1 - core, sent.at[d])
        core_copy(d).start()
        if d % 2 == 0:
            ticks(1)
    for d in order:
        core_copy(d).wait_recv()
        block_of(chip_at(chip, d) * 2 + core, core_land.at[d], core_land.at[d])
        if d > 0:
            sum_copy(d).start()
        if d % 2 == 0:
            ticks(1)
    for d in order[:-1]:
        part_copy(d).start()
    ticks(last_inner)
    for d in range(1, chips):
        sum_copy(d).wait_recv()
    across = total.shape[0]
    puts = []
    core_copy(0).wait_send()
    for k in range(across):
        columns = pl.ds(k * units, units)
        value = core_land[0, :, columns].astype(f32)
        for d in range(1, chips):
            value = value + sum_land[d, :, columns].astype(f32)
        sent[0, :, columns] = value.astype(bf16)
    for k in range(across):
        put = pltpu.make_async_copy(
            sent.at[0, :, pl.ds(k * units, units)], total.at[k], total_sem.at[k]
        )
        put.start()
        puts.append(put)
    for k in range(across):
        puts[k].wait()
        if line:
            from_end(last_inner + k)
    if line:
        for k in range(across):
            middle(last_inner + k)

        @pl.when(is_inner)
        def _():
            finish(chunks - 1)

    for s in range(seqs):
        for d in range(1, shards):
            grad_copy(d, s).wait_send()
            turn_copy(d, s).wait_send()
    for which in range(2):
        for d in range(1, shards):
            inner_copy(which, d).wait_send()
    for d in range(chips):
        if d > 0:
            core_copy(d).wait_send()
            sum_copy(d).wait_send()
            part_copy(d).wait_send()
            part_copy(d).wait_recv()
    if line:

        @pl.when(is_inner)
        def _():
            for c in (chunks - 2, chunks - 1):
                mid_copy(c).wait_send()
                out_copy(c).wait_send()
                keep_copy(c).wait()

        @pl.when(jnp.logical_not(is_inner))
        def _():
            for c in range(chunks):
                end_copy(c).wait_send()
                out_copy(c).wait_recv()


def tail(heads, down, gate, up, outs, grads, qkv, normed, attn, branch, norms, *tables):
    shards, seqs, span, part = qkv.shape
    rows, width = normed.shape
    units = gate.shape[1]
    owned = width // shards
    chips = shards // 2
    full = shards * part + width
    across = full // units
    chunks = (down.shape[0] // owned) * (width // units) + 2 * shards + across
    hbm = pl.BlockSpec(memory_space=pl.ANY)
    vmem = pl.BlockSpec(memory_space=pltpu.VMEM)
    dma = pltpu.SemaphoreType.DMA

    def low(*shape):
        return jax.ShapeDtypeStruct(shape, bf16)

    out_shape = (
        low(2, shards, owned, units), low(*grads.shape), low(shards, rows, part),
        low(chunks, owned, units), low(chunks, owned, units), low(*outs.shape),
        low(across, owned, units),
        low(*down.shape), low(owned, shards * units), low(owned, shards * units), low(owned, full),
    )
    length = shards * span
    wide = grads.shape[2]
    return pl.pallas_call(
        functools.partial(tail_kernel, heads),
        in_specs=[hbm] * 9 + [vmem] * 5,
        out_specs=(hbm,) * len(out_shape),
        out_shape=out_shape,
        scratch_shapes=[
            pltpu.VMEM((shards, span, part), bf16),
            pltpu.VMEM((shards, span, wide), bf16),
            pltpu.VMEM((seqs, shards, span, part), bf16),
            pltpu.VMEM((2, length, HEAD_DIM), f32),
            pltpu.VMEM((shards, rows, part), bf16),
            pltpu.VMEM((rows, width), bf16),
            pltpu.VMEM((rows, width), bf16),
            pltpu.VMEM((rows, width), bf16),
            pltpu.VMEM((chips, owned, full), bf16),
            pltpu.VMEM((chips, owned, full), bf16),
            pltpu.VMEM((chips, owned, full), bf16),
            pltpu.VMEM((owned, units), bf16),
            pltpu.VMEM((2, owned, units), bf16),
            pltpu.VMEM((2, owned, units), bf16),
            pltpu.VMEM((2, owned, units), bf16),
            dma((2, shards)), dma((2, shards)), dma((shards, seqs)), dma((shards, seqs)),
            dma((shards, seqs)), dma((shards, seqs)), dma((chips,)), dma((chips,)),
            dma((chips,)), dma((chips,)), dma((chips,)), dma((chips,)), dma((chunks,)), dma((chunks,)),
            dma((chunks,)), dma((chunks,)), dma((chunks,)), dma((chunks,)),
            dma((3,)), dma((4,)), dma((2 + seqs,)), dma((3,)), dma((2,)), dma((across,)),
        ],
        compiler_params=pltpu.CompilerParams(
            collective_id=1, has_side_effects=True, vmem_limit_bytes=62 * 2**20
        ),
        cost_estimate=pl.CostEstimate(
            flops=10 * seqs * heads * length * length * HEAD_DIM,
            bytes_accessed=2**29,
            transcendentals=seqs * heads * length * length,
        ),
    )(down, gate, up, outs, grads, qkv, normed, attn, branch, norms, *tables)


def norm_back(grad_normed, unit_rows, scale_rows, gain_rows):
    scaled_grad = grad_normed * gain_rows
    return scale_rows * (
        scaled_grad - unit_rows * jnp.mean(scaled_grad * unit_rows, -1, keepdims=True)
    )


def body(
    tokens,
    segments,
    positions,
    cotangent,
    attention_gain,
    query_weight,
    key_weight,
    value_weight,
    output_weight,
    mlp_gain,
    gate_weight,
    up_weight,
    down_weight,
):
    seqs, span, width = tokens.shape
    shards = lax.axis_size("shard")
    me = lax.axis_index("shard")
    rows = seqs * span
    length = shards * span
    owned = query_weight.shape[0]
    heads = HEADS // shards
    copies = max(1, shards // KV_HEADS)
    wide = heads * HEAD_DIM
    part = wide + 2 * HEAD_DIM
    hidden_share = down_weight.shape[0]

    chips = shards // 2
    replicas = lax.axis_size("replica")
    swap = [(i, i + 1 - 2 * (i % 2)) for i in range(shards)]

    small = jnp.concatenate(
        [
            attention_gain.astype(f32), mlp_gain.astype(f32),
            segments.astype(f32).reshape(rows), positions.astype(f32).reshape(rows),
        ]
    )
    small = lax.all_gather(small, "shard")
    gain_one, gain_two = small[:, :owned].reshape(width), small[:, owned : 2 * owned].reshape(width)
    places = jnp.swapaxes(small[:, 2 * owned :].reshape(shards, 2, seqs, span), 0, 1)
    places = jnp.swapaxes(places, 1, 2).reshape(2, seqs, length)
    seg_row, seg_col = places[0][:, None, :], places[0][:, :, None]
    angle_all = jnp.swapaxes(angles(places[1]), 1, 2)
    cos_all, sin_all = jnp.cos(angle_all), jnp.sin(angle_all)

    share = owned // replicas
    units = 2 * hidden_share
    share_own = lax.dynamic_slice_in_dim(
        jnp.stack([gate_weight, up_weight]), lax.axis_index("replica") * share, share, 1
    )
    share_own = jnp.transpose(share_own.reshape(2, share, chips, units), (2, 0, 1, 3))
    down_other = lax.ppermute(down_weight, "shard", swap)

    def per_head(weight):
        return jnp.repeat(weight.reshape(owned, KV_HEADS, HEAD_DIM), copies, axis=1)

    qkv_owned = jnp.concatenate(
        [query_weight.reshape(owned, shards, wide), per_head(key_weight), per_head(value_weight)],
        -1,
    ).reshape(owned, shards * part)

    x = tokens.reshape(rows, width).astype(f32)
    scale_one = lax.rsqrt(jnp.mean(x * x, -1, keepdims=True) + epsilon)
    unit_one = x * scale_one
    normed_one = (unit_one * gain_one).astype(bf16)
    angle = angles(positions).reshape(rows, HEAD_DIM // 2)
    cosine, sine = jnp.cos(angle), jnp.sin(angle)
    still = jnp.ones((rows, HEAD_DIM), f32)
    cos_lanes = jnp.concatenate([cosine] * (2 * heads + 2) + [still], 1)
    sin_lanes = jnp.concatenate([-sine, sine] * (heads + 1) + [still * 0.0], 1)
    shares, qkv_full, output_full, qkv, attn, norms = head(
        heads, seqs, share_own, qkv_owned, output_weight, normed_one, cos_lanes, sin_lanes,
        seg_col, seg_row,
    )
    qkv_full = qkv_full.reshape(width, shards * part)
    output_full = output_full.reshape(width, width)
    hidden = x + dot_nn(attn, output_full)
    scale_two = lax.rsqrt(jnp.mean(hidden * hidden, -1, keepdims=True) + epsilon)
    unit_two = hidden * scale_two
    normed_two = (unit_two * gain_two).astype(bf16)

    cot_rows = cotangent.reshape(rows, width)
    _, partials, outs, _, _, _, down_part, gate_part, up_part, _, _, _ = feed_forward(
        normed_two, cot_rows, shares, down_weight, down_other
    )
    grad_two = jnp.sum(partials.astype(f32), 0)
    grad_hidden = cot_rows.astype(f32) + norm_back(grad_two, unit_two, scale_two, gain_two)
    branch = grad_hidden.astype(bf16)
    grad_attn = dot_nt(branch, output_full).astype(bf16).reshape(rows, shards, wide)
    inner_blocks, _, grad_qkv, _, _, out_land, total, *summed = tail(
        heads, down_part, gate_part, up_part, outs, jnp.swapaxes(grad_attn, 0, 1), qkv, normed_one,
        attn, branch, norms, seg_col, seg_row, cos_all, sin_all,
    )
    out_sum = lax.dynamic_index_in_dim(outs, me // 2, 0, keepdims=False).astype(f32)
    out_sum = out_sum + jnp.sum(out_land[1:].astype(f32), 0)
    block_out = (hidden + out_sum).astype(bf16)
    grad_qkv = jnp.swapaxes(grad_qkv, 0, 1).reshape(rows, shards * part)
    grad_one = dot_nt(grad_qkv, qkv_full)
    if replicas != 4:

        def side_by_side(some):
            return jnp.swapaxes(some, 0, 1).reshape(owned, some.shape[0] * hidden_share)

        summed = lax.psum(
            (
                down_part, side_by_side(inner_blocks[0]), side_by_side(inner_blocks[1]),
                side_by_side(total),
            ),
            "replica",
        )
    down_grad, gate_grad, up_grad, rest = [some.astype(f32) for some in summed]
    qkv_grad = rest[:, : shards * part].reshape(owned, shards, part)
    output_grad = rest[:, shards * part :]

    own_one, own_two = attention_gain.astype(f32), mlp_gain.astype(f32)
    gain_one_grad = jnp.sum(qkv_owned.astype(f32) * rest[:, : shards * part], 1) / own_one
    gain_two_grad = (
        jnp.sum(gate_weight.astype(f32) * gate_grad + up_weight.astype(f32) * up_grad, 1) / own_two
    )

    def kv_grad(columns):
        return jnp.sum(columns.reshape(owned, KV_HEADS, copies, HEAD_DIM), 2).reshape(
            owned, KV_HEADS * HEAD_DIM
        )

    query_grad = qkv_grad[:, :, :wide].reshape(owned, HEADS * HEAD_DIM)
    key_grad = kv_grad(qkv_grad[:, :, wide : wide + HEAD_DIM])
    value_grad = kv_grad(qkv_grad[:, :, wide + HEAD_DIM :])
    token_grad = grad_hidden + norm_back(grad_one, unit_one, scale_one, gain_one)
    return (
        block_out.reshape(seqs, span, width),
        token_grad.reshape(seqs, span, width),
        gain_one_grad,
        query_grad,
        key_grad,
        value_grad,
        output_grad,
        gain_two_grad,
        gate_grad,
        up_grad,
        down_grad,
    )


def solution(mesh):
    rows = P("shard", None)
    blocks = P("replica", "shard", None)
    in_specs = (
        blocks, P("replica", "shard"), P("replica", "shard"), blocks, P("shard"),
        rows, rows, rows, rows, P("shard"), rows, rows, rows,
    )
    out_specs = (
        blocks, blocks, P("shard"), rows, rows, rows, rows, P("shard"), rows, rows, rows,
    )
    return jax.shard_map(body, mesh=mesh, in_specs=in_specs, out_specs=out_specs, check_vma=False)
```

```python
import functools
import math

import jax
import jax.numpy as jnp
from jax import lax
from jax.experimental import pallas as pl
from jax.experimental.pallas import tpu as pltpu
from jax.sharding import PartitionSpec as P

HEADS = 32
KV_HEADS = 8
HEAD_DIM = 64

epsilon = 1e-05
rope_base = 500000.0
masked_score = -1e30
f32 = jnp.float32
bf16 = jnp.bfloat16


def angles(doc_positions):
    freq_index = jnp.arange(HEAD_DIM // 2, dtype=f32)
    inverse_freq = jnp.exp(freq_index * (-2.0 * math.log(rope_base) / HEAD_DIM))
    return doc_positions.astype(f32)[..., None] * inverse_freq


def outer_sum(left, right):
    return lax.dot_general(left, right, (((0,), (0,)), ((), ())), preferred_element_type=f32)


def dot_nt(left, right):
    return lax.dot_general(left, right, (((1,), (1,)), ((), ())), preferred_element_type=f32)


def dot_nn(left, right):
    return lax.dot_general(left, right, (((1,), (0,)), ((), ())), preferred_element_type=f32)


def score_bias(seg_col, seg_row, first, rows):
    last = first + rows
    key_at = lax.broadcasted_iota(jnp.int32, (last, rows), 0)
    query_at = lax.broadcasted_iota(jnp.int32, (last, rows), 1) + first
    allowed = (seg_col[:last] == seg_row[:, first:last]) & (key_at <= query_at)
    return jnp.where(allowed, 0.0, masked_score)


def attention_fore(heads, rows, qkv_ref, seg_col, seg_row, out_ref, norm_ref):
    shards, span, _ = qkv_ref.shape
    length = shards * span
    wide = heads * HEAD_DIM
    keys = qkv_ref[:, :, wide : wide + HEAD_DIM].reshape(length, HEAD_DIM)
    values = qkv_ref[:, :, wide + HEAD_DIM :].reshape(length, HEAD_DIM)
    values_t = values.astype(f32).T.astype(bf16)
    for first in range(0, length, rows):
        last = first + rows
        at = slice(first // span, last // span)
        bias = score_bias(seg_col, seg_row, first, rows)
        queries = qkv_ref[at, :, :wide].reshape(rows, wide) * HEAD_DIM ** (-0.5)
        parts = []
        for head in range(heads):
            one = queries[:, head * HEAD_DIM : (head + 1) * HEAD_DIM]
            scores = dot_nt(keys[:last], one) + bias
            top = jnp.max(scores, 0, keepdims=True)
            lifted = jnp.exp(scores - top)
            total = jnp.sum(lifted, 0, keepdims=True)
            probs = (lifted * (1.0 / total)).astype(bf16)
            parts.append(dot_nn(values_t[:, :last], probs))
            norm_ref[head : head + 1, first:last] = top + jnp.log(total)
        out = jnp.concatenate(parts, 0).T.astype(bf16)
        out_ref[at] = out.reshape(rows // span, span, wide)


def turn_back(part, cosine, sine):
    half = HEAD_DIM // 2
    lower, upper = part[:half], part[half:]
    return [lower * cosine + upper * sine, upper * cosine - lower * sine]


def attention_back(
    heads, rows, qkv_ref, grad_ref, norm, seg_col, seg_row, cos, sin, out_ref, sums, between
):
    shards, span, _ = qkv_ref.shape
    length = shards * span
    wide = heads * HEAD_DIM
    keys = qkv_ref[:, :, wide : wide + HEAD_DIM].reshape(length, HEAD_DIM)
    values = qkv_ref[:, :, wide + HEAD_DIM :].reshape(length, HEAD_DIM)
    keys_t = keys.astype(f32).T.astype(bf16)
    sums[...] = jnp.zeros_like(sums)
    key_sum, value_sum = sums.at[0], sums.at[1]
    for first in range(0, length, rows):
        last = first + rows
        at = slice(first // span, last // span)
        bias = score_bias(seg_col, seg_row, first, rows)
        queries = qkv_ref[at, :, :wide].reshape(rows, wide) * HEAD_DIM ** (-0.5)
        grads = grad_ref[at].reshape(rows, wide)
        cosine, sine = cos[:, first:last], sin[:, first:last]
        parts = []
        for head in range(heads):
            lanes = slice(head * HEAD_DIM, (head + 1) * HEAD_DIM)
            one, grad = queries[:, lanes], grads[:, lanes]
            scores = dot_nt(keys[:last], one) + bias
            probs = jnp.exp(scores - norm[head : head + 1, first:last])
            grad_probs = dot_nt(values[:last], grad)
            level = jnp.sum(probs * grad_probs, 0, keepdims=True)
            grad_scores = (probs * (grad_probs - level)).astype(bf16)
            value_sum[:last] += dot_nn(probs.astype(bf16), grad)
            key_sum[:last] += dot_nn(grad_scores, one)
            turned = dot_nn(keys_t[:, :last], grad_scores) * HEAD_DIM ** (-0.5)
            parts.extend(turn_back(turned, cosine, sine))
        out = jnp.concatenate(parts, 0).T.astype(bf16)
        out_ref[at, :, :wide] = out.reshape(rows // span, span, wide)
        if last * 4 == length * 3:
            between()
    key_parts = turn_back(key_sum[...].T, cos[...], sin[...])
    both = jnp.concatenate([jnp.concatenate(key_parts, 0).T, value_sum[...]], -1)
    out_ref[:, :, wide:] = both.astype(bf16).reshape(shards, span, 2 * HEAD_DIM)


def chip_at(chip, distance):
    result, bit = chip, 1
    while bit <= distance:
        if distance & bit:
            result = result + bit * (1 - 2 * ((chip // bit) % 2))
        bit *= 2
    return result


def head_kernel(
    heads,
    share_ref, weight_ref, output_ref, normed_ref, cos_ref, sin_ref, seg_col_ref, seg_row_ref,
    share_land, weight_out, output_land, qkv_land, attn_land, norm_ref,
    weights, normed, made, qkv, attended,
    share_send, share_recv, line_send, line_recv, swap_send, swap_recv,
    weight_send, weight_recv, near_send, near_recv, output_send, output_recv, close_send, close_recv,
    qkv_send, qkv_recv, attn_send, attn_recv, self_sem, load_sem,
):
    shards, owned, columns = weights.shape
    chips = shards // 2
    rows, width = normed_ref.shape
    _, seqs, span, part = qkv_land.shape
    wide = heads * HEAD_DIM
    replicas = lax.axis_size("replica")
    me, replica = lax.axis_index("shard"), lax.axis_index("replica")
    chip, core = me // 2, me % 2
    partner = [
        chip_at(chip, d // 2) * 2 + (core if d % 2 == 0 else 1 - core) for d in range(shards)
    ]
    relay = chips == 4
    half_owned = owned // 2

    def remote(source, target, send, recv, shard, to=None):
        return pltpu.make_async_remote_copy(
            src_ref=source, dst_ref=target, send_sem=send, recv_sem=recv,
            device_id=(replica if to is None else to, shard),
            device_id_type=pl.DeviceIdType.MESH,
        )

    barrier = pltpu.get_barrier_semaphore()

    def greet(to, shard):
        pl.semaphore_signal(
            barrier, inc=1, device_id=(to, shard), device_id_type=pl.DeviceIdType.MESH
        )

    for d in range(1, shards):
        greet(replica, partner[d])
    has_left, has_right = replica > 0, replica < replicas - 1

    @pl.when(has_left)
    def _():
        greet(replica - 1, me)

    @pl.when(has_right)
    def _():
        greet(replica + 1, me)

    @pl.when(has_left & has_right)
    def _():
        pl.semaphore_wait(barrier, shards + 1)

    @pl.when(jnp.logical_not(has_left & has_right))
    def _():
        pl.semaphore_wait(barrier, shards)

    def share_copy(d):
        return remote(
            share_ref.at[chip_at(chip, d)], share_land.at[core, replica, chip],
            share_send.at[d], share_recv.at[d], partner[2 * d],
        )

    own_share = pltpu.make_async_copy(
        share_ref.at[chip], share_land.at[core, replica, chip], self_sem.at[0]
    )
    own_share.start()
    for d in range(1, chips):
        share_copy(d).start()

    def rows_copies(ref, land, far_send, far_recv, side_send, side_recv):
        def half(index):
            return pl.ds(index * half_owned, half_owned)

        def far(d, index):
            if relay and d == 3:
                origin, way = (1, 2) if index == 0 else (2, 1)
                at = partner[2 * origin]
                return remote(
                    land.at[at, half(index)], land.at[at, half(index)],
                    far_send.at[d, index], far_recv.at[d, index], partner[2 * way],
                )
            return remote(
                ref.at[half(index)], land.at[me, half(index)],
                far_send.at[d, index], far_recv.at[d, index], partner[2 * d],
            )

        def near(d, index):
            at = partner[2 * d]
            source = ref.at[half(index)] if d == 0 else land.at[at, half(index)]
            return remote(
                source, land.at[at, half(index)],
                side_send.at[d, index], side_recv.at[d, index], partner[1],
            )

        return far, near

    def start_rows(far, near):
        for index in range(2):
            for d in range(1, chips):
                if not (relay and d == 3):
                    far(d, index).start()
        for index in range(2):
            near(0, index).start()

    def pass_rows(far, near, between=None):
        if relay:
            for index in range(2):
                for d in (1, 2):
                    far(d, index).wait_recv()
                far(3, index).start()
                for d in (1, 2):
                    near(d, index).start()
                if between is not None:
                    between(index)
            for index in range(2):
                far(3, index).wait_recv()
                near(3, index).start()
        else:
            for d in range(1, chips):
                for index in range(2):
                    far(d, index).wait_recv()
                    near(d, index).start()

    def end_rows(far, near):
        for d in range(chips):
            for index in range(2):
                near(d, index).wait_recv()

    def sent_rows(far, near):
        for d in range(chips):
            for index in range(2):
                near(d, index).wait_send()
                if d > 0:
                    far(d, index).wait_send()

    weight_rows = rows_copies(
        weight_ref, weights, weight_send, weight_recv, near_send, near_recv
    )
    output_rows = rows_copies(
        output_ref, output_land, output_send, output_recv, close_send, close_recv
    )
    own_weight = pltpu.make_async_copy(weight_ref, weights.at[me], self_sem.at[1])
    own_weight.start()
    own_output = pltpu.make_async_copy(output_ref, output_land.at[me], self_sem.at[2])
    own_output.start()
    take_normed = pltpu.make_async_copy(normed_ref, normed, load_sem.at[0])
    take_normed.start()

    def share_at(way, distance, index):
        far = replica - distance if way == 0 else replica + distance
        return share_land.at[core, far, pl.ds(index * (chips // 2), chips // 2)]

    def line_copy(way, step, index):
        at = share_at(way, step, index)
        return remote(
            at, at, line_send.at[way, step, index], line_recv.at[way, step, index], me,
            replica + 1 if way == 0 else replica - 1,
        )

    def came(way, step, index):
        at = share_at(way, step + 1, index)
        return remote(
            at, at, line_send.at[way, step, index], line_recv.at[way, step, index], me
        )

    def swap_copy(way, step, index):
        at = share_at(way, step, index)
        return remote(
            at, at, swap_send.at[way, step, index], swap_recv.at[way, step, index], partner[1]
        )

    def line_step(step, index):
        if step == 0 and index == 0:
            own_share.wait()
            for d in range(1, chips):
                share_copy(d).wait_recv()
        if step == 0:
            swap_copy(0, 0, index).start()
        for way in range(2):
            room = replica - step >= 0 if way == 0 else replica + step < replicas
            onward = has_right if way == 0 else has_left
            if step > 0:

                @pl.when(room)
                def _():
                    came(way, step - 1, index).wait_recv()
                    swap_copy(way, step, index).start()

            if step < replicas - 1:

                @pl.when(room & onward)
                def _():
                    line_copy(way, step, index).start()

    line_step(0, 0)
    line_step(0, 1)
    start_rows(*weight_rows)
    if relay and replicas > 2:
        pass_rows(*weight_rows, between=lambda index: line_step(1, index))
    else:
        pass_rows(*weight_rows)
        if replicas > 2:
            line_step(1, 0)
            line_step(1, 1)
    own_weight.wait()
    take_normed.wait()
    end_rows(*weight_rows)
    keep_weight = pltpu.make_async_copy(weights, weight_out, self_sem.at[1])
    keep_weight.start()

    lane = lax.broadcasted_iota(jnp.int32, (rows, part), 1)
    lower = lane % HEAD_DIM < HEAD_DIM // 2

    def project(owner):
        at = pl.ds(pl.multiple_of(owner * part, part), part)
        value = dot_nn(normed[...], weights[:, :, at].reshape(width, part))
        swapped = jnp.where(
            lower,
            pltpu.roll(value, part - HEAD_DIM // 2, 1),
            pltpu.roll(value, HEAD_DIM // 2, 1),
        )
        turned = value * cos_ref[...] + swapped * sin_ref[...]
        made[owner] = turned.astype(bf16)

    @pl.loop(0, shards)
    def _(k):
        project(k)

    def at_seq(s):
        return pl.ds(pl.multiple_of(s * span, span), span)

    def qkv_copy(d, s):
        return remote(
            made.at[partner[d], at_seq(s)], qkv_land.at[me, s],
            qkv_send.at[d, s], qkv_recv.at[d, s], partner[d],
        )

    def own_qkv(s):
        return pltpu.make_async_copy(made.at[me, at_seq(s)], qkv_land.at[me, s], load_sem.at[1 + s])

    for s in range(seqs):
        own_qkv(s).start()
        for d in range(shards - 1, 0, -1):
            qkv_copy(d, s).start()
    start_rows(*output_rows)
    if replicas > 3:
        line_step(2, 0)

    def attn_copy(d, s):
        return remote(
            attended.at[s, partner[d]],
            attn_land.at[at_seq(s), pl.ds(pl.multiple_of(me * wide, wide), wide)],
            attn_send.at[d, s], attn_recv.at[d, s], partner[d],
        )

    def own_attn(s):
        return pltpu.make_async_copy(
            attended.at[s, me],
            attn_land.at[at_seq(s), pl.ds(pl.multiple_of(me * wide, wide), wide)],
            load_sem.at[1 + s],
        )

    @pl.loop(0, seqs)
    def _(s):
        own_qkv(s).wait()
        for d in range(1, shards):
            qkv_copy(d, s).wait_recv()
        take = pltpu.make_async_copy(qkv_land.at[:, s], qkv, load_sem.at[0])
        take.start()
        take.wait()
        attention_fore(
            heads, 256, qkv, seg_col_ref[s], seg_row_ref[s], attended.at[s], norm_ref.at[s]
        )
        own_attn(s).start()
        for d in range(1, shards):
            attn_copy(d, s).start()
        if replicas > 3:

            @pl.when(s == 0)
            def _():
                line_step(2, 1)

    for step in range(2, replicas):
        for index in range(2):
            if (step, index) not in ((2, 0), (2, 1)) and step < replicas - 1:
                line_step(step, index)
    pass_rows(*output_rows)
    for s in range(seqs):
        own_attn(s).wait()
        for d in range(1, shards):
            attn_copy(d, s).wait_recv()
    line_step(replicas - 1, 0)
    line_step(replicas - 1, 1)

    end_rows(*output_rows)
    own_output.wait()
    keep_weight.wait()
    sent_rows(*weight_rows)
    sent_rows(*output_rows)
    for d in range(1, chips):
        share_copy(d).wait_send()
    for s in range(seqs):
        for d in range(1, shards):
            qkv_copy(d, s).wait_send()
            attn_copy(d, s).wait_send()
    for index in range(2):
        swap_copy(0, 0, index).wait_send()
        swap_copy(0, 0, index).wait_recv()
        for way in range(2):
            for step in range(replicas):
                room = replica - step >= 0 if way == 0 else replica + step < replicas
                onward = has_right if way == 0 else has_left
                if step > 0:

                    @pl.when(room)
                    def _():
                        swap_copy(way, step, index).wait_send()
                        swap_copy(way, step, index).wait_recv()

                if step < replicas - 1:

                    @pl.when(room & onward)
                    def _():
                        line_copy(way, step, index).wait_send()


def head(heads, seqs, share, weight, output, normed, cosine, sine, seg_col, seg_row):
    chips = share.shape[0]
    shards = 2 * chips
    rows, width = normed.shape
    span = rows // seqs
    owned, columns = weight.shape
    part = columns // shards
    wide = heads * HEAD_DIM
    length = shards * span
    replicas = lax.axis_size("replica")
    hbm = pl.BlockSpec(memory_space=pl.ANY)
    vmem = pl.BlockSpec(memory_space=pltpu.VMEM)
    dma = pltpu.SemaphoreType.DMA

    def low(*shape):
        return jax.ShapeDtypeStruct(shape, bf16)

    out_shape = (
        low(2, replicas, *share.shape), low(shards, owned, columns), low(shards, owned, width),
        low(shards, seqs, span, part), low(rows, shards * wide),
        jax.ShapeDtypeStruct((seqs, heads, length), f32),
    )
    return pl.pallas_call(
        functools.partial(head_kernel, heads),
        in_specs=[hbm] * 4 + [vmem] * 4,
        out_specs=(hbm,) * 5 + (vmem,),
        out_shape=out_shape,
        scratch_shapes=[
            pltpu.VMEM((shards, owned, columns), bf16),
            pltpu.VMEM((rows, width), bf16),
            pltpu.VMEM((shards, rows, part), bf16),
            pltpu.VMEM((shards, span, part), bf16),
            pltpu.VMEM((seqs, shards, span, wide), bf16),
            dma((chips,)), dma((chips,)), dma((2, replicas, 2)), dma((2, replicas, 2)),
            dma((2, replicas, 2)), dma((2, replicas, 2)),
            dma((chips, 2)), dma((chips, 2)), dma((chips, 2)), dma((chips, 2)),
            dma((chips, 2)), dma((chips, 2)), dma((chips, 2)), dma((chips, 2)),
            dma((shards, seqs)), dma((shards, seqs)), dma((shards, seqs)), dma((shards, seqs)),
            dma((3,)), dma((1 + seqs,)),
        ],
        compiler_params=pltpu.CompilerParams(
            collective_id=2, has_side_effects=True, vmem_limit_bytes=56 * 2**20
        ),
        cost_estimate=pl.CostEstimate(
            flops=4 * seqs * heads * length * length * HEAD_DIM,
            bytes_accessed=2**28,
            transcendentals=seqs * heads * length * length,
        ),
    )(share, weight, output, normed, cosine, sine, seg_col, seg_row)


def pieces_of(chips):
    if chips == 4:
        return [[(0, 0), (0, 1)], [(1, 0), (2, 0)], [(1, 1), (2, 1)], [(3, 0), (3, 1)]]
    return [[(d, 0), (d, 1)] for d in range(chips)]


def feed_kernel(
    normed_ref, cot_own_ref, share_ref, down_own_ref, down_other_ref,
    normed_out, cot_ref, partial_ref, late_ref, out_ref, mixed_ref, gate_ref, up_ref,
    weights, normed, cot, inner, sent, out_stage,
    weight_sem, normed_send, normed_recv, far_send, far_recv, cot_sem, inner_sem,
    sum_send, sum_recv, own_sem, late_sem, out_sem, keep_sem,
):
    chips, rows, width = normed.shape
    units = mixed_ref.shape[1]
    half_rows, half_units = rows // 2, units // 2
    _, replicas, _, _, share, _ = share_ref.shape
    me = lax.axis_index("shard")
    replica = lax.axis_index("replica")
    chip, core = me // 2, me % 2
    partner = [chip_at(chip, d) * 2 + core for d in range(chips)]
    steps = pieces_of(chips)
    spot = {piece: (i, at) for i, step in enumerate(steps) for at, piece in enumerate(step)}
    relay = chips == 4

    def remote(source, target, send, recv, shard):
        return pltpu.make_async_remote_copy(
            src_ref=source, dst_ref=target, send_sem=send, recv_sem=recv,
            device_id=(replica, shard), device_id_type=pl.DeviceIdType.MESH,
        )

    barrier = pltpu.get_barrier_semaphore()
    for shard in partner[1:]:
        pl.semaphore_signal(
            barrier, inc=1, device_id=(replica, shard), device_id_type=pl.DeviceIdType.MESH
        )
    pl.semaphore_wait(barrier, chips - 1)

    def half(index):
        return pl.ds(index * half_rows, half_rows)

    def block_copy(which, d, part):
        own, land = ((normed_ref, normed), (cot_own_ref, cot_ref))[which]
        send, recv = ((normed_send, normed_recv), (far_send, far_recv))[which]
        index, at = spot[d, part]
        if relay and d == 3:
            origin, way = (1, 2) if part == 0 else (2, 1)
            from_index, from_at = spot[origin, part]
            source, to = land.at[from_index, half(from_at)], partner[way]
        else:
            source, to = own.at[half(part)], partner[d]
        return remote(source, land.at[index, half(at)], send.at[d, part], recv.at[d, part], to)

    for part in range(2):
        for which in range(2):
            for d in range(1, 3 if relay else chips):
                block_copy(which, d, part).start()
    own_copy = pltpu.make_async_copy(normed_ref, normed.at[0], own_sem.at[0])
    own_copy.start()
    own_cot = pltpu.make_async_copy(cot_own_ref, cot_ref.at[0], own_sem.at[1])
    own_cot.start()

    def cot_copy(index):
        source = cot_own_ref if index == 0 else cot_ref.at[index]
        return pltpu.make_async_copy(source, cot.at[index % 2], cot_sem.at[index % 2])

    cot_copy(0).start()
    owned = share * replicas
    for which in range(2):
        for k in range(chips):
            for z in range(replicas):
                for c in range(2):
                    pltpu.make_async_copy(
                        share_ref.at[c, z, k, which],
                        weights.at[which, pl.ds((2 * k + c) * owned + z * share, share), pl.ds(0, units)],
                        weight_sem.at[which],
                    ).start()
    down_own = pltpu.make_async_copy(
        down_own_ref, weights.at[2, pl.ds(core * half_units, half_units)], weight_sem.at[2]
    )
    down_other = pltpu.make_async_copy(
        down_other_ref, weights.at[2, pl.ds((1 - core) * half_units, half_units)], weight_sem.at[3]
    )
    down_own.start()
    down_other.start()
    own_copy.wait()
    for which in range(2):
        whole = weights.at[which, pl.ds(0, width), pl.ds(0, units)]
        pltpu.make_async_copy(whole, whole, weight_sem.at[which]).wait()
    down_own.wait()
    down_other.wait()

    def inner_copies(index):
        return [
            pltpu.make_async_copy(
                inner.at[which], ref.at[pl.ds(index * rows, rows)], inner_sem.at[which]
            )
            for which, ref in enumerate((mixed_ref, gate_ref, up_ref))
        ]

    def out_copies(index):
        return [
            pltpu.make_async_copy(
                out_stage.at[half(at)], out_ref.at[chip_at(chip, d), half(part)], out_sem.at[at]
            )
            for at, (d, part) in enumerate(steps[index])
        ]

    def sum_copy(index, at):
        d, part = steps[index][at]
        return remote(
            sent.at[index % 2, half(at)], partial_ref.at[d, half(part)],
            sum_send.at[d, part], sum_recv.at[d, part], partner[d],
        )

    own_sum = pltpu.make_async_copy(sent.at[0], partial_ref.at[0], own_sem.at[2])
    late_sum = pltpu.make_async_copy(sent.at[(chips - 1) % 2], late_ref, late_sem)
    keep_normed = pltpu.make_async_copy(normed, normed_out, keep_sem)
    tile = min(512, units)
    for index in range(chips):
        for d, part in steps[index]:
            if d > 0:
                block_copy(0, d, part).wait_recv()
                block_copy(1, d, part).wait_recv()
        if relay and index in (1, 2):
            for which in range(2):
                block_copy(which, 3, index - 1).start()
        if index > 0:
            cot_copy(index).start()
        if index == chips - 1:
            keep_normed.start()
        if index > 0:
            for copy in inner_copies(index - 1):
                copy.wait()
        cot_copy(index).wait()

        @pl.loop(0, units // tile)
        def _(j):
            columns = pl.ds(pl.multiple_of(j * tile, tile), tile)
            block = normed[index]
            gate = dot_nn(block, weights[0, :width, columns])
            up = dot_nn(block, weights[1, :width, columns])
            grad = dot_nt(cot[index % 2], weights[2, columns, :])
            sigmoid = jax.nn.sigmoid(gate)
            swish = gate * sigmoid
            inner[0, :, columns] = (swish * up).astype(bf16)
            inner[1, :, columns] = (grad * up * (sigmoid + swish * (1.0 - sigmoid))).astype(bf16)
            inner[2, :, columns] = (grad * swish).astype(bf16)

        for copy in inner_copies(index):
            copy.start()
        if index > 0:
            for copy in out_copies(index - 1):
                copy.wait()
        if index == 2:
            own_sum.wait()
        if index >= 3:
            for at in range(2):
                sum_copy(index - 2, at).wait_send()

        @pl.loop(0, width // 512)
        def _(j):
            columns = pl.ds(pl.multiple_of(j * 512, 512), 512)
            sent[index % 2, :, columns] = (
                dot_nt(inner[1], weights[0, columns, :units])
                + dot_nt(inner[2], weights[1, columns, :units])
            ).astype(bf16)

        if index == 0:
            own_sum.start()
        elif index == chips - 1:
            late_sum.start()
        else:
            for at in range(2):
                sum_copy(index, at).start()

        @pl.loop(0, width // 512)
        def _(j):
            columns = pl.ds(pl.multiple_of(j * 512, 512), 512)
            out_stage[:, columns] = dot_nn(inner[0], weights[2, :units, columns]).astype(bf16)

        for copy in out_copies(index):
            copy.start()

    for copy in inner_copies(chips - 1):
        copy.wait()
    for copy in out_copies(chips - 1):
        copy.wait()
    late_sum.wait()
    keep_normed.wait()
    own_cot.wait()
    for at in range(2):
        sum_copy(chips - 2, at).wait_send()
    for index in range(1, chips - 1):
        for at in range(2):
            sum_copy(index, at).wait_recv()
    for d in range(1, chips):
        for part in range(2):
            for which in range(2):
                block_copy(which, d, part).wait_send()


def feed_forward(normed, cot, share, down_own, down_other):
    chips = share.shape[2]
    rows, width = normed.shape
    units = down_own.shape[0] * 2
    tokens = chips * rows
    hbm = pl.BlockSpec(memory_space=pl.ANY)
    dma = pltpu.SemaphoreType.DMA

    def low(*shape):
        return jax.ShapeDtypeStruct(shape, bf16)

    out_shape = (
        low(chips, rows, width), low(chips, rows, width), low(chips - 1, rows, width),
        low(rows, width), low(chips, rows, width),
        low(tokens, units), low(tokens, units), low(tokens, units),
    )
    return pl.pallas_call(
        feed_kernel,
        in_specs=[hbm] * 5,
        out_specs=(hbm,) * len(out_shape),
        out_shape=out_shape,
        scratch_shapes=[
            pltpu.VMEM((3, width, width), bf16),
            pltpu.VMEM((chips, rows, width), bf16),
            pltpu.VMEM((2, rows, width), bf16),
            pltpu.VMEM((3, rows, units), bf16),
            pltpu.VMEM((2, rows, width), bf16),
            pltpu.VMEM((rows, width), bf16),
            dma((4,)), dma((chips, 2)), dma((chips, 2)), dma((chips, 2)), dma((chips, 2)),
            dma((2,)), dma((3,)), dma((chips, 2)), dma((chips, 2)), dma((3,)), dma(()), dma((2,)),
            dma(()),
        ],
        compiler_params=pltpu.CompilerParams(
            collective_id=0, has_side_effects=True, vmem_limit_bytes=60 * 2**20
        ),
        cost_estimate=pl.CostEstimate(
            flops=12 * tokens * units * width, bytes_accessed=2**27, transcendentals=tokens * units
        ),
    )(normed, cot, share, down_own, down_other)


def tail_kernel(
    heads,
    normed_all, cot_all, mixed_ref, gate_ref, up_ref, partial_ref, late_ref, outs_ref,
    hidden_ref, cot_ref, output_ref, weight_ref, qkv_ref, normed_ref, attn_ref,
    scale_ref, gain_ref, norm_ref, seg_col_ref, seg_row_ref, cos_ref, sin_ref,
    down_sum, inner_sum, down_got, inner_got, late_land, hidden_out,
    inner_land, grad_land, turn_land, end_land, mid_land, sum_out, sum_qkv, pass_land, out_land, total,
    one_out, down_result, gate_result, up_result, rest_result,
    branch, grad_made, core_out, core_qkv, relay_out, relay_qkv, mine, theirs, half, whole,
    pair_send, pair_recv, late_send, late_recv,
    inner_send, inner_recv, grad_send, grad_recv, turn_send, turn_recv, core_send, core_recv,
    sum_send, sum_recv, part_send, part_recv, end_send, end_recv, mid_send, mid_recv, out_send,
    out_recv, relay_send, relay_recv, pass_send, pass_recv,
    big_sem, tile_sem, got_sem, self_sem, load_sem, seq_sem, tick_sem, whole_sem, total_sem,
    one_sem,
):
    shards, seqs, span, part = qkv_ref.shape
    rows, width = normed_ref.shape
    _, owned, units = inner_land.shape[1:]
    chips = shards // 2
    tokens = chips * rows
    wide = heads * HEAD_DIM
    chunks = end_land.shape[0]
    qkv_width = shards * part
    full = qkv_width + width
    across = total.shape[0]
    line = lax.axis_size("replica") == 4
    relay = chips == 4
    me, replica = lax.axis_index("shard"), lax.axis_index("replica")
    chip, core = me // 2, me % 2
    partner = [
        chip_at(chip, d // 2) * 2 + (core if d % 2 == 0 else 1 - core) for d in range(shards)
    ]
    is_inner = (replica == 1) | (replica == 2)
    inward = jnp.where(replica < 2, 1, 2)
    outward = jnp.where(replica < 2, 0, 3)

    def partner_at(d):
        if isinstance(d, int):
            return partner[d]
        result, bit = 0, 1
        while bit < shards:
            result = result + bit * (((me // bit) % 2 + (d // bit) % 2) % 2)
            bit *= 2
        return result

    def remote(source, target, send, recv, shard, to=None):
        return pltpu.make_async_remote_copy(
            src_ref=source, dst_ref=target, send_sem=send, recv_sem=recv,
            device_id=(replica if to is None else to, shard),
            device_id_type=pl.DeviceIdType.MESH,
        )

    barrier = pltpu.get_barrier_semaphore()

    def greet(to, shard):
        pl.semaphore_signal(
            barrier, inc=1, device_id=(to, shard), device_id_type=pl.DeviceIdType.MESH
        )

    for d in range(1, shards):
        greet(replica, partner[d])
    if line:

        @pl.when(is_inner)
        def _():
            greet(outward, me)
            greet(3 - replica, me)
            pl.semaphore_wait(barrier, shards + 1)

        @pl.when(jnp.logical_not(is_inner))
        def _():
            greet(inward, me)
            pl.semaphore_wait(barrier, shards)

    else:
        pl.semaphore_wait(barrier, shards - 1)

    half_rows = rows // 2

    def late_copy(index):
        at = pl.ds(index * half_rows, half_rows)
        return remote(
            late_ref.at[at], late_land.at[at], late_send.at[index], late_recv.at[index],
            partner[2 * (chips - 1)],
        )

    late_copy(0).start()
    late_copy(1).start()

    down_across = width // units
    down_chunks = down_sum.shape[0] // owned * down_across
    last_inner = down_chunks + 2 * shards
    up_first = down_chunks + shards
    out_chunks = width // units

    def block(ref, row, column):
        return ref.at[
            pl.ds(pl.multiple_of(row * owned, owned), owned),
            pl.ds(pl.multiple_of(column * units, units), units),
        ]

    def inner_of(c):
        return (c - down_chunks) // shards, (c - down_chunks) % shards

    def source_of(c):
        if isinstance(c, int):
            if c < down_chunks:
                return block(down_sum, c // down_across, c % down_across)
            if c >= last_inner:
                return total.at[c - last_inner]
        which, d = inner_of(c)
        return inner_land.at[which, partner_at(d)]

    def place_of(c):
        if isinstance(c, int):
            if c < down_chunks:
                return block(down_result, c // down_across, c % down_across)
            if c >= last_inner + out_chunks:
                return block(rest_result, 0, c - last_inner - out_chunks)
            if c >= last_inner:
                return block(rest_result, 0, qkv_width // units + c - last_inner)
            which, d = inner_of(c)
            return block((gate_result, up_result)[which], 0, partner[d])
        return block(gate_result, 0, partner_at(inner_of(c)[1]))

    def end_copy(c):
        return remote(source_of(c), end_land.at[c], end_send.at[c], end_recv.at[c], me, inward)

    def mid_copy(c):
        return remote(
            half.at[c % 4], mid_land.at[c], mid_send.at[c], mid_recv.at[c], me, 3 - replica
        )

    def out_copy(c):
        return remote(whole.at[c % 2], place_of(c), out_send.at[c], out_recv.at[c], me, outward)

    def keep_copy(c):
        return pltpu.make_async_copy(whole.at[c % 2], place_of(c), whole_sem.at[c % 2])

    def from_end(c):
        if line:

            @pl.when(jnp.logical_not(is_inner))
            def _():
                end_copy(c).start()

    def take_mine(c):
        return pltpu.make_async_copy(source_of(c), mine, tick_sem.at[0])

    def take_other(c):
        return pltpu.make_async_copy(mid_land.at[c], theirs.at[1], tick_sem.at[2])

    def send_out(c):
        mid_copy(c).wait_recv()
        take_other(c).start()
        if not isinstance(c, int) or c >= 2:
            out_copy(c - 2).wait_send()
            keep_copy(c - 2).wait()
        take_other(c).wait()
        whole[c % 2] = (half[c % 4].astype(f32) + theirs[1].astype(f32)).astype(bf16)
        if isinstance(c, int):
            out_copy(c).start()
            keep_copy(c).start()
            return

        @pl.when(c >= down_chunks)
        def _():
            out_copy(c).start()
            keep_copy(c).start()

        for old in (down_chunks - 2, down_chunks - 1):

            @pl.when(c == old)
            def _():
                out_copy(old).start()
                keep_copy(old).start()

    def middle(c):
        if not line:
            return
        static = isinstance(c, int)

        @pl.when(is_inner)
        def _():
            if static and (c == 0 or c == up_first or c >= last_inner):
                take_mine(c).start()
            end_copy(c).wait_recv()
            two = pltpu.make_async_copy(end_land.at[c], theirs.at[0], tick_sem.at[1])
            two.start()
            if not static or c >= 4:
                mid_copy(c - 4).wait_send()
            take_mine(c).wait()
            two.wait()
            half[c % 4] = (mine[...].astype(f32) + theirs[0].astype(f32)).astype(bf16)
            mid_copy(c).start()
            if not static:

                @pl.when(c + 1 < up_first)
                def _():
                    take_mine(c + 1).start()

            elif c + 1 < last_inner and c + 1 != up_first:
                take_mine(c + 1).start()
            if not static or c >= 2:
                send_out(c - 2)

    lead = 3
    position = [0]

    settled = [down_chunks]

    def ticks(count):
        for _ in range(count):
            c = position[0]
            if c >= last_inner:
                return
            position[0] += 1
            ahead = c + lead
            if c >= up_first:
                ahead = min(ahead, up_first + 2 * (c - up_first) + 1)
            while settled[0] <= min(ahead, last_inner - 1):
                settle(settled[0])
                from_end(settled[0])
                settled[0] += 1
            middle(c)

    def later_tick(c):
        @pl.when(c + lead < up_first)
        def _():
            settle(c + lead)
            from_end(c + lead)

        middle(c)

    def inner_copy(which, d):
        at = partner_at(d)
        return remote(
            inner_sum.at[which, pl.ds(pl.multiple_of(at * owned, owned), owned)],
            inner_land.at[which, me],
            inner_send.at[which, d], inner_recv.at[which, d], at,
        )

    def own_inner(which):
        return pltpu.make_async_copy(
            inner_sum.at[which, pl.ds(pl.multiple_of(me * owned, owned), owned)],
            inner_land.at[which, me], self_sem.at[which],
        )

    def start_inner(which):
        own_inner(which).start()
        for d in range(1, shards):
            inner_copy(which, d).start()

    def settle(c):
        which, d = inner_of(c)
        if isinstance(c, int):
            if d == 0:
                own_inner(which).wait()
            else:
                inner_copy(which, d).wait_recv()
            return

        @pl.when(d == 0)
        def _():
            own_inner(which).wait()

        @pl.when(d > 0)
        def _():
            inner_copy(which, d).wait_recv()

    half_units = units
    tiles = width // rows
    per_slot = width // half_units

    def weight_gradients(big, sent_stage, kept_stage):
        got = branch
        def load(ref, slot, columns):
            return pltpu.make_async_copy(
                ref, big.at[slot, pl.ds(0, tokens), pl.ds(0, columns)], big_sem.at[slot]
            )

        def load_blocks(ref, slot):
            return [
                pltpu.make_async_copy(
                    ref.at[k], big.at[slot, pl.ds(k * rows, rows)], big_sem.at[3 + slot * chips + k]
                )
                for k in range(chips)
            ]

        first_loads = load_blocks(cot_all, 1) + [load(mixed_ref, 0, 2 * half_units)]
        normed_loads = load_blocks(normed_all, 2)
        for copy in first_loads + normed_loads:
            copy.start()
        for copy in first_loads:
            copy.wait()

        sums = (down_sum, inner_sum.at[0], inner_sum.at[1])
        gots = (down_got, inner_got.at[0], inner_got.at[1])

        def tile_copies(which, owner, stage):
            result = []
            for t in range(half_units // rows if which == 0 else tiles):
                if which == 0:
                    source = stage.at[t]
                else:
                    source = stage.at[
                        t // per_slot, :, pl.ds((t % per_slot) * half_units, half_units)
                    ]
                place = pl.ds(t * rows, rows)
                if owner == 0:
                    copy = remote(
                        source, gots[which].at[place], pair_send.at[which, t],
                        pair_recv.at[which, t], partner[1],
                    )
                else:
                    copy = pltpu.make_async_copy(
                        source, sums[which].at[place], tile_sem.at[which, t]
                    )
                result.append(copy)
            return result

        pair, made = {}, [0]
        for which in range(3):
            if which == 1:
                later = load(gate_ref, 0, 2 * half_units)
                later.start()
                following = load(up_ref, 1, 2 * half_units)
                following.start()
                for copy in normed_loads:
                    copy.wait()
                later.wait()
            if which == 2:
                following.wait()
            for owner in range(2):
                stage = (sent_stage, kept_stage)[owner]
                first = ((1 - core) if owner == 0 else core) * half_units
                copies = tile_copies(which, owner, stage)
                pair[which, owner] = copies
                if which > 0 and owner == 0:
                    for copy in pair[which - 1, 0]:
                        copy.wait_send()
                for t, copy in enumerate(copies):
                    columns = width if which == 0 else half_units
                    if owner == 1:
                        pair[which, 0][t].wait_recv()
                        take = pltpu.make_async_copy(
                            gots[which].at[pl.ds(t * rows, rows)], got.at[:, pl.ds(0, columns)],
                            got_sem,
                        )
                        take.start()
                    if which == 0:
                        at = pl.ds(pl.multiple_of(first + t * rows, rows), rows)
                        left, right, slot, begin = big[0, :tokens, at], 1, t, 0
                    else:
                        left = big[2, :tokens, t * rows : (t + 1) * rows]
                        right = which - 1
                        slot, begin = t // per_slot, (t % per_slot) * half_units
                    step = min(1024, columns)
                    for j in range(columns // step):
                        if which == 0:
                            at = pl.ds(j * step, step)
                        else:
                            at = pl.ds(pl.multiple_of(first, half_units), half_units)
                        product = outer_sum(left, big[right, :tokens, at])
                        if owner == 1:
                            if j == 0:
                                take.wait()
                            product = product + got[:, j * step : (j + 1) * step].astype(f32)
                        stage[slot, :, begin + j * step : begin + (j + 1) * step] = product.astype(
                            bf16
                        )
                    copy.start()
                    if which == 0 and owner == 1:
                        copy.wait()
                        per_tile = rows // owned * down_across
                        for c in range(t * per_tile, (t + 1) * per_tile):
                            from_end(c)
                    if which > 0:
                        made[0] += 1
                        if made[0] % 3 == 0 and position[0] < down_chunks - lead:
                            ticks(1)
                if owner == 1 and which > 0:
                    for copy in copies:
                        copy.wait()
                    if which == 1:
                        start_inner(0)
        for copy in pair[2, 0]:
            copy.wait_send()

    pl.run_scoped(
        weight_gradients,
        pltpu.VMEM((3, tokens, width), bf16),
        pltpu.VMEM((2, rows, width), bf16),
        pltpu.VMEM((2, rows, width), bf16),
    )

    def grad_copy(d, s):
        at = pl.ds(pl.multiple_of(s * span, span), span)
        return remote(
            grad_made.at[partner[d], at], grad_land.at[me, at],
            grad_send.at[d, s], grad_recv.at[d, s], partner[d],
        )

    own_grad = pltpu.make_async_copy(grad_made.at[me], grad_land.at[me], self_sem.at[2])

    def norm_backward(partials, hidden, cot, output):
        loads = [
            pltpu.make_async_copy(partial_ref, partials.at[pl.ds(0, chips - 1)], load_sem.at[0]),
            pltpu.make_async_copy(hidden_ref, hidden, load_sem.at[1]),
            pltpu.make_async_copy(cot_ref, cot, load_sem.at[2]),
            pltpu.make_async_copy(output_ref, output, load_sem.at[3]),
        ]
        for copy in loads:
            copy.start()
        late_copy(0).wait_recv()
        late_copy(1).wait_recv()
        last = pltpu.make_async_copy(late_land, partials.at[chips - 1], load_sem.at[4])
        last.start()
        ticks(1)
        for copy in loads[:3] + [last]:
            copy.wait()

        @pl.loop(0, rows // 32)
        def _(i):
            at = pl.ds(pl.multiple_of(i * 32, 32), 32)
            grad = partials[0, at].astype(f32)
            for d in range(1, chips):
                grad = grad + partials[d, at].astype(f32)
            scale = scale_ref[at]
            unit = hidden[at] * scale
            scaled = grad * gain_ref[...]
            level = jnp.mean(scaled * unit, -1, keepdims=True)
            result = cot[at].astype(f32) + scale * (scaled - unit * level)
            hidden[at] = result
            branch[at] = result.astype(bf16)

        keep = pltpu.make_async_copy(hidden, hidden_out, load_sem.at[1])
        keep.start()
        ticks(1)
        loads[3].wait()

        @pl.loop(0, shards)
        def _(k):
            grad_made[k] = dot_nt(branch[...], output[k]).astype(bf16)

        own_grad.start()
        for s in range(seqs):
            for d in range(1, shards):
                grad_copy(d, s).start()
        keep.wait()

    pl.run_scoped(
        norm_backward,
        pltpu.VMEM((chips, rows, width), bf16),
        pltpu.VMEM((rows, width), f32),
        pltpu.VMEM((rows, width), bf16),
        pltpu.VMEM((shards, owned, width), bf16),
    )

    def turn_copy(turned, d, s):
        at = pl.ds(pl.multiple_of(s * span, span), span)
        return remote(
            turned.at[s, partner[d]], turn_land.at[me, at],
            turn_send.at[d, s], turn_recv.at[d, s], partner[d],
        )

    def attention(qkv, grads, turned, sums, turned_all, normed, attn, sent, weight, one):
        loads = [
            pltpu.make_async_copy(normed_ref, normed, load_sem.at[0]),
            pltpu.make_async_copy(attn_ref, attn, load_sem.at[1]),
        ]
        for copy in loads:
            copy.start()
        own_grad.wait()
        half_owned = owned // 2

        def part_of(index):
            return pl.ds(index * half_owned, half_owned)

        def scatter_steps(which, product, core_land, relay_land, sum_land):
            wide_of = core_land.shape[2]

            def core_copy(d):
                return remote(
                    sent.at[d, :, pl.ds(0, wide_of)], core_land.at[d],
                    core_send.at[which, d], core_recv.at[which, d], partner[1],
                )

            def sum_copy(d, index):
                return remote(
                    core_land.at[d, part_of(index)], sum_land.at[d, part_of(index)],
                    sum_send.at[which, d, index], sum_recv.at[which, d, index], partner[2 * d],
                )

            def relay_copy(index):
                return remote(
                    core_land.at[3, part_of(index)], relay_land.at[index],
                    relay_send.at[which, index], relay_recv.at[which, index],
                    partner[2 * (index + 1)],
                )

            order = list(range(chips - 1, -1, -1))

            def near():
                for d in order:
                    for place, value in product(chip_at(chip, d) * 2 + 1 - core):
                        sent[d, :, place] = value.astype(bf16)
                    core_copy(d).start()

            def far():
                for d in order:
                    core_copy(d).wait_recv()
                    for place, value in product(chip_at(chip, d) * 2 + core):
                        core_land[d, :, place] = (
                            core_land[d, :, place].astype(f32) + value
                        ).astype(bf16)
                    if relay and d == 3:
                        relay_copy(0).start()
                        relay_copy(1).start()
                    elif d > 0:
                        for index in range(2):
                            if not relay or index != 2 - d:
                                sum_copy(d, index).start()
                for d in range(chips):
                    core_copy(d).wait_send()

            def onward():
                for index in range(2 if relay else 0):
                    relay_copy(index).wait_recv()
                    at = part_of(index)
                    core_land[2 - index, at] = (
                        core_land[2 - index, at].astype(f32) + relay_land[index].astype(f32)
                    ).astype(bf16)
                    sum_copy(2 - index, index).start()

            def arrive(first):
                direct = range(1, 3 if relay else chips)
                for d in direct:
                    for index in range(2):
                        sum_copy(d, index).wait_recv()
                gets = [
                    pltpu.make_async_copy(
                        sum_land.at[d], sent.at[d, :, pl.ds(0, wide_of)], load_sem.at[2 + d]
                    )
                    for d in direct
                ]
                for copy in gets:
                    copy.start()
                for copy in gets:
                    copy.wait()
                count = wide_of // units
                for k in range(count):
                    columns = slice(k * units, (k + 1) * units)
                    value = core_land[0, :, columns].astype(f32)
                    for d in direct:
                        value = value + sent[d, :, columns].astype(f32)
                    sent[0, :, columns] = value.astype(bf16)
                puts = [
                    pltpu.make_async_copy(
                        sent.at[0, :, pl.ds(k * units, units)], total.at[first + k],
                        total_sem.at[first + k],
                    )
                    for k in range(count)
                ]
                for put in puts:
                    put.start()
                for k, put in enumerate(puts):
                    put.wait()
                    from_end(last_inner + first + k)

            def leave():
                for index in range(2 if relay else 0):
                    relay_copy(index).wait_send()
                for d in range(1, 3 if relay else chips):
                    for index in range(2):
                        sum_copy(d, index).wait_send()

            return near, far, onward, arrive, leave

        def rows_for(owner):
            return pl.ds(pl.multiple_of(owner * owned, owned), owned)

        def out_product(owner):
            left = attn[:, rows_for(owner)]
            for k in range(out_chunks):
                at = slice(k * units, (k + 1) * units)
                yield at, outer_sum(left, branch[:, at])

        def qkv_product(owner):
            left = normed[:, rows_for(owner)]
            for k in range(shards):
                value = outer_sum(left, turned_all[k])
                key_at = shards * wide + k * HEAD_DIM
                value_at = key_at + shards * HEAD_DIM
                yield slice(k * wide, (k + 1) * wide), value[:, :wide]
                yield slice(key_at, key_at + HEAD_DIM), value[:, wide : wide + HEAD_DIM]
                yield slice(value_at, value_at + HEAD_DIM), value[:, wide + HEAD_DIM :]

        out_scatter = scatter_steps(0, out_product, core_out, relay_out, sum_out)
        qkv_scatter = scatter_steps(1, qkv_product, core_qkv, relay_qkv, sum_qkv)
        loads[1].wait()
        out_scatter[0]()
        ticks(1)
        out_scatter[1]()
        ticks(down_chunks - position[0])

        def own_turn(s):
            at = pl.ds(pl.multiple_of(s * span, span), span)
            return pltpu.make_async_copy(turned.at[s, me], turn_land.at[me, at], seq_sem.at[2 + s])

        @pl.loop(0, seqs)
        def _(s):
            for d in range(1, shards):
                grad_copy(d, s).wait_recv()
            at = pl.ds(pl.multiple_of(s * span, span), span)
            takes = [
                pltpu.make_async_copy(qkv_ref.at[:, s], qkv, seq_sem.at[0]),
                pltpu.make_async_copy(grad_land.at[:, at], grads, seq_sem.at[1]),
            ]
            for copy in takes:
                copy.start()
            for copy in takes:
                copy.wait()
            attention_back(
                heads, 256, qkv, grads, norm_ref.at[s], seg_col_ref[s], seg_row_ref[s],
                cos_ref.at[s], sin_ref.at[s], turned.at[s], sums,
                between=lambda: later_tick(down_chunks + 2 * s) if line else None,
            )
            own_turn(s).start()
            for d in range(1, shards):
                turn_copy(turned, d, s).start()
            if line:
                later_tick(down_chunks + 1 + 2 * s)

        if line:
            position[0] = down_chunks + 2 * seqs
            settled[0] = up_first
        start_inner(1)
        ticks(1)
        for s in range(seqs):
            own_turn(s).wait()
            for d in range(1, shards):
                turn_copy(turned, d, s).wait_recv()
        take = pltpu.make_async_copy(turn_land, turned_all, load_sem.at[2])
        take.start()
        weight_load(weight, 0).start()
        ticks(1)
        loads[0].wait()
        take.wait()

        qkv_scatter[0]()
        ticks(1)
        qkv_scatter[1]()
        ticks(1)
        out_scatter[2]()
        qkv_scatter[2]()

        def rows_of(index):
            return pl.ds(index * half_rows, half_rows)

        def part_copy(d, index):
            return remote(
                outs_ref.at[chip_at(chip, d), rows_of(index)], out_land.at[d, rows_of(index)],
                part_send.at[d, index], part_recv.at[d, index], partner[2 * d],
            )

        def pass_copy(index):
            return remote(
                outs_ref.at[chip_at(chip, 3), rows_of(index)], pass_land.at[index],
                pass_send.at[index], pass_recv.at[index], partner[2 * (index + 1)],
            )

        if relay:
            pass_copy(0).start()
            pass_copy(1).start()
            part_copy(1, 0).start()
            part_copy(2, 1).start()
        else:
            for d in range(1, chips):
                for index in range(2):
                    part_copy(d, index).start()

        def one_copy(k):
            at = pl.ds(k * owned, owned)
            return pltpu.make_async_copy(one.at[k % 2], one_out.at[:, at], one_sem.at[2 + k % 2])

        for k in range(shards):
            weight_load(weight, k).wait()
            if k + 1 < shards:
                weight_load(weight, k + 1).start()
            if k >= 2:
                one_copy(k - 2).wait()
            value = dot_nt(turned_all[0], weight[k % 2, :, :part])
            for j in range(1, shards):
                value = value + dot_nt(
                    turned_all[j], weight[k % 2, :, j * part : (j + 1) * part]
                )
            one[k % 2] = value
            one_copy(k).start()
            if k % 2 == 1:
                ticks(1)
            if k == 3:
                out_scatter[3](0)
        one_copy(shards - 2).wait()
        one_copy(shards - 1).wait()

        if relay:
            for index in range(2):
                pass_copy(index).wait_recv()
                at = rows_of(index)
                gets = [
                    pltpu.make_async_copy(
                        outs_ref.at[chip_at(chip, 2 - index), at], normed.at[rows_of(0)],
                        load_sem.at[0],
                    ),
                    pltpu.make_async_copy(
                        pass_land.at[index], normed.at[rows_of(1)], load_sem.at[1]
                    ),
                ]
                for copy in gets:
                    copy.start()
                for copy in gets:
                    copy.wait()
                attn[at] = (
                    normed[rows_of(0)].astype(f32) + normed[rows_of(1)].astype(f32)
                ).astype(bf16)
                remote(
                    attn.at[at], out_land.at[2 - index, at],
                    part_send.at[2 - index, index], part_recv.at[2 - index, index],
                    partner[2 * (2 - index)],
                ).start()
                ticks(1)
        ticks(last_inner - 4 - position[0])
        qkv_scatter[3](out_chunks)
        ticks(last_inner)
        for k in range(across):
            middle(last_inner + k)
        if line:

            @pl.when(is_inner)
            def _():
                send_out(chunks - 2)
                send_out(chunks - 1)

        for s in range(seqs):
            for d in range(1, shards):
                turn_copy(turned, d, s).wait_send()
        out_scatter[4]()
        qkv_scatter[4]()
        if relay:
            for index in range(2):
                pass_copy(index).wait_send()
        for d in range(1, 3 if relay else chips):
            for index in range(2):
                part_copy(d, index).wait_send()
                part_copy(d, index).wait_recv()

    def weight_load(weight, k):
        return pltpu.make_async_copy(weight_ref.at[k], weight.at[k % 2], one_sem.at[k % 2])

    pl.run_scoped(
        attention,
        pltpu.VMEM((shards, span, part), bf16),
        pltpu.VMEM((shards, span, wide), bf16),
        pltpu.VMEM((seqs, shards, span, part), bf16),
        pltpu.VMEM((2, shards * span, HEAD_DIM), f32),
        pltpu.VMEM((shards, rows, part), bf16),
        pltpu.VMEM((rows, width), bf16),
        pltpu.VMEM((rows, width), bf16),
        pltpu.VMEM((chips, owned, qkv_width), bf16),
        pltpu.VMEM((2, owned, qkv_width), bf16),
        pltpu.VMEM((2, rows, owned), f32),
    )

    late_copy(0).wait_send()
    late_copy(1).wait_send()
    for s in range(seqs):
        for d in range(1, shards):
            grad_copy(d, s).wait_send()
    for which in range(2):
        for d in range(1, shards):
            inner_copy(which, d).wait_send()
    if line:

        @pl.when(is_inner)
        def _():
            for c in range(chunks - 4, chunks):
                mid_copy(c).wait_send()
            for c in (chunks - 2, chunks - 1):
                out_copy(c).wait_send()
                keep_copy(c).wait()

        @pl.when(jnp.logical_not(is_inner))
        def _():
            for c in range(chunks):
                end_copy(c).wait_send()
                out_copy(c).wait_recv()


def tail(
    heads, normed_all, cot_all, mixed, gate, up, partials, late, outs,
    hidden, cot, output, weight, qkv, normed, attn, *tables,
):
    shards, seqs, span, part = qkv.shape
    rows, width = normed.shape
    chips = shards // 2
    units = mixed.shape[1] // 2
    owned = width // shards
    wide = heads * HEAD_DIM
    full = shards * part + width
    across = full // units
    chunks = (units // owned) * (width // units) + 2 * shards + across
    tiles = width // rows
    hbm = pl.BlockSpec(memory_space=pl.ANY)
    vmem = pl.BlockSpec(memory_space=pltpu.VMEM)
    dma = pltpu.SemaphoreType.DMA

    def low(*shape):
        return jax.ShapeDtypeStruct(shape, bf16)

    def high(*shape):
        return jax.ShapeDtypeStruct(shape, f32)

    pieces = low(chunks, owned, units)
    out_shape = (
        low(units, width), low(2, width, units), low(units, width), low(2, width, units),
        low(rows, width), high(rows, width),
        low(2, shards, owned, units), low(shards, rows, wide), low(shards, rows, part),
        pieces, pieces, low(chips, owned, width), low(chips, owned, shards * part),
        low(2, rows // 2, width), low(*outs.shape),
        low(across, owned, units), high(rows, width),
        low(units, width), low(owned, shards * units), low(owned, shards * units), low(owned, full),
    )
    length = shards * span
    return pl.pallas_call(
        functools.partial(tail_kernel, heads),
        in_specs=[hbm] * 15 + [vmem] * 7,
        out_specs=(hbm,) * len(out_shape),
        out_shape=out_shape,
        scratch_shapes=[
            pltpu.VMEM((rows, width), bf16),
            pltpu.VMEM((shards, rows, wide), bf16),
            pltpu.VMEM((chips, owned, width), bf16),
            pltpu.VMEM((chips, owned, shards * part), bf16),
            pltpu.VMEM((2, owned // 2, width), bf16),
            pltpu.VMEM((2, owned // 2, shards * part), bf16),
            pltpu.VMEM((owned, units), bf16),
            pltpu.VMEM((2, owned, units), bf16),
            pltpu.VMEM((4, owned, units), bf16),
            pltpu.VMEM((2, owned, units), bf16),
            dma((3, tiles)), dma((3, tiles)), dma((2,)), dma((2,)),
            dma((2, shards)), dma((2, shards)), dma((shards, seqs)), dma((shards, seqs)),
            dma((shards, seqs)), dma((shards, seqs)), dma((2, chips)), dma((2, chips)),
            dma((2, chips, 2)), dma((2, chips, 2)), dma((chips, 2)), dma((chips, 2)),
            dma((chunks,)), dma((chunks,)), dma((chunks,)), dma((chunks,)), dma((chunks,)),
            dma((chunks,)), dma((2, 2)), dma((2, 2)), dma((2,)), dma((2,)),
            dma((3 + 3 * chips,)), dma((3, tiles)), dma(()), dma((3,)), dma((5 + chips,)),
            dma((2 + seqs,)), dma((3,)), dma((2,)), dma((across,)), dma((4,)),
        ],
        compiler_params=pltpu.CompilerParams(
            collective_id=1, has_side_effects=True, vmem_limit_bytes=63 * 2**20
        ),
        cost_estimate=pl.CostEstimate(
            flops=10 * seqs * heads * length * length * HEAD_DIM + 6 * chips * rows * width * width,
            bytes_accessed=2**29,
            transcendentals=seqs * heads * length * length,
        ),
    )(
        normed_all, cot_all, mixed, gate, up, partials, late, outs,
        hidden, cot, output, weight, qkv, normed, attn, *tables,
    )


def norm_back(grad_normed, unit_rows, scale_rows, gain_rows):
    scaled_grad = grad_normed * gain_rows
    return scale_rows * (
        scaled_grad - unit_rows * jnp.mean(scaled_grad * unit_rows, -1, keepdims=True)
    )


def body(
    tokens,
    segments,
    positions,
    cotangent,
    attention_gain,
    query_weight,
    key_weight,
    value_weight,
    output_weight,
    mlp_gain,
    gate_weight,
    up_weight,
    down_weight,
):
    seqs, span, width = tokens.shape
    shards = lax.axis_size("shard")
    me = lax.axis_index("shard")
    rows = seqs * span
    length = shards * span
    owned = query_weight.shape[0]
    heads = HEADS // shards
    copies = max(1, shards // KV_HEADS)
    wide = heads * HEAD_DIM
    part = wide + 2 * HEAD_DIM
    hidden_share = down_weight.shape[0]

    chips = shards // 2
    replicas = lax.axis_size("replica")
    swap = [(i, i + 1 - 2 * (i % 2)) for i in range(shards)]

    small = jnp.concatenate(
        [
            attention_gain.astype(f32), mlp_gain.astype(f32),
            segments.astype(f32).reshape(rows), positions.astype(f32).reshape(rows),
        ]
    )
    small = lax.all_gather(small, "shard")
    gain_one, gain_two = small[:, :owned].reshape(width), small[:, owned : 2 * owned].reshape(width)
    places = jnp.swapaxes(small[:, 2 * owned :].reshape(shards, 2, seqs, span), 0, 1)
    places = jnp.swapaxes(places, 1, 2).reshape(2, seqs, length)
    seg_row, seg_col = places[0][:, None, :], places[0][:, :, None]
    angle_all = jnp.swapaxes(angles(places[1]), 1, 2)
    cos_all, sin_all = jnp.cos(angle_all), jnp.sin(angle_all)

    share = owned // replicas
    units = 2 * hidden_share
    share_own = lax.dynamic_slice_in_dim(
        jnp.stack([gate_weight, up_weight]), lax.axis_index("replica") * share, share, 1
    )
    share_own = jnp.transpose(share_own.reshape(2, share, chips, units), (2, 0, 1, 3))
    down_other = lax.ppermute(down_weight, "shard", swap)

    def per_head(weight):
        return jnp.repeat(weight.reshape(owned, KV_HEADS, HEAD_DIM), copies, axis=1)

    qkv_owned = jnp.concatenate(
        [query_weight.reshape(owned, shards, wide), per_head(key_weight), per_head(value_weight)],
        -1,
    ).reshape(owned, shards * part)

    x = tokens.reshape(rows, width).astype(f32)
    scale_one = lax.rsqrt(jnp.mean(x * x, -1, keepdims=True) + epsilon)
    unit_one = x * scale_one
    normed_one = (unit_one * gain_one).astype(bf16)
    angle = angles(positions).reshape(rows, HEAD_DIM // 2)
    cosine, sine = jnp.cos(angle), jnp.sin(angle)
    still = jnp.ones((rows, HEAD_DIM), f32)
    cos_lanes = jnp.concatenate([cosine] * (2 * heads + 2) + [still], 1)
    sin_lanes = jnp.concatenate([-sine, sine] * (heads + 1) + [still * 0.0], 1)
    shares, qkv_full, output_full, qkv, attn, norms = head(
        heads, seqs, share_own, qkv_owned, output_weight, normed_one, cos_lanes, sin_lanes,
        seg_col, seg_row,
    )
    hidden = x + dot_nn(attn, output_full.reshape(width, width))
    scale_two = lax.rsqrt(jnp.mean(hidden * hidden, -1, keepdims=True) + epsilon)
    normed_two = (hidden * scale_two * gain_two).astype(bf16)

    cot_rows = cotangent.reshape(rows, width)
    normed_all, cot_all, partials, late, outs, mixed, gate, up = feed_forward(
        normed_two, cot_rows, shares, down_weight, down_other
    )
    results = tail(
        heads, normed_all, cot_all, mixed, gate, up, partials, late, outs, hidden, cot_rows,
        output_full, qkv_full, qkv, normed_one, attn, scale_two, gain_two[None], norms, seg_col,
        seg_row, cos_all, sin_all,
    )
    down_part, grad_hidden, inner_blocks = results[0], results[5], results[6]
    out_land, total, grad_one, summed = results[14], results[15], results[16], results[17:]
    out_sum = lax.dynamic_index_in_dim(outs, me // 2, 0, keepdims=False).astype(f32)
    arrived = 3 if chips == 4 else chips
    out_sum = out_sum + jnp.sum(out_land[1:arrived].astype(f32), 0)
    block_out = (hidden + out_sum).astype(bf16)

    if replicas != 4:

        def side_by_side(some):
            return jnp.swapaxes(some, 0, 1).reshape(owned, some.shape[0] * hidden_share)

        out_blocks = width // hidden_share
        rest_blocks = jnp.concatenate([total[out_blocks:], total[:out_blocks]])
        summed = lax.psum(
            (
                down_part, side_by_side(inner_blocks[0]), side_by_side(inner_blocks[1]),
                side_by_side(rest_blocks),
            ),
            "replica",
        )
    down_grad, gate_grad, up_grad, rest = [some.astype(f32) for some in summed]
    key_at, value_at = shards * wide, shards * (wide + HEAD_DIM)
    output_grad = rest[:, shards * part :]

    def kv_grad(columns):
        return jnp.sum(columns.reshape(owned, KV_HEADS, copies, HEAD_DIM), 2).reshape(
            owned, KV_HEADS * HEAD_DIM
        )

    query_grad = rest[:, :key_at]
    key_grad = kv_grad(rest[:, key_at:value_at])
    value_grad = kv_grad(rest[:, value_at : shards * part])

    own_one, own_two = attention_gain.astype(f32), mlp_gain.astype(f32)
    gain_one_grad = (
        jnp.sum(query_weight.astype(f32) * query_grad, 1)
        + jnp.sum(key_weight.astype(f32) * key_grad + value_weight.astype(f32) * value_grad, 1)
    ) / own_one
    gain_two_grad = (
        jnp.sum(gate_weight.astype(f32) * gate_grad + up_weight.astype(f32) * up_grad, 1) / own_two
    )
    token_grad = grad_hidden + norm_back(grad_one, unit_one, scale_one, gain_one)
    return (
        block_out.reshape(seqs, span, width),
        token_grad.reshape(seqs, span, width),
        gain_one_grad,
        query_grad,
        key_grad,
        value_grad,
        output_grad,
        gain_two_grad,
        gate_grad,
        up_grad,
        down_grad,
    )


def solution(mesh):
    rows = P("shard", None)
    blocks = P("replica", "shard", None)
    in_specs = (
        blocks, P("replica", "shard"), P("replica", "shard"), blocks, P("shard"),
        rows, rows, rows, rows, P("shard"), rows, rows, rows,
    )
    out_specs = (
        blocks, blocks, P("shard"), rows, rows, rows, rows, P("shard"), rows, rows, rows,
    )
    return jax.shard_map(body, mesh=mesh, in_specs=in_specs, out_specs=out_specs, check_vma=False)
```

```python
import functools
import math

import jax
import jax.numpy as jnp
from jax import lax
from jax.experimental import pallas as pl
from jax.experimental.pallas import tpu as pltpu
from jax.sharding import PartitionSpec as P

HEADS = 32
KV_HEADS = 8
HEAD_DIM = 64

epsilon = 1e-05
rope_base = 500000.0
masked_score = -1e30
f32 = jnp.float32
bf16 = jnp.bfloat16


def angles(doc_positions):
    freq_index = jnp.arange(HEAD_DIM // 2, dtype=f32)
    inverse_freq = jnp.exp(freq_index * (-2.0 * math.log(rope_base) / HEAD_DIM))
    return doc_positions.astype(f32)[..., None] * inverse_freq


def outer_sum(left, right):
    return lax.dot_general(left, right, (((0,), (0,)), ((), ())), preferred_element_type=f32)


def dot_nt(left, right):
    return lax.dot_general(left, right, (((1,), (1,)), ((), ())), preferred_element_type=f32)


def dot_nn(left, right):
    return lax.dot_general(left, right, (((1,), (0,)), ((), ())), preferred_element_type=f32)


def score_bias(seg_col, seg_row, first, rows):
    last = first + rows
    key_at = lax.broadcasted_iota(jnp.int32, (last, rows), 0)
    query_at = lax.broadcasted_iota(jnp.int32, (last, rows), 1) + first
    allowed = (seg_col[:last] == seg_row[:, first:last]) & (key_at <= query_at)
    return jnp.where(allowed, 0.0, masked_score)


def attention_fore(heads, rows, qkv_ref, seg_col, seg_row, out_ref, norm_ref):
    shards, span, _ = qkv_ref.shape
    length = shards * span
    wide = heads * HEAD_DIM
    keys = qkv_ref[:, :, wide : wide + HEAD_DIM].reshape(length, HEAD_DIM)
    values = qkv_ref[:, :, wide + HEAD_DIM :].reshape(length, HEAD_DIM)
    values_t = values.astype(f32).T.astype(bf16)
    for first in range(0, length, rows):
        last = first + rows
        at = slice(first // span, last // span)
        bias = score_bias(seg_col, seg_row, first, rows)
        queries = qkv_ref[at, :, :wide].reshape(rows, wide) * HEAD_DIM ** (-0.5)
        parts = []
        for head in range(heads):
            one = queries[:, head * HEAD_DIM : (head + 1) * HEAD_DIM]
            scores = dot_nt(keys[:last], one) + bias
            top = jnp.max(scores, 0, keepdims=True)
            lifted = jnp.exp(scores - top)
            total = jnp.sum(lifted, 0, keepdims=True)
            probs = (lifted * (1.0 / total)).astype(bf16)
            parts.append(dot_nn(values_t[:, :last], probs))
            norm_ref[head : head + 1, first:last] = top + jnp.log(total)
        out = jnp.concatenate(parts, 0).T.astype(bf16)
        out_ref[at] = out.reshape(rows // span, span, wide)


def turn_back(part, cosine, sine):
    half = HEAD_DIM // 2
    lower, upper = part[:half], part[half:]
    return [lower * cosine + upper * sine, upper * cosine - lower * sine]


def attention_back(
    heads, rows, qkv_ref, grad_ref, norm, seg_col, seg_row, cos, sin, out_ref, sums, between
):
    shards, span, _ = qkv_ref.shape
    length = shards * span
    wide = heads * HEAD_DIM
    keys = qkv_ref[:, :, wide : wide + HEAD_DIM].reshape(length, HEAD_DIM)
    values = qkv_ref[:, :, wide + HEAD_DIM :].reshape(length, HEAD_DIM)
    keys_t = keys.astype(f32).T.astype(bf16)
    sums[...] = jnp.zeros_like(sums)
    key_sum, value_sum = sums.at[0], sums.at[1]
    for first in range(0, length, rows):
        last = first + rows
        at = slice(first // span, last // span)
        bias = score_bias(seg_col, seg_row, first, rows)
        queries = qkv_ref[at, :, :wide].reshape(rows, wide) * HEAD_DIM ** (-0.5)
        grads = grad_ref[at].reshape(rows, wide)
        cosine, sine = cos[:, first:last], sin[:, first:last]
        parts = []
        for head in range(heads):
            lanes = slice(head * HEAD_DIM, (head + 1) * HEAD_DIM)
            one, grad = queries[:, lanes], grads[:, lanes]
            scores = dot_nt(keys[:last], one) + bias
            probs = jnp.exp(scores - norm[head : head + 1, first:last])
            grad_probs = dot_nt(values[:last], grad)
            level = jnp.sum(probs * grad_probs, 0, keepdims=True)
            grad_scores = (probs * (grad_probs - level)).astype(bf16)
            value_sum[:last] += dot_nn(probs.astype(bf16), grad)
            key_sum[:last] += dot_nn(grad_scores, one)
            turned = dot_nn(keys_t[:, :last], grad_scores) * HEAD_DIM ** (-0.5)
            parts.extend(turn_back(turned, cosine, sine))
        out = jnp.concatenate(parts, 0).T.astype(bf16)
        out_ref[at, :, :wide] = out.reshape(rows // span, span, wide)
        if last * 4 == length * 3:
            between()
    key_parts = turn_back(key_sum[...].T, cos[...], sin[...])
    both = jnp.concatenate([jnp.concatenate(key_parts, 0).T, value_sum[...]], -1)
    out_ref[:, :, wide:] = both.astype(bf16).reshape(shards, span, 2 * HEAD_DIM)


def chip_at(chip, distance):
    result, bit = chip, 1
    while bit <= distance:
        if distance & bit:
            result = result + bit * (1 - 2 * ((chip // bit) % 2))
        bit *= 2
    return result


def head_kernel(
    heads,
    share_ref, weight_ref, output_ref, token_ref, gain_ref, place_ref, cos_ref, sin_ref,
    share_land, weight_out, output_land, qkv_land, attn_land, normed_out, hidden_out, second_out,
    norm_ref, scale_ref, gain_out, place_out, seg_col_ref, seg_row_ref,
    weights, tokens, normed, made, qkv, attended, hidden, gains, places,
    small_send, small_recv,
    share_send, share_recv, line_send, line_recv, swap_send, swap_recv,
    weight_send, weight_recv, near_send, near_recv, output_send, output_recv, close_send, close_recv,
    qkv_send, qkv_recv, attn_send, attn_recv, self_sem, load_sem,
):
    shards, owned, columns = weights.shape
    chips = shards // 2
    rows, width = token_ref.shape
    _, seqs, span, part = qkv_land.shape
    wide = heads * HEAD_DIM
    replicas = lax.axis_size("replica")
    me, replica = lax.axis_index("shard"), lax.axis_index("replica")
    chip, core = me // 2, me % 2
    partner = [
        chip_at(chip, d // 2) * 2 + (core if d % 2 == 0 else 1 - core) for d in range(shards)
    ]
    relay = chips == 4
    half_owned = owned // 2

    def remote(source, target, send, recv, shard, to=None):
        return pltpu.make_async_remote_copy(
            src_ref=source, dst_ref=target, send_sem=send, recv_sem=recv,
            device_id=(replica if to is None else to, shard),
            device_id_type=pl.DeviceIdType.MESH,
        )

    barrier = pltpu.get_barrier_semaphore()

    def greet(to, shard):
        pl.semaphore_signal(
            barrier, inc=1, device_id=(to, shard), device_id_type=pl.DeviceIdType.MESH
        )

    for d in range(1, shards):
        greet(replica, partner[d])
    has_left, has_right = replica > 0, replica < replicas - 1

    @pl.when(has_left)
    def _():
        greet(replica - 1, me)

    @pl.when(has_right)
    def _():
        greet(replica + 1, me)

    @pl.when(has_left & has_right)
    def _():
        pl.semaphore_wait(barrier, shards + 1)

    @pl.when(jnp.logical_not(has_left & has_right))
    def _():
        pl.semaphore_wait(barrier, shards)

    def small_copy(which, d):
        source, land = ((gain_ref, gains), (place_ref, places))[which]
        return remote(
            source, land.at[me], small_send.at[which, d], small_recv.at[which, d], partner[d]
        )

    for which in range(2):
        for d in range(1, shards):
            small_copy(which, d).start()
    take_tokens = pltpu.make_async_copy(token_ref, tokens, load_sem.at[0])
    take_tokens.start()
    gains[me] = gain_ref[...]
    places[me] = place_ref[...]

    def share_copy(d):
        return remote(
            share_ref.at[chip_at(chip, d)], share_land.at[core, replica, chip],
            share_send.at[d], share_recv.at[d], partner[2 * d],
        )

    own_share = pltpu.make_async_copy(
        share_ref.at[chip], share_land.at[core, replica, chip], self_sem.at[0]
    )
    own_share.start()
    for d in range(1, chips):
        share_copy(d).start()

    def rows_copies(ref, land, far_send, far_recv, side_send, side_recv):
        def half(index):
            return pl.ds(index * half_owned, half_owned)

        def far(d, index):
            if relay and d == 3:
                origin, way = (1, 2) if index == 0 else (2, 1)
                at = partner[2 * origin]
                return remote(
                    land.at[at, half(index)], land.at[at, half(index)],
                    far_send.at[d, index], far_recv.at[d, index], partner[2 * way],
                )
            return remote(
                ref.at[half(index)], land.at[me, half(index)],
                far_send.at[d, index], far_recv.at[d, index], partner[2 * d],
            )

        def near(d, index):
            at = partner[2 * d]
            source = ref.at[half(index)] if d == 0 else land.at[at, half(index)]
            return remote(
                source, land.at[at, half(index)],
                side_send.at[d, index], side_recv.at[d, index], partner[1],
            )

        return far, near

    def start_rows(far, near, halves=range(2)):
        for index in halves:
            for d in range(1, chips):
                if not (relay and d == 3):
                    far(d, index).start()
        for index in halves:
            near(0, index).start()

    def pass_rows(far, near, between=None):
        if relay:
            for index in range(2):
                for d in (1, 2):
                    far(d, index).wait_recv()
                far(3, index).start()
                for d in (1, 2):
                    near(d, index).start()
                if between is not None:
                    between(index)
            for index in range(2):
                far(3, index).wait_recv()
                near(3, index).start()
        else:
            for d in range(1, chips):
                for index in range(2):
                    far(d, index).wait_recv()
                    near(d, index).start()

    def end_rows(far, near):
        for d in range(chips):
            for index in range(2):
                near(d, index).wait_recv()

    def sent_rows(far, near):
        for d in range(chips):
            for index in range(2):
                near(d, index).wait_send()
                if d > 0:
                    far(d, index).wait_send()

    weight_rows = rows_copies(
        weight_ref, weights, weight_send, weight_recv, near_send, near_recv
    )
    output_rows = rows_copies(
        output_ref, output_land, output_send, output_recv, close_send, close_recv
    )
    own_weight = pltpu.make_async_copy(weight_ref, weights.at[me], self_sem.at[1])
    own_weight.start()
    own_output = pltpu.make_async_copy(output_ref, output_land.at[me], self_sem.at[2])
    own_output.start()

    def share_at(way, distance, index):
        far = replica - distance if way == 0 else replica + distance
        return share_land.at[core, far, pl.ds(index * (chips // 2), chips // 2)]

    def line_copy(way, step, index):
        at = share_at(way, step, index)
        return remote(
            at, at, line_send.at[way, step, index], line_recv.at[way, step, index], me,
            replica + 1 if way == 0 else replica - 1,
        )

    def came(way, step, index):
        at = share_at(way, step + 1, index)
        return remote(
            at, at, line_send.at[way, step, index], line_recv.at[way, step, index], me
        )

    def swap_copy(way, step, index):
        at = share_at(way, step, index)
        return remote(
            at, at, swap_send.at[way, step, index], swap_recv.at[way, step, index], partner[1]
        )

    def line_step(step, index):
        if step == 0 and index == 0:
            own_share.wait()
            for d in range(1, chips):
                share_copy(d).wait_recv()
        if step == 0:
            swap_copy(0, 0, index).start()
        for way in range(2):
            room = replica - step >= 0 if way == 0 else replica + step < replicas
            onward = has_right if way == 0 else has_left
            if step > 0:

                @pl.when(room)
                def _():
                    came(way, step - 1, index).wait_recv()
                    swap_copy(way, step, index).start()

            if step < replicas - 1:

                @pl.when(room & onward)
                def _():
                    line_copy(way, step, index).start()

    line_step(0, 0)
    line_step(0, 1)
    start_rows(*weight_rows)

    for which in range(2):
        for d in range(1, shards):
            small_copy(which, d).wait_recv()
    gain_out[...] = gains[...]
    place_out[...] = places[...]
    for s in range(seqs):
        seg_row_ref[s] = jnp.concatenate([places[k, 0, s : s + 1] for k in range(shards)], 1)
        turned = jnp.concatenate([places[k, 0, s : s + 1] for k in range(shards)], 0).T
        seg_col_ref[s] = jnp.concatenate([turned[:, k : k + 1] for k in range(shards)], 0)

    def gain_row(which):
        return jnp.concatenate([gains[k, which : which + 1] for k in range(shards)], 1)

    take_tokens.wait()
    gain_one = gain_row(0)

    @pl.loop(0, rows // 32)
    def _(i):
        at = pl.ds(pl.multiple_of(i * 32, 32), 32)
        x = tokens[at].astype(f32)
        unit = x * lax.rsqrt(jnp.mean(x * x, -1, keepdims=True) + epsilon)
        normed[at] = (unit * gain_one).astype(bf16)

    keep_normed = pltpu.make_async_copy(normed, normed_out, load_sem.at[0])
    keep_normed.start()
    if relay and replicas > 2:
        pass_rows(*weight_rows, between=lambda index: line_step(1, index))
    else:
        pass_rows(*weight_rows)
        if replicas > 2:
            line_step(1, 0)
            line_step(1, 1)
    own_weight.wait()
    keep_normed.wait()
    start_rows(*output_rows, halves=range(1))
    end_rows(*weight_rows)
    keep_weight = pltpu.make_async_copy(weights, weight_out, self_sem.at[1])
    keep_weight.start()

    lane = lax.broadcasted_iota(jnp.int32, (rows, part), 1)
    lower = lane % HEAD_DIM < HEAD_DIM // 2

    def project(owner):
        at = pl.ds(pl.multiple_of(owner * part, part), part)
        value = dot_nn(normed[...], weights[:, :, at].reshape(width, part))
        swapped = jnp.where(
            lower,
            pltpu.roll(value, part - HEAD_DIM // 2, 1),
            pltpu.roll(value, HEAD_DIM // 2, 1),
        )
        turned = value * cos_ref[...] + swapped * sin_ref[...]
        made[owner] = turned.astype(bf16)

    @pl.loop(0, shards)
    def _(k):
        project(k)

    def at_seq(s):
        return pl.ds(pl.multiple_of(s * span, span), span)

    def qkv_copy(d, s):
        return remote(
            made.at[partner[d], at_seq(s)], qkv_land.at[me, s],
            qkv_send.at[d, s], qkv_recv.at[d, s], partner[d],
        )

    def own_qkv(s):
        return pltpu.make_async_copy(made.at[me, at_seq(s)], qkv_land.at[me, s], load_sem.at[1 + s])

    for s in range(seqs):
        own_qkv(s).start()
        for d in range(shards - 1, 0, -1):
            qkv_copy(d, s).start()
    if replicas > 3:
        line_step(2, 0)

    def attn_copy(d, s):
        return remote(
            attended.at[s, partner[d]],
            attn_land.at[at_seq(s), pl.ds(pl.multiple_of(me * wide, wide), wide)],
            attn_send.at[d, s], attn_recv.at[d, s], partner[d],
        )

    def own_attn(s):
        return pltpu.make_async_copy(
            attended.at[s, me],
            attn_land.at[at_seq(s), pl.ds(pl.multiple_of(me * wide, wide), wide)],
            load_sem.at[1 + s],
        )

    @pl.loop(0, seqs)
    def _(s):
        own_qkv(s).wait()
        for d in range(1, shards):
            qkv_copy(d, s).wait_recv()
        take = pltpu.make_async_copy(qkv_land.at[:, s], qkv, load_sem.at[0])
        take.start()
        take.wait()
        attention_fore(
            heads, 256, qkv, seg_col_ref[s], seg_row_ref[s], attended.at[s], norm_ref.at[s]
        )
        own_attn(s).start()
        for d in range(1, shards):
            attn_copy(d, s).start()

        @pl.when(s == 0)
        def _():
            start_rows(*output_rows, halves=range(1, 2))
            if replicas > 3:
                line_step(2, 1)

    for step in range(2, replicas):
        for index in range(2):
            if (step, index) not in ((2, 0), (2, 1)) and step < replicas - 1:
                line_step(step, index)
    pass_rows(*output_rows)
    for s in range(seqs):
        own_attn(s).wait()
        for d in range(1, shards):
            attn_copy(d, s).wait_recv()
    end_rows(*output_rows)
    own_output.wait()
    keep_weight.wait()
    sent_rows(*weight_rows)
    take_output = pltpu.make_async_copy(
        output_land, weights.at[:, :, pl.ds(0, width)], self_sem.at[1]
    )
    take_attn = pltpu.make_async_copy(attn_land, normed, load_sem.at[0])
    take_output.start()
    take_attn.start()
    line_step(replicas - 1, 0)
    take_output.wait()
    take_attn.wait()

    @pl.loop(0, width // 512)
    def _(j):
        at = pl.ds(pl.multiple_of(j * 512, 512), 512)
        hidden[:, at] = tokens[:, at].astype(f32) + dot_nn(
            normed[...], weights[:, :, at].reshape(width, 512)
        )

    keep_hidden = pltpu.make_async_copy(hidden, hidden_out, self_sem.at[1])
    keep_hidden.start()
    gain_two = gain_row(1)

    @pl.loop(0, rows // 32)
    def _(i):
        at = pl.ds(pl.multiple_of(i * 32, 32), 32)
        x = hidden[at]
        scale = lax.rsqrt(jnp.mean(x * x, -1, keepdims=True) + epsilon)
        scale_ref[at] = scale
        normed[at] = (x * scale * gain_two).astype(bf16)

    keep_second = pltpu.make_async_copy(normed, second_out, load_sem.at[0])
    keep_second.start()
    line_step(replicas - 1, 1)
    keep_hidden.wait()
    keep_second.wait()

    for which in range(2):
        for d in range(1, shards):
            small_copy(which, d).wait_send()
    sent_rows(*output_rows)
    for d in range(1, chips):
        share_copy(d).wait_send()
    for s in range(seqs):
        for d in range(1, shards):
            qkv_copy(d, s).wait_send()
            attn_copy(d, s).wait_send()
    for index in range(2):
        swap_copy(0, 0, index).wait_send()
        swap_copy(0, 0, index).wait_recv()
        for way in range(2):
            for step in range(replicas):
                room = replica - step >= 0 if way == 0 else replica + step < replicas
                onward = has_right if way == 0 else has_left
                if step > 0:

                    @pl.when(room)
                    def _():
                        swap_copy(way, step, index).wait_send()
                        swap_copy(way, step, index).wait_recv()

                if step < replicas - 1:

                    @pl.when(room & onward)
                    def _():
                        line_copy(way, step, index).wait_send()


def head(heads, share, weight, output, tokens, gains, places, cosine, sine):
    chips = share.shape[0]
    shards = 2 * chips
    rows, width = tokens.shape
    _, seqs, span = places.shape
    owned, columns = weight.shape
    part = columns // shards
    wide = heads * HEAD_DIM
    length = shards * span
    replicas = lax.axis_size("replica")
    hbm = pl.BlockSpec(memory_space=pl.ANY)
    vmem = pl.BlockSpec(memory_space=pltpu.VMEM)
    dma = pltpu.SemaphoreType.DMA

    def low(*shape):
        return jax.ShapeDtypeStruct(shape, bf16)

    def high(*shape):
        return jax.ShapeDtypeStruct(shape, f32)

    out_shape = (
        low(2, replicas, *share.shape), low(shards, owned, columns), low(shards, owned, width),
        low(shards, seqs, span, part), low(rows, shards * wide),
        low(rows, width), high(rows, width), low(rows, width),
        high(seqs, heads, length), high(rows, 1), high(shards, *gains.shape),
        high(shards, *places.shape), high(seqs, length, 1), high(seqs, 1, length),
    )
    return pl.pallas_call(
        functools.partial(head_kernel, heads),
        in_specs=[hbm] * 4 + [vmem] * 4,
        out_specs=(hbm,) * 8 + (vmem,) * 6,
        out_shape=out_shape,
        scratch_shapes=[
            pltpu.VMEM((shards, owned, columns), bf16),
            pltpu.VMEM((rows, width), bf16),
            pltpu.VMEM((rows, width), bf16),
            pltpu.VMEM((shards, rows, part), bf16),
            pltpu.VMEM((shards, span, part), bf16),
            pltpu.VMEM((seqs, shards, span, wide), bf16),
            pltpu.VMEM((rows, width), f32),
            pltpu.VMEM((shards, *gains.shape), f32),
            pltpu.VMEM((shards, *places.shape), f32),
            dma((2, shards)), dma((2, shards)),
            dma((chips,)), dma((chips,)), dma((2, replicas, 2)), dma((2, replicas, 2)),
            dma((2, replicas, 2)), dma((2, replicas, 2)),
            dma((chips, 2)), dma((chips, 2)), dma((chips, 2)), dma((chips, 2)),
            dma((chips, 2)), dma((chips, 2)), dma((chips, 2)), dma((chips, 2)),
            dma((shards, seqs)), dma((shards, seqs)), dma((shards, seqs)), dma((shards, seqs)),
            dma((3,)), dma((1 + seqs,)),
        ],
        compiler_params=pltpu.CompilerParams(
            collective_id=2, has_side_effects=True, vmem_limit_bytes=56 * 2**20
        ),
        cost_estimate=pl.CostEstimate(
            flops=4 * seqs * heads * length * length * HEAD_DIM,
            bytes_accessed=2**28,
            transcendentals=seqs * heads * length * length,
        ),
    )(share, weight, output, tokens, gains, places, cosine, sine)


def pieces_of(chips):
    if chips == 4:
        return [[(0, 0), (0, 1)], [(1, 0), (2, 0)], [(1, 1), (2, 1)], [(3, 0), (3, 1)]]
    return [[(d, 0), (d, 1)] for d in range(chips)]


def feed_kernel(
    normed_ref, cot_own_ref, share_ref, down_own_ref, down_other_ref,
    normed_out, cot_ref, partial_ref, late_ref, out_ref, mixed_ref, gate_ref, up_ref,
    weights, normed, cot, inner, sent, out_stage, kept,
    weight_sem, normed_send, normed_recv, far_send, far_recv, cot_sem, inner_sem,
    sum_send, sum_recv, own_sem, late_sem, out_sem, keep_sem,
):
    chips, rows, width = normed.shape
    units = mixed_ref.shape[1]
    half_rows, half_units = rows // 2, units // 2
    _, replicas, _, _, share, _ = share_ref.shape
    me = lax.axis_index("shard")
    replica = lax.axis_index("replica")
    chip, core = me // 2, me % 2
    partner = [chip_at(chip, d) * 2 + core for d in range(chips)]
    steps = pieces_of(chips)
    spot = {piece: (i, at) for i, step in enumerate(steps) for at, piece in enumerate(step)}
    relay = chips == 4

    def remote(source, target, send, recv, shard):
        return pltpu.make_async_remote_copy(
            src_ref=source, dst_ref=target, send_sem=send, recv_sem=recv,
            device_id=(replica, shard), device_id_type=pl.DeviceIdType.MESH,
        )

    barrier = pltpu.get_barrier_semaphore()
    for shard in partner[1:]:
        pl.semaphore_signal(
            barrier, inc=1, device_id=(replica, shard), device_id_type=pl.DeviceIdType.MESH
        )
    pl.semaphore_wait(barrier, chips - 1)

    def half(index):
        return pl.ds(index * half_rows, half_rows)

    def block_copy(which, d, part):
        own, land = ((normed_ref, normed), (cot_own_ref, cot_ref))[which]
        send, recv = ((normed_send, normed_recv), (far_send, far_recv))[which]
        index, at = spot[d, part]
        if relay and d == 3:
            origin, way = (1, 2) if part == 0 else (2, 1)
            from_index, from_at = spot[origin, part]
            source, to = land.at[from_index, half(from_at)], partner[way]
        else:
            source, to = own.at[half(part)], partner[d]
        return remote(source, land.at[index, half(at)], send.at[d, part], recv.at[d, part], to)

    for part in range(2):
        for which in range(2):
            for d in range(1, 3 if relay else chips):
                block_copy(which, d, part).start()
    own_copy = pltpu.make_async_copy(normed_ref, normed.at[0], own_sem.at[0])
    own_copy.start()
    own_cot = pltpu.make_async_copy(cot_own_ref, cot_ref.at[0], own_sem.at[1])
    own_cot.start()

    def cot_copy(index):
        source = cot_own_ref if index == 0 else cot_ref.at[index]
        return pltpu.make_async_copy(source, cot.at[index % 2], cot_sem.at[index % 2])

    cot_copy(0).start()
    owned = share * replicas
    for which in range(2):
        for k in range(chips):
            for z in range(replicas):
                for c in range(2):
                    pltpu.make_async_copy(
                        share_ref.at[c, z, k, which],
                        weights.at[which, pl.ds((2 * k + c) * owned + z * share, share), pl.ds(0, units)],
                        weight_sem.at[which],
                    ).start()
    down_own = pltpu.make_async_copy(
        down_own_ref, weights.at[2, pl.ds(core * half_units, half_units)], weight_sem.at[2]
    )
    down_other = pltpu.make_async_copy(
        down_other_ref, weights.at[2, pl.ds((1 - core) * half_units, half_units)], weight_sem.at[3]
    )
    down_own.start()
    down_other.start()
    own_copy.wait()
    for which in range(2):
        whole = weights.at[which, pl.ds(0, width), pl.ds(0, units)]
        pltpu.make_async_copy(whole, whole, weight_sem.at[which]).wait()
    down_own.wait()
    down_other.wait()

    def inner_copies(index):
        return [
            pltpu.make_async_copy(
                inner.at[which], ref.at[pl.ds(index * rows, rows)], inner_sem.at[which]
            )
            for which, ref in enumerate((mixed_ref, gate_ref, up_ref))
        ]

    def out_copies(index):
        return [
            pltpu.make_async_copy(
                out_stage.at[half(at)], out_ref.at[chip_at(chip, d), half(part)], out_sem.at[at]
            )
            for at, (d, part) in enumerate(steps[index])
        ]

    def sum_copy(index, at):
        d, part = steps[index][at]
        return remote(
            sent.at[index % 2, half(at)], partial_ref.at[d, half(part)],
            sum_send.at[d, part], sum_recv.at[d, part], partner[d],
        )

    own_sum = pltpu.make_async_copy(sent.at[0], partial_ref.at[0], own_sem.at[2])
    late_sum = pltpu.make_async_copy(sent.at[(chips - 1) % 2], late_ref, late_sem)
    keep_normed = pltpu.make_async_copy(normed, normed_out, keep_sem)
    tile = min(512, units)
    for index in range(chips):
        split = index == chips - 1
        for d, part in steps[index]:
            if d > 0:
                block_copy(0, d, part).wait_recv()
                if not split:
                    block_copy(1, d, part).wait_recv()
        if relay and index in (1, 2):
            for which in range(2):
                block_copy(which, 3, index - 1).start()
        if index > 0 and not split:
            cot_copy(index).start()
        if index == chips - 1:
            keep_normed.start()
        if index > 0:
            for copy in inner_copies(index - 1):
                copy.wait()
        if not split:
            cot_copy(index).wait()

        def project_out():
            @pl.loop(0, width // 512)
            def _(j):
                columns = pl.ds(pl.multiple_of(j * 512, 512), 512)
                out_stage[:, columns] = dot_nn(inner[0], weights[2, :units, columns]).astype(bf16)

            for copy in out_copies(index):
                copy.start()

        if split:
            @pl.loop(0, units // tile)
            def _(j):
                columns = pl.ds(pl.multiple_of(j * tile, tile), tile)
                gate = dot_nn(normed[index], weights[0, :width, columns])
                up = dot_nn(normed[index], weights[1, :width, columns])
                kept[0, :, columns] = gate
                kept[1, :, columns] = up
                inner[0, :, columns] = (gate * jax.nn.sigmoid(gate) * up).astype(bf16)

            for copy in out_copies(index - 1):
                copy.wait()
            project_out()
            for d, part in steps[index]:
                block_copy(1, d, part).wait_recv()
            cot_copy(index).start()
            cot_copy(index).wait()

        @pl.loop(0, units // tile)
        def _(j):
            columns = pl.ds(pl.multiple_of(j * tile, tile), tile)
            if split:
                gate, up = kept[0, :, columns], kept[1, :, columns]
            else:
                gate = dot_nn(normed[index], weights[0, :width, columns])
                up = dot_nn(normed[index], weights[1, :width, columns])
            grad = dot_nt(cot[index % 2], weights[2, columns, :])
            sigmoid = jax.nn.sigmoid(gate)
            swish = gate * sigmoid
            if not split:
                inner[0, :, columns] = (swish * up).astype(bf16)
            inner[1, :, columns] = (grad * up * (sigmoid + swish * (1.0 - sigmoid))).astype(bf16)
            inner[2, :, columns] = (grad * swish).astype(bf16)

        for copy in inner_copies(index):
            copy.start()
        if index > 0 and not split:
            for copy in out_copies(index - 1):
                copy.wait()
        if index == 2:
            own_sum.wait()
        if index >= 3:
            for at in range(2):
                sum_copy(index - 2, at).wait_send()

        @pl.loop(0, width // 512)
        def _(j):
            columns = pl.ds(pl.multiple_of(j * 512, 512), 512)
            sent[index % 2, :, columns] = (
                dot_nt(inner[1], weights[0, columns, :units])
                + dot_nt(inner[2], weights[1, columns, :units])
            ).astype(bf16)

        if index == 0:
            own_sum.start()
        elif index == chips - 1:
            late_sum.start()
        else:
            for at in range(2):
                sum_copy(index, at).start()

        if not split:
            project_out()

    for copy in inner_copies(chips - 1):
        copy.wait()
    for copy in out_copies(chips - 1):
        copy.wait()
    late_sum.wait()
    keep_normed.wait()
    own_cot.wait()
    for at in range(2):
        sum_copy(chips - 2, at).wait_send()
    for index in range(1, chips - 1):
        for at in range(2):
            sum_copy(index, at).wait_recv()
    for d in range(1, chips):
        for part in range(2):
            for which in range(2):
                block_copy(which, d, part).wait_send()


def feed_forward(normed, cot, share, down_own, down_other):
    chips = share.shape[2]
    rows, width = normed.shape
    units = down_own.shape[0] * 2
    tokens = chips * rows
    hbm = pl.BlockSpec(memory_space=pl.ANY)
    dma = pltpu.SemaphoreType.DMA

    def low(*shape):
        return jax.ShapeDtypeStruct(shape, bf16)

    out_shape = (
        low(chips, rows, width), low(chips, rows, width), low(chips - 1, rows, width),
        low(rows, width), low(chips, rows, width),
        low(tokens, units), low(tokens, units), low(tokens, units),
    )
    return pl.pallas_call(
        feed_kernel,
        in_specs=[hbm] * 5,
        out_specs=(hbm,) * len(out_shape),
        out_shape=out_shape,
        scratch_shapes=[
            pltpu.VMEM((3, width, width), bf16),
            pltpu.VMEM((chips, rows, width), bf16),
            pltpu.VMEM((2, rows, width), bf16),
            pltpu.VMEM((3, rows, units), bf16),
            pltpu.VMEM((2, rows, width), bf16),
            pltpu.VMEM((rows, width), bf16),
            pltpu.VMEM((2, rows, units), f32),
            dma((4,)), dma((chips, 2)), dma((chips, 2)), dma((chips, 2)), dma((chips, 2)),
            dma((2,)), dma((3,)), dma((chips, 2)), dma((chips, 2)), dma((3,)), dma(()), dma((2,)),
            dma(()),
        ],
        compiler_params=pltpu.CompilerParams(
            collective_id=0, has_side_effects=True, vmem_limit_bytes=63 * 2**20
        ),
        cost_estimate=pl.CostEstimate(
            flops=12 * tokens * units * width, bytes_accessed=2**27, transcendentals=tokens * units
        ),
    )(normed, cot, share, down_own, down_other)


def tail_kernel(
    heads,
    normed_all, cot_all, mixed_ref, gate_ref, up_ref, partial_ref, late_ref, outs_ref,
    hidden_ref, cot_ref, output_ref, weight_ref, qkv_ref, normed_ref, attn_ref,
    scale_ref, gain_ref, norm_ref, seg_col_ref, seg_row_ref, cos_ref, sin_ref,
    down_sum, inner_sum, down_got, inner_got, late_land, hidden_out,
    inner_land, grad_land, turn_land, end_land, mid_land, sum_out, sum_qkv, pass_land, out_land, total,
    one_out, down_result, gate_result, up_result, rest_result,
    branch, grad_made, core_out, core_qkv, relay_out, relay_qkv, mine, theirs, half, whole,
    pair_send, pair_recv, late_send, late_recv,
    inner_send, inner_recv, grad_send, grad_recv, turn_send, turn_recv, core_send, core_recv,
    sum_send, sum_recv, part_send, part_recv, end_send, end_recv, mid_send, mid_recv, out_send,
    out_recv, relay_send, relay_recv, pass_send, pass_recv,
    big_sem, tile_sem, got_sem, self_sem, load_sem, seq_sem, tick_sem, whole_sem, total_sem,
    one_sem,
):
    shards, seqs, span, part = qkv_ref.shape
    rows, width = normed_ref.shape
    _, owned, units = inner_land.shape[1:]
    chips = shards // 2
    tokens = chips * rows
    wide = heads * HEAD_DIM
    chunks = end_land.shape[0]
    qkv_width = shards * part
    full = qkv_width + width
    across = total.shape[0]
    line = lax.axis_size("replica") == 4
    relay = chips == 4
    me, replica = lax.axis_index("shard"), lax.axis_index("replica")
    chip, core = me // 2, me % 2
    partner = [
        chip_at(chip, d // 2) * 2 + (core if d % 2 == 0 else 1 - core) for d in range(shards)
    ]
    is_inner = (replica == 1) | (replica == 2)
    inward = jnp.where(replica < 2, 1, 2)
    outward = jnp.where(replica < 2, 0, 3)

    def partner_at(d):
        if isinstance(d, int):
            return partner[d]
        result, bit = 0, 1
        while bit < shards:
            result = result + bit * (((me // bit) % 2 + (d // bit) % 2) % 2)
            bit *= 2
        return result

    def remote(source, target, send, recv, shard, to=None):
        return pltpu.make_async_remote_copy(
            src_ref=source, dst_ref=target, send_sem=send, recv_sem=recv,
            device_id=(replica if to is None else to, shard),
            device_id_type=pl.DeviceIdType.MESH,
        )

    barrier = pltpu.get_barrier_semaphore()

    def greet(to, shard):
        pl.semaphore_signal(
            barrier, inc=1, device_id=(to, shard), device_id_type=pl.DeviceIdType.MESH
        )

    for d in range(1, shards):
        greet(replica, partner[d])
    if line:

        @pl.when(is_inner)
        def _():
            greet(outward, me)
            greet(3 - replica, me)
            pl.semaphore_wait(barrier, shards + 1)

        @pl.when(jnp.logical_not(is_inner))
        def _():
            greet(inward, me)
            pl.semaphore_wait(barrier, shards)

    else:
        pl.semaphore_wait(barrier, shards - 1)

    half_rows = rows // 2

    def late_copy(index):
        at = pl.ds(index * half_rows, half_rows)
        return remote(
            late_ref.at[at], late_land.at[at], late_send.at[index], late_recv.at[index],
            partner[2 * (chips - 1)],
        )

    late_copy(0).start()
    late_copy(1).start()

    down_across = width // units
    down_chunks = down_sum.shape[0] // owned * down_across
    last_inner = down_chunks + 2 * shards
    up_first = down_chunks + shards
    out_chunks = width // units

    def block(ref, row, column):
        return ref.at[
            pl.ds(pl.multiple_of(row * owned, owned), owned),
            pl.ds(pl.multiple_of(column * units, units), units),
        ]

    def inner_of(c):
        return (c - down_chunks) // shards, (c - down_chunks) % shards

    def source_of(c):
        if isinstance(c, int):
            if c < down_chunks:
                return block(down_sum, c // down_across, c % down_across)
            if c >= last_inner:
                return total.at[c - last_inner]
        which, d = inner_of(c)
        return inner_land.at[which, partner_at(d)]

    def place_of(c):
        if isinstance(c, int):
            if c < down_chunks:
                return block(down_result, c // down_across, c % down_across)
            if c >= last_inner + out_chunks:
                return block(rest_result, 0, c - last_inner - out_chunks)
            if c >= last_inner:
                return block(rest_result, 0, qkv_width // units + c - last_inner)
            which, d = inner_of(c)
            return block((gate_result, up_result)[which], 0, partner[d])
        return block(gate_result, 0, partner_at(inner_of(c)[1]))

    def end_copy(c):
        return remote(source_of(c), end_land.at[c], end_send.at[c], end_recv.at[c], me, inward)

    def mid_copy(c):
        return remote(
            half.at[c % 4], mid_land.at[c], mid_send.at[c], mid_recv.at[c], me, 3 - replica
        )

    def out_copy(c):
        return remote(whole.at[c % 2], place_of(c), out_send.at[c], out_recv.at[c], me, outward)

    def keep_copy(c):
        return pltpu.make_async_copy(whole.at[c % 2], place_of(c), whole_sem.at[c % 2])

    def from_end(c):
        if line:

            @pl.when(jnp.logical_not(is_inner))
            def _():
                end_copy(c).start()

    def take_mine(c):
        return pltpu.make_async_copy(source_of(c), mine, tick_sem.at[0])

    def take_other(c):
        return pltpu.make_async_copy(mid_land.at[c], theirs.at[1], tick_sem.at[2])

    def send_out(c):
        mid_copy(c).wait_recv()
        take_other(c).start()
        if not isinstance(c, int) or c >= 2:
            out_copy(c - 2).wait_send()
            keep_copy(c - 2).wait()
        take_other(c).wait()
        whole[c % 2] = (half[c % 4].astype(f32) + theirs[1].astype(f32)).astype(bf16)
        if isinstance(c, int):
            out_copy(c).start()
            keep_copy(c).start()
            return

        @pl.when(c >= down_chunks)
        def _():
            out_copy(c).start()
            keep_copy(c).start()

        for old in (down_chunks - 2, down_chunks - 1):

            @pl.when(c == old)
            def _():
                out_copy(old).start()
                keep_copy(old).start()

    def middle(c):
        if not line:
            return
        static = isinstance(c, int)

        @pl.when(is_inner)
        def _():
            if static and (c == 0 or c == up_first or c >= last_inner):
                take_mine(c).start()
            end_copy(c).wait_recv()
            two = pltpu.make_async_copy(end_land.at[c], theirs.at[0], tick_sem.at[1])
            two.start()
            if not static or c >= 4:
                mid_copy(c - 4).wait_send()
            take_mine(c).wait()
            two.wait()
            half[c % 4] = (mine[...].astype(f32) + theirs[0].astype(f32)).astype(bf16)
            mid_copy(c).start()
            if not static:

                @pl.when(c + 1 < up_first)
                def _():
                    take_mine(c + 1).start()

            elif c + 1 < last_inner and c + 1 != up_first:
                take_mine(c + 1).start()
            if not static or c >= 2:
                send_out(c - 2)

    lead = 3
    position = [0]

    settled = [down_chunks]

    def ticks(count):
        for _ in range(count):
            c = position[0]
            if c >= last_inner:
                return
            position[0] += 1
            ahead = c + lead
            if c >= up_first:
                ahead = min(ahead, up_first + 2 * (c - up_first) + 1)
            while settled[0] <= min(ahead, last_inner - 1):
                settle(settled[0])
                from_end(settled[0])
                settled[0] += 1
            middle(c)

    def later_tick(c):
        @pl.when(c + lead < up_first)
        def _():
            settle(c + lead)
            from_end(c + lead)

        middle(c)

    def inner_copy(which, d):
        at = partner_at(d)
        return remote(
            inner_sum.at[which, pl.ds(pl.multiple_of(at * owned, owned), owned)],
            inner_land.at[which, me],
            inner_send.at[which, d], inner_recv.at[which, d], at,
        )

    def own_inner(which):
        return pltpu.make_async_copy(
            inner_sum.at[which, pl.ds(pl.multiple_of(me * owned, owned), owned)],
            inner_land.at[which, me], self_sem.at[which],
        )

    def start_inner(which):
        own_inner(which).start()
        for d in range(1, shards):
            inner_copy(which, d).start()

    def settle(c):
        which, d = inner_of(c)
        if isinstance(c, int):
            if d == 0:
                own_inner(which).wait()
            else:
                inner_copy(which, d).wait_recv()
            return

        @pl.when(d == 0)
        def _():
            own_inner(which).wait()

        @pl.when(d > 0)
        def _():
            inner_copy(which, d).wait_recv()

    half_units = units
    tiles = width // rows
    per_slot = width // half_units

    def weight_gradients(big, sent_stage, kept_stage):
        got = branch
        def load(ref, slot, columns):
            return pltpu.make_async_copy(
                ref, big.at[slot, pl.ds(0, tokens), pl.ds(0, columns)], big_sem.at[slot]
            )

        def load_blocks(ref, slot):
            return [
                pltpu.make_async_copy(
                    ref.at[k], big.at[slot, pl.ds(k * rows, rows)], big_sem.at[3 + slot * chips + k]
                )
                for k in range(chips)
            ]

        first_loads = load_blocks(cot_all, 1) + [load(mixed_ref, 0, 2 * half_units)]
        normed_loads = load_blocks(normed_all, 2)
        for copy in first_loads + normed_loads:
            copy.start()
        for copy in first_loads:
            copy.wait()

        sums = (down_sum, inner_sum.at[0], inner_sum.at[1])
        gots = (down_got, inner_got.at[0], inner_got.at[1])

        def tile_copies(which, owner, stage):
            result = []
            for t in range(half_units // rows if which == 0 else tiles):
                if which == 0:
                    source = stage.at[t]
                else:
                    source = stage.at[
                        t // per_slot, :, pl.ds((t % per_slot) * half_units, half_units)
                    ]
                place = pl.ds(t * rows, rows)
                if owner == 0:
                    copy = remote(
                        source, gots[which].at[place], pair_send.at[which, t],
                        pair_recv.at[which, t], partner[1],
                    )
                else:
                    copy = pltpu.make_async_copy(
                        source, sums[which].at[place], tile_sem.at[which, t]
                    )
                result.append(copy)
            return result

        pair, made = {}, [0]
        for which in range(3):
            if which == 1:
                later = load(gate_ref, 0, 2 * half_units)
                later.start()
                following = load(up_ref, 1, 2 * half_units)
                following.start()
                for copy in normed_loads:
                    copy.wait()
                later.wait()
            if which == 2:
                following.wait()
            for owner in range(2):
                stage = (sent_stage, kept_stage)[owner]
                first = ((1 - core) if owner == 0 else core) * half_units
                copies = tile_copies(which, owner, stage)
                pair[which, owner] = copies
                if which > 0 and owner == 0:
                    for copy in pair[which - 1, 0]:
                        copy.wait_send()
                for t, copy in enumerate(copies):
                    columns = width if which == 0 else half_units
                    if owner == 1:
                        pair[which, 0][t].wait_recv()
                        take = pltpu.make_async_copy(
                            gots[which].at[pl.ds(t * rows, rows)], got.at[:, pl.ds(0, columns)],
                            got_sem,
                        )
                        take.start()
                    if which == 0:
                        at = pl.ds(pl.multiple_of(first + t * rows, rows), rows)
                        left, right, slot, begin = big[0, :tokens, at], 1, t, 0
                    else:
                        left = big[2, :tokens, t * rows : (t + 1) * rows]
                        right = which - 1
                        slot, begin = t // per_slot, (t % per_slot) * half_units
                    step = min(1024, columns)
                    for j in range(columns // step):
                        if which == 0:
                            at = pl.ds(j * step, step)
                        else:
                            at = pl.ds(pl.multiple_of(first, half_units), half_units)
                        product = outer_sum(left, big[right, :tokens, at])
                        if owner == 1:
                            if j == 0:
                                take.wait()
                            product = product + got[:, j * step : (j + 1) * step].astype(f32)
                        stage[slot, :, begin + j * step : begin + (j + 1) * step] = product.astype(
                            bf16
                        )
                    copy.start()
                    if which == 0 and owner == 1:
                        copy.wait()
                        per_tile = rows // owned * down_across
                        for c in range(t * per_tile, (t + 1) * per_tile):
                            from_end(c)
                    if which > 0:
                        made[0] += 1
                        if made[0] % 3 == 0 and position[0] < down_chunks - lead:
                            ticks(1)
                if owner == 1 and which > 0:
                    for copy in copies:
                        copy.wait()
                    if which == 1:
                        start_inner(0)
        for copy in pair[2, 0]:
            copy.wait_send()

    pl.run_scoped(
        weight_gradients,
        pltpu.VMEM((3, tokens, width), bf16),
        pltpu.VMEM((2, rows, width), bf16),
        pltpu.VMEM((2, rows, width), bf16),
    )

    def grad_copy(d, s):
        at = pl.ds(pl.multiple_of(s * span, span), span)
        return remote(
            grad_made.at[partner[d], at], grad_land.at[me, at],
            grad_send.at[d, s], grad_recv.at[d, s], partner[d],
        )

    own_grad = pltpu.make_async_copy(grad_made.at[me], grad_land.at[me], self_sem.at[2])

    def norm_backward(partials, hidden, cot, output):
        loads = [
            pltpu.make_async_copy(partial_ref, partials.at[pl.ds(0, chips - 1)], load_sem.at[0]),
            pltpu.make_async_copy(hidden_ref, hidden, load_sem.at[1]),
            pltpu.make_async_copy(cot_ref, cot, load_sem.at[2]),
            pltpu.make_async_copy(output_ref, output, load_sem.at[3]),
        ]
        for copy in loads:
            copy.start()
        late_copy(0).wait_recv()
        late_copy(1).wait_recv()
        last = pltpu.make_async_copy(late_land, partials.at[chips - 1], load_sem.at[4])
        last.start()
        ticks(1)
        for copy in loads[:3] + [last]:
            copy.wait()

        @pl.loop(0, rows // 32)
        def _(i):
            at = pl.ds(pl.multiple_of(i * 32, 32), 32)
            grad = partials[0, at].astype(f32)
            for d in range(1, chips):
                grad = grad + partials[d, at].astype(f32)
            scale = scale_ref[at]
            unit = hidden[at] * scale
            scaled = grad * gain_ref[...]
            level = jnp.mean(scaled * unit, -1, keepdims=True)
            result = cot[at].astype(f32) + scale * (scaled - unit * level)
            hidden[at] = result
            branch[at] = result.astype(bf16)

        keep = pltpu.make_async_copy(hidden, hidden_out, load_sem.at[1])
        keep.start()
        ticks(1)
        loads[3].wait()

        @pl.loop(0, shards)
        def _(k):
            grad_made[k] = dot_nt(branch[...], output[k]).astype(bf16)

        own_grad.start()
        for s in range(seqs):
            for d in range(1, shards):
                grad_copy(d, s).start()
        keep.wait()

    pl.run_scoped(
        norm_backward,
        pltpu.VMEM((chips, rows, width), bf16),
        pltpu.VMEM((rows, width), f32),
        pltpu.VMEM((rows, width), bf16),
        pltpu.VMEM((shards, owned, width), bf16),
    )

    def turn_copy(turned, d, s):
        at = pl.ds(pl.multiple_of(s * span, span), span)
        return remote(
            turned.at[s, partner[d]], turn_land.at[me, at],
            turn_send.at[d, s], turn_recv.at[d, s], partner[d],
        )

    def attention(qkv, grads, turned, sums, turned_all, normed, attn, sent, weight, one):
        loads = [
            pltpu.make_async_copy(normed_ref, normed, load_sem.at[0]),
            pltpu.make_async_copy(attn_ref, attn, load_sem.at[1]),
        ]
        for copy in loads:
            copy.start()
        own_grad.wait()
        half_owned = owned // 2

        def part_of(index):
            return pl.ds(index * half_owned, half_owned)

        def scatter_steps(which, product, core_land, relay_land, sum_land):
            wide_of = core_land.shape[2]

            def core_copy(d):
                return remote(
                    sent.at[d, :, pl.ds(0, wide_of)], core_land.at[d],
                    core_send.at[which, d], core_recv.at[which, d], partner[1],
                )

            def sum_copy(d, index):
                return remote(
                    core_land.at[d, part_of(index)], sum_land.at[d, part_of(index)],
                    sum_send.at[which, d, index], sum_recv.at[which, d, index], partner[2 * d],
                )

            def relay_copy(index):
                return remote(
                    core_land.at[3, part_of(index)], relay_land.at[index],
                    relay_send.at[which, index], relay_recv.at[which, index],
                    partner[2 * (index + 1)],
                )

            order = list(range(chips - 1, -1, -1))

            def near():
                for d in order:
                    for place, value in product(chip_at(chip, d) * 2 + 1 - core):
                        sent[d, :, place] = value.astype(bf16)
                    core_copy(d).start()

            def far():
                for d in order:
                    core_copy(d).wait_recv()
                    for place, value in product(chip_at(chip, d) * 2 + core):
                        core_land[d, :, place] = (
                            core_land[d, :, place].astype(f32) + value
                        ).astype(bf16)
                    if relay and d == 3:
                        relay_copy(0).start()
                        relay_copy(1).start()
                    elif d > 0:
                        for index in range(2):
                            if not relay or index != 2 - d:
                                sum_copy(d, index).start()
                for d in range(chips):
                    core_copy(d).wait_send()

            def onward():
                for index in range(2 if relay else 0):
                    relay_copy(index).wait_recv()
                    at = part_of(index)
                    core_land[2 - index, at] = (
                        core_land[2 - index, at].astype(f32) + relay_land[index].astype(f32)
                    ).astype(bf16)
                    sum_copy(2 - index, index).start()

            def arrive(first):
                direct = range(1, 3 if relay else chips)
                for d in direct:
                    for index in range(2):
                        sum_copy(d, index).wait_recv()
                gets = [
                    pltpu.make_async_copy(
                        sum_land.at[d], sent.at[d, :, pl.ds(0, wide_of)], load_sem.at[2 + d]
                    )
                    for d in direct
                ]
                for copy in gets:
                    copy.start()
                for copy in gets:
                    copy.wait()
                count = wide_of // units
                for k in range(count):
                    columns = slice(k * units, (k + 1) * units)
                    value = core_land[0, :, columns].astype(f32)
                    for d in direct:
                        value = value + sent[d, :, columns].astype(f32)
                    sent[0, :, columns] = value.astype(bf16)
                puts = [
                    pltpu.make_async_copy(
                        sent.at[0, :, pl.ds(k * units, units)], total.at[first + k],
                        total_sem.at[first + k],
                    )
                    for k in range(count)
                ]
                for put in puts:
                    put.start()
                for k, put in enumerate(puts):
                    put.wait()
                    from_end(last_inner + first + k)

            def leave():
                for index in range(2 if relay else 0):
                    relay_copy(index).wait_send()
                for d in range(1, 3 if relay else chips):
                    for index in range(2):
                        sum_copy(d, index).wait_send()

            return near, far, onward, arrive, leave

        def rows_for(owner):
            return pl.ds(pl.multiple_of(owner * owned, owned), owned)

        def out_product(owner):
            left = attn[:, rows_for(owner)]
            for k in range(out_chunks):
                at = slice(k * units, (k + 1) * units)
                yield at, outer_sum(left, branch[:, at])

        def qkv_product(owner):
            left = normed[:, rows_for(owner)]
            for k in range(shards):
                value = outer_sum(left, turned_all[k])
                key_at = shards * wide + k * HEAD_DIM
                value_at = key_at + shards * HEAD_DIM
                yield slice(k * wide, (k + 1) * wide), value[:, :wide]
                yield slice(key_at, key_at + HEAD_DIM), value[:, wide : wide + HEAD_DIM]
                yield slice(value_at, value_at + HEAD_DIM), value[:, wide + HEAD_DIM :]

        out_scatter = scatter_steps(0, out_product, core_out, relay_out, sum_out)
        qkv_scatter = scatter_steps(1, qkv_product, core_qkv, relay_qkv, sum_qkv)
        loads[1].wait()
        out_scatter[0]()
        ticks(1)
        out_scatter[1]()
        ticks(down_chunks - position[0])

        def own_turn(s):
            at = pl.ds(pl.multiple_of(s * span, span), span)
            return pltpu.make_async_copy(turned.at[s, me], turn_land.at[me, at], seq_sem.at[2 + s])

        @pl.loop(0, seqs)
        def _(s):
            for d in range(1, shards):
                grad_copy(d, s).wait_recv()
            at = pl.ds(pl.multiple_of(s * span, span), span)
            takes = [
                pltpu.make_async_copy(qkv_ref.at[:, s], qkv, seq_sem.at[0]),
                pltpu.make_async_copy(grad_land.at[:, at], grads, seq_sem.at[1]),
            ]
            for copy in takes:
                copy.start()
            for copy in takes:
                copy.wait()
            attention_back(
                heads, 256, qkv, grads, norm_ref.at[s], seg_col_ref[s], seg_row_ref[s],
                cos_ref.at[s], sin_ref.at[s], turned.at[s], sums,
                between=lambda: later_tick(down_chunks + 2 * s) if line else None,
            )
            own_turn(s).start()
            for d in range(1, shards):
                turn_copy(turned, d, s).start()
            if line:
                later_tick(down_chunks + 1 + 2 * s)

        if line:
            position[0] = down_chunks + 2 * seqs
            settled[0] = up_first
        start_inner(1)
        ticks(1)
        for s in range(seqs):
            own_turn(s).wait()
            for d in range(1, shards):
                turn_copy(turned, d, s).wait_recv()
        take = pltpu.make_async_copy(turn_land, turned_all, load_sem.at[2])
        take.start()
        weight_load(weight, 0).start()
        ticks(1)
        loads[0].wait()
        take.wait()

        qkv_scatter[0]()
        ticks(1)
        qkv_scatter[1]()
        ticks(1)
        out_scatter[2]()
        qkv_scatter[2]()

        def rows_of(index):
            return pl.ds(index * half_rows, half_rows)

        def part_copy(d, index):
            return remote(
                outs_ref.at[chip_at(chip, d), rows_of(index)], out_land.at[d, rows_of(index)],
                part_send.at[d, index], part_recv.at[d, index], partner[2 * d],
            )

        def pass_copy(index):
            return remote(
                outs_ref.at[chip_at(chip, 3), rows_of(index)], pass_land.at[index],
                pass_send.at[index], pass_recv.at[index], partner[2 * (index + 1)],
            )

        if relay:
            pass_copy(0).start()
            pass_copy(1).start()
            part_copy(1, 0).start()
            part_copy(2, 1).start()
        else:
            for d in range(1, chips):
                for index in range(2):
                    part_copy(d, index).start()

        def one_copy(k):
            at = pl.ds(k * owned, owned)
            return pltpu.make_async_copy(one.at[k % 2], one_out.at[:, at], one_sem.at[2 + k % 2])

        for k in range(shards):
            weight_load(weight, k).wait()
            if k + 1 < shards:
                weight_load(weight, k + 1).start()
            if k >= 2:
                one_copy(k - 2).wait()
            value = dot_nt(turned_all[0], weight[k % 2, :, :part])
            for j in range(1, shards):
                value = value + dot_nt(
                    turned_all[j], weight[k % 2, :, j * part : (j + 1) * part]
                )
            one[k % 2] = value
            one_copy(k).start()
            if k % 2 == 1:
                ticks(1)
            if k == 3:
                out_scatter[3](0)
        one_copy(shards - 2).wait()
        one_copy(shards - 1).wait()

        if relay:
            for index in range(2):
                pass_copy(index).wait_recv()
                at = rows_of(index)
                gets = [
                    pltpu.make_async_copy(
                        outs_ref.at[chip_at(chip, 2 - index), at], normed.at[rows_of(0)],
                        load_sem.at[0],
                    ),
                    pltpu.make_async_copy(
                        pass_land.at[index], normed.at[rows_of(1)], load_sem.at[1]
                    ),
                ]
                for copy in gets:
                    copy.start()
                for copy in gets:
                    copy.wait()
                attn[at] = (
                    normed[rows_of(0)].astype(f32) + normed[rows_of(1)].astype(f32)
                ).astype(bf16)
                remote(
                    attn.at[at], out_land.at[2 - index, at],
                    part_send.at[2 - index, index], part_recv.at[2 - index, index],
                    partner[2 * (2 - index)],
                ).start()
                ticks(1)
        ticks(last_inner - 4 - position[0])
        qkv_scatter[3](out_chunks)
        ticks(last_inner)
        for k in range(across):
            middle(last_inner + k)
        if line:

            @pl.when(is_inner)
            def _():
                send_out(chunks - 2)
                send_out(chunks - 1)

        for s in range(seqs):
            for d in range(1, shards):
                turn_copy(turned, d, s).wait_send()
        out_scatter[4]()
        qkv_scatter[4]()
        if relay:
            for index in range(2):
                pass_copy(index).wait_send()
        for d in range(1, 3 if relay else chips):
            for index in range(2):
                part_copy(d, index).wait_send()
                part_copy(d, index).wait_recv()

    def weight_load(weight, k):
        return pltpu.make_async_copy(weight_ref.at[k], weight.at[k % 2], one_sem.at[k % 2])

    pl.run_scoped(
        attention,
        pltpu.VMEM((shards, span, part), bf16),
        pltpu.VMEM((shards, span, wide), bf16),
        pltpu.VMEM((seqs, shards, span, part), bf16),
        pltpu.VMEM((2, shards * span, HEAD_DIM), f32),
        pltpu.VMEM((shards, rows, part), bf16),
        pltpu.VMEM((rows, width), bf16),
        pltpu.VMEM((rows, width), bf16),
        pltpu.VMEM((chips, owned, qkv_width), bf16),
        pltpu.VMEM((2, owned, qkv_width), bf16),
        pltpu.VMEM((2, rows, owned), f32),
    )

    late_copy(0).wait_send()
    late_copy(1).wait_send()
    for s in range(seqs):
        for d in range(1, shards):
            grad_copy(d, s).wait_send()
    for which in range(2):
        for d in range(1, shards):
            inner_copy(which, d).wait_send()
    if line:

        @pl.when(is_inner)
        def _():
            for c in range(chunks - 4, chunks):
                mid_copy(c).wait_send()
            for c in (chunks - 2, chunks - 1):
                out_copy(c).wait_send()
                keep_copy(c).wait()

        @pl.when(jnp.logical_not(is_inner))
        def _():
            for c in range(chunks):
                end_copy(c).wait_send()
                out_copy(c).wait_recv()


def tail(
    heads, normed_all, cot_all, mixed, gate, up, partials, late, outs,
    hidden, cot, output, weight, qkv, normed, attn, *tables,
):
    shards, seqs, span, part = qkv.shape
    rows, width = normed.shape
    chips = shards // 2
    units = mixed.shape[1] // 2
    owned = width // shards
    wide = heads * HEAD_DIM
    full = shards * part + width
    across = full // units
    chunks = (units // owned) * (width // units) + 2 * shards + across
    tiles = width // rows
    hbm = pl.BlockSpec(memory_space=pl.ANY)
    vmem = pl.BlockSpec(memory_space=pltpu.VMEM)
    dma = pltpu.SemaphoreType.DMA

    def low(*shape):
        return jax.ShapeDtypeStruct(shape, bf16)

    def high(*shape):
        return jax.ShapeDtypeStruct(shape, f32)

    pieces = low(chunks, owned, units)
    out_shape = (
        low(units, width), low(2, width, units), low(units, width), low(2, width, units),
        low(rows, width), high(rows, width),
        low(2, shards, owned, units), low(shards, rows, wide), low(shards, rows, part),
        pieces, pieces, low(chips, owned, width), low(chips, owned, shards * part),
        low(2, rows // 2, width), low(*outs.shape),
        low(across, owned, units), high(rows, width),
        low(units, width), low(owned, shards * units), low(owned, shards * units), low(owned, full),
    )
    length = shards * span
    return pl.pallas_call(
        functools.partial(tail_kernel, heads),
        in_specs=[hbm] * 15 + [vmem] * 7,
        out_specs=(hbm,) * len(out_shape),
        out_shape=out_shape,
        scratch_shapes=[
            pltpu.VMEM((rows, width), bf16),
            pltpu.VMEM((shards, rows, wide), bf16),
            pltpu.VMEM((chips, owned, width), bf16),
            pltpu.VMEM((chips, owned, shards * part), bf16),
            pltpu.VMEM((2, owned // 2, width), bf16),
            pltpu.VMEM((2, owned // 2, shards * part), bf16),
            pltpu.VMEM((owned, units), bf16),
            pltpu.VMEM((2, owned, units), bf16),
            pltpu.VMEM((4, owned, units), bf16),
            pltpu.VMEM((2, owned, units), bf16),
            dma((3, tiles)), dma((3, tiles)), dma((2,)), dma((2,)),
            dma((2, shards)), dma((2, shards)), dma((shards, seqs)), dma((shards, seqs)),
            dma((shards, seqs)), dma((shards, seqs)), dma((2, chips)), dma((2, chips)),
            dma((2, chips, 2)), dma((2, chips, 2)), dma((chips, 2)), dma((chips, 2)),
            dma((chunks,)), dma((chunks,)), dma((chunks,)), dma((chunks,)), dma((chunks,)),
            dma((chunks,)), dma((2, 2)), dma((2, 2)), dma((2,)), dma((2,)),
            dma((3 + 3 * chips,)), dma((3, tiles)), dma(()), dma((3,)), dma((5 + chips,)),
            dma((2 + seqs,)), dma((3,)), dma((2,)), dma((across,)), dma((4,)),
        ],
        compiler_params=pltpu.CompilerParams(
            collective_id=1, has_side_effects=True, vmem_limit_bytes=63 * 2**20
        ),
        cost_estimate=pl.CostEstimate(
            flops=10 * seqs * heads * length * length * HEAD_DIM + 6 * chips * rows * width * width,
            bytes_accessed=2**29,
            transcendentals=seqs * heads * length * length,
        ),
    )(
        normed_all, cot_all, mixed, gate, up, partials, late, outs,
        hidden, cot, output, weight, qkv, normed, attn, *tables,
    )


def norm_back(grad_normed, unit_rows, scale_rows, gain_rows):
    scaled_grad = grad_normed * gain_rows
    return scale_rows * (
        scaled_grad - unit_rows * jnp.mean(scaled_grad * unit_rows, -1, keepdims=True)
    )


def body(
    tokens,
    segments,
    positions,
    cotangent,
    attention_gain,
    query_weight,
    key_weight,
    value_weight,
    output_weight,
    mlp_gain,
    gate_weight,
    up_weight,
    down_weight,
):
    seqs, span, width = tokens.shape
    shards = lax.axis_size("shard")
    me = lax.axis_index("shard")
    rows = seqs * span
    length = shards * span
    owned = query_weight.shape[0]
    heads = HEADS // shards
    copies = max(1, shards // KV_HEADS)
    wide = heads * HEAD_DIM
    part = wide + 2 * HEAD_DIM
    hidden_share = down_weight.shape[0]

    chips = shards // 2
    replicas = lax.axis_size("replica")
    swap = [(i, i + 1 - 2 * (i % 2)) for i in range(shards)]

    share = owned // replicas
    units = 2 * hidden_share
    share_own = lax.dynamic_slice_in_dim(
        jnp.stack([gate_weight, up_weight]), lax.axis_index("replica") * share, share, 1
    )
    share_own = jnp.transpose(share_own.reshape(2, share, chips, units), (2, 0, 1, 3))
    down_other = lax.ppermute(down_weight, "shard", swap)

    def per_head(weight):
        return jnp.repeat(weight.reshape(owned, KV_HEADS, HEAD_DIM), copies, axis=1)

    qkv_owned = jnp.concatenate(
        [query_weight.reshape(owned, shards, wide), per_head(key_weight), per_head(value_weight)],
        -1,
    ).reshape(owned, shards * part)

    angle = angles(positions).reshape(rows, HEAD_DIM // 2)
    cosine, sine = jnp.cos(angle), jnp.sin(angle)
    still = jnp.ones((rows, HEAD_DIM), f32)
    cos_lanes = jnp.concatenate([cosine] * (2 * heads + 2) + [still], 1)
    sin_lanes = jnp.concatenate([-sine, sine] * (heads + 1) + [still * 0.0], 1)
    small_gains = jnp.stack([attention_gain, mlp_gain]).astype(f32)
    small_places = jnp.stack([segments, positions]).astype(f32)
    (
        shares, qkv_full, output_full, qkv, attn, normed_one, hidden, normed_two,
        norms, scale_two, gains, places, seg_col, seg_row,
    ) = head(
        heads, share_own, qkv_owned, output_weight, tokens.reshape(rows, width), small_gains,
        small_places, cos_lanes, sin_lanes,
    )
    gain_one, gain_two = gains[:, 0].reshape(width), gains[:, 1].reshape(width)
    spots = jnp.swapaxes(places[:, 1], 0, 1).reshape(seqs, length)
    angle_all = jnp.swapaxes(angles(spots), 1, 2)
    cos_all, sin_all = jnp.cos(angle_all), jnp.sin(angle_all)

    x = tokens.reshape(rows, width).astype(f32)
    scale_one = lax.rsqrt(jnp.mean(x * x, -1, keepdims=True) + epsilon)
    unit_one = x * scale_one

    cot_rows = cotangent.reshape(rows, width)
    normed_all, cot_all, partials, late, outs, mixed, gate, up = feed_forward(
        normed_two, cot_rows, shares, down_weight, down_other
    )
    results = tail(
        heads, normed_all, cot_all, mixed, gate, up, partials, late, outs, hidden, cot_rows,
        output_full, qkv_full, qkv, normed_one, attn, scale_two, gain_two[None], norms, seg_col,
        seg_row, cos_all, sin_all,
    )
    down_part, grad_hidden, inner_blocks = results[0], results[5], results[6]
    out_land, total, grad_one, summed = results[14], results[15], results[16], results[17:]
    out_sum = lax.dynamic_index_in_dim(outs, me // 2, 0, keepdims=False).astype(f32)
    arrived = 3 if chips == 4 else chips
    out_sum = out_sum + jnp.sum(out_land[1:arrived].astype(f32), 0)
    block_out = (hidden + out_sum).astype(bf16)

    if replicas != 4:

        def side_by_side(some):
            return jnp.swapaxes(some, 0, 1).reshape(owned, some.shape[0] * hidden_share)

        out_blocks = width // hidden_share
        rest_blocks = jnp.concatenate([total[out_blocks:], total[:out_blocks]])
        summed = lax.psum(
            (
                down_part, side_by_side(inner_blocks[0]), side_by_side(inner_blocks[1]),
                side_by_side(rest_blocks),
            ),
            "replica",
        )
    down_grad, gate_grad, up_grad, rest = [some.astype(f32) for some in summed]
    key_at, value_at = shards * wide, shards * (wide + HEAD_DIM)
    output_grad = rest[:, shards * part :]

    def kv_grad(columns):
        return jnp.sum(columns.reshape(owned, KV_HEADS, copies, HEAD_DIM), 2).reshape(
            owned, KV_HEADS * HEAD_DIM
        )

    query_grad = rest[:, :key_at]
    key_grad = kv_grad(rest[:, key_at:value_at])
    value_grad = kv_grad(rest[:, value_at : shards * part])

    own_one, own_two = attention_gain.astype(f32), mlp_gain.astype(f32)
    gain_one_grad = (
        jnp.sum(query_weight.astype(f32) * query_grad, 1)
        + jnp.sum(key_weight.astype(f32) * key_grad + value_weight.astype(f32) * value_grad, 1)
    ) / own_one
    gain_two_grad = (
        jnp.sum(gate_weight.astype(f32) * gate_grad + up_weight.astype(f32) * up_grad, 1) / own_two
    )
    token_grad = grad_hidden + norm_back(grad_one, unit_one, scale_one, gain_one)
    return (
        block_out.reshape(seqs, span, width),
        token_grad.reshape(seqs, span, width),
        gain_one_grad,
        query_grad,
        key_grad,
        value_grad,
        output_grad,
        gain_two_grad,
        gate_grad,
        up_grad,
        down_grad,
    )


def solution(mesh):
    rows = P("shard", None)
    blocks = P("replica", "shard", None)
    in_specs = (
        blocks, P("replica", "shard"), P("replica", "shard"), blocks, P("shard"),
        rows, rows, rows, rows, P("shard"), rows, rows, rows,
    )
    out_specs = (
        blocks, blocks, P("shard"), rows, rows, rows, rows, P("shard"), rows, rows, rows,
    )
    return jax.shard_map(body, mesh=mesh, in_specs=in_specs, out_specs=out_specs, check_vma=False)
```

```python
import functools
import math

import jax
import jax.numpy as jnp
from jax import lax
from jax.experimental import pallas as pl
from jax.experimental.pallas import tpu as pltpu
from jax.sharding import PartitionSpec as P

HEADS = 32
KV_HEADS = 8
HEAD_DIM = 64

epsilon = 1e-05
rope_base = 500000.0
masked_score = -1e30
f32 = jnp.float32
bf16 = jnp.bfloat16


def angles(doc_positions):
    freq_index = jnp.arange(HEAD_DIM // 2, dtype=f32)
    inverse_freq = jnp.exp(freq_index * (-2.0 * math.log(rope_base) / HEAD_DIM))
    return doc_positions.astype(f32)[..., None] * inverse_freq


def outer_sum(left, right):
    return lax.dot_general(left, right, (((0,), (0,)), ((), ())), preferred_element_type=f32)


def dot_nt(left, right):
    return lax.dot_general(left, right, (((1,), (1,)), ((), ())), preferred_element_type=f32)


def dot_nn(left, right):
    return lax.dot_general(left, right, (((1,), (0,)), ((), ())), preferred_element_type=f32)


def score_bias(seg_col, seg_row, first, rows):
    last = first + rows
    key_at = lax.broadcasted_iota(jnp.int32, (last, rows), 0)
    query_at = lax.broadcasted_iota(jnp.int32, (last, rows), 1) + first
    allowed = (seg_col[:last] == seg_row[:, first:last]) & (key_at <= query_at)
    return jnp.where(allowed, 0.0, masked_score)


def attention_fore(heads, rows, qkv_ref, seg_col, seg_row, out_ref, norm_ref):
    shards, span, _ = qkv_ref.shape
    length = shards * span
    wide = heads * HEAD_DIM
    keys = qkv_ref[:, :, wide : wide + HEAD_DIM].reshape(length, HEAD_DIM)
    values = qkv_ref[:, :, wide + HEAD_DIM :].reshape(length, HEAD_DIM)
    values_t = values.astype(f32).T.astype(bf16)
    for first in range(0, length, rows):
        last = first + rows
        at = slice(first // span, last // span)
        bias = score_bias(seg_col, seg_row, first, rows)
        queries = qkv_ref[at, :, :wide].reshape(rows, wide) * HEAD_DIM ** (-0.5)
        parts = []
        for head in range(heads):
            one = queries[:, head * HEAD_DIM : (head + 1) * HEAD_DIM]
            scores = dot_nt(keys[:last], one) + bias
            top = jnp.max(scores, 0, keepdims=True)
            lifted = jnp.exp(scores - top)
            total = jnp.sum(lifted, 0, keepdims=True)
            probs = (lifted * (1.0 / total)).astype(bf16)
            parts.append(dot_nn(values_t[:, :last], probs))
            norm_ref[head : head + 1, first:last] = top + jnp.log(total)
        out = jnp.concatenate(parts, 0).T.astype(bf16)
        out_ref[at] = out.reshape(rows // span, span, wide)


def turn_back(part, cosine, sine):
    half = HEAD_DIM // 2
    lower, upper = part[:half], part[half:]
    return [lower * cosine + upper * sine, upper * cosine - lower * sine]


def attention_back(
    heads, rows, qkv_ref, grad_ref, norm, seg_col, seg_row, cos, sin, out_ref, sums, between
):
    shards, span, _ = qkv_ref.shape
    length = shards * span
    wide = heads * HEAD_DIM
    keys = qkv_ref[:, :, wide : wide + HEAD_DIM].reshape(length, HEAD_DIM)
    values = qkv_ref[:, :, wide + HEAD_DIM :].reshape(length, HEAD_DIM)
    keys_t = keys.astype(f32).T.astype(bf16)
    sums[...] = jnp.zeros_like(sums)
    key_sum, value_sum = sums.at[0], sums.at[1]
    for first in range(0, length, rows):
        last = first + rows
        at = slice(first // span, last // span)
        bias = score_bias(seg_col, seg_row, first, rows)
        queries = qkv_ref[at, :, :wide].reshape(rows, wide) * HEAD_DIM ** (-0.5)
        grads = grad_ref[at].reshape(rows, wide)
        cosine, sine = cos[:, first:last], sin[:, first:last]
        parts = []
        for head in range(heads):
            lanes = slice(head * HEAD_DIM, (head + 1) * HEAD_DIM)
            one, grad = queries[:, lanes], grads[:, lanes]
            scores = dot_nt(keys[:last], one) + bias
            probs = jnp.exp(scores - norm[head : head + 1, first:last])
            grad_probs = dot_nt(values[:last], grad)
            level = jnp.sum(probs * grad_probs, 0, keepdims=True)
            grad_scores = (probs * (grad_probs - level)).astype(bf16)
            value_sum[:last] += dot_nn(probs.astype(bf16), grad)
            key_sum[:last] += dot_nn(grad_scores, one)
            turned = dot_nn(keys_t[:, :last], grad_scores) * HEAD_DIM ** (-0.5)
            parts.extend(turn_back(turned, cosine, sine))
        out = jnp.concatenate(parts, 0).T.astype(bf16)
        out_ref[at, :, :wide] = out.reshape(rows // span, span, wide)
        if last * 4 == length * 3:
            between()
    key_parts = turn_back(key_sum[...].T, cos[...], sin[...])
    both = jnp.concatenate([jnp.concatenate(key_parts, 0).T, value_sum[...]], -1)
    out_ref[:, :, wide:] = both.astype(bf16).reshape(shards, span, 2 * HEAD_DIM)


def chip_at(chip, distance):
    result, bit = chip, 1
    while bit <= distance:
        if distance & bit:
            result = result + bit * (1 - 2 * ((chip // bit) % 2))
        bit *= 2
    return result


def head_kernel(
    heads,
    share_ref, weight_ref, output_ref, token_ref, gain_ref, place_ref, cos_ref, sin_ref,
    share_land, weight_out, output_land, qkv_land, attn_land, normed_out, hidden_out, second_out,
    norm_ref, scale_ref, gain_out, place_out, seg_col_ref, seg_row_ref,
    weights, tokens, normed, made, qkv, attended, hidden, gains, places,
    small_send, small_recv,
    share_send, share_recv, line_send, line_recv, swap_send, swap_recv,
    weight_send, weight_recv, near_send, near_recv, output_send, output_recv, close_send, close_recv,
    qkv_send, qkv_recv, attn_send, attn_recv, self_sem, load_sem,
):
    shards, owned, columns = weights.shape
    chips = shards // 2
    rows, width = token_ref.shape
    _, seqs, span, part = qkv_land.shape
    wide = heads * HEAD_DIM
    replicas = lax.axis_size("replica")
    me, replica = lax.axis_index("shard"), lax.axis_index("replica")
    chip, core = me // 2, me % 2
    partner = [
        chip_at(chip, d // 2) * 2 + (core if d % 2 == 0 else 1 - core) for d in range(shards)
    ]
    relay = chips == 4
    half_owned = owned // 2

    def remote(source, target, send, recv, shard, to=None):
        return pltpu.make_async_remote_copy(
            src_ref=source, dst_ref=target, send_sem=send, recv_sem=recv,
            device_id=(replica if to is None else to, shard),
            device_id_type=pl.DeviceIdType.MESH,
        )

    barrier = pltpu.get_barrier_semaphore()

    def greet(to, shard):
        pl.semaphore_signal(
            barrier, inc=1, device_id=(to, shard), device_id_type=pl.DeviceIdType.MESH
        )

    for d in range(1, shards):
        greet(replica, partner[d])
    has_left, has_right = replica > 0, replica < replicas - 1

    @pl.when(has_left)
    def _():
        greet(replica - 1, me)

    @pl.when(has_right)
    def _():
        greet(replica + 1, me)

    @pl.when(has_left & has_right)
    def _():
        pl.semaphore_wait(barrier, shards + 1)

    @pl.when(jnp.logical_not(has_left & has_right))
    def _():
        pl.semaphore_wait(barrier, shards)

    def small_copy(which, d):
        source, land = ((gain_ref, gains), (place_ref, places))[which]
        return remote(
            source, land.at[me], small_send.at[which, d], small_recv.at[which, d], partner[d]
        )

    for which in range(2):
        for d in range(1, shards):
            small_copy(which, d).start()
    take_tokens = pltpu.make_async_copy(token_ref, tokens, load_sem.at[0])
    take_tokens.start()
    gains[me] = gain_ref[...]
    places[me] = place_ref[...]

    def share_copy(d):
        return remote(
            share_ref.at[chip_at(chip, d)], share_land.at[core, replica, chip],
            share_send.at[d], share_recv.at[d], partner[2 * d],
        )

    own_share = pltpu.make_async_copy(
        share_ref.at[chip], share_land.at[core, replica, chip], self_sem.at[0]
    )
    own_share.start()
    for d in range(1, chips):
        share_copy(d).start()

    def rows_copies(ref, land, far_send, far_recv, side_send, side_recv):
        def half(index):
            return pl.ds(index * half_owned, half_owned)

        def far(d, index):
            if relay and d == 3:
                origin, way = (1, 2) if index == 0 else (2, 1)
                at = partner[2 * origin]
                return remote(
                    land.at[at, half(index)], land.at[at, half(index)],
                    far_send.at[d, index], far_recv.at[d, index], partner[2 * way],
                )
            return remote(
                ref.at[half(index)], land.at[me, half(index)],
                far_send.at[d, index], far_recv.at[d, index], partner[2 * d],
            )

        def near(d, index):
            at = partner[2 * d]
            source = ref.at[half(index)] if d == 0 else land.at[at, half(index)]
            return remote(
                source, land.at[at, half(index)],
                side_send.at[d, index], side_recv.at[d, index], partner[1],
            )

        return far, near

    def start_rows(far, near, halves=range(2)):
        for index in halves:
            for d in range(1, chips):
                if not (relay and d == 3):
                    far(d, index).start()
        for index in halves:
            near(0, index).start()

    def pass_rows(far, near, between=None):
        if relay:
            for index in range(2):
                for d in (1, 2):
                    far(d, index).wait_recv()
                far(3, index).start()
                for d in (1, 2):
                    near(d, index).start()
                if between is not None:
                    between(index)
            for index in range(2):
                far(3, index).wait_recv()
                near(3, index).start()
        else:
            for d in range(1, chips):
                for index in range(2):
                    far(d, index).wait_recv()
                    near(d, index).start()

    def end_rows(far, near):
        for d in range(chips):
            for index in range(2):
                near(d, index).wait_recv()

    def sent_rows(far, near):
        for d in range(chips):
            for index in range(2):
                near(d, index).wait_send()
                if d > 0:
                    far(d, index).wait_send()

    weight_rows = rows_copies(
        weight_ref, weights, weight_send, weight_recv, near_send, near_recv
    )
    output_rows = rows_copies(
        output_ref, output_land, output_send, output_recv, close_send, close_recv
    )
    own_weight = pltpu.make_async_copy(weight_ref, weights.at[me], self_sem.at[1])
    own_weight.start()
    own_output = pltpu.make_async_copy(output_ref, output_land.at[me], self_sem.at[2])
    own_output.start()

    def share_at(way, distance, index):
        far = replica - distance if way == 0 else replica + distance
        return share_land.at[core, far, pl.ds(index * (chips // 2), chips // 2)]

    def line_copy(way, step, index):
        at = share_at(way, step, index)
        return remote(
            at, at, line_send.at[way, step, index], line_recv.at[way, step, index], me,
            replica + 1 if way == 0 else replica - 1,
        )

    def came(way, step, index):
        at = share_at(way, step + 1, index)
        return remote(
            at, at, line_send.at[way, step, index], line_recv.at[way, step, index], me
        )

    def swap_copy(way, step, index):
        at = share_at(way, step, index)
        return remote(
            at, at, swap_send.at[way, step, index], swap_recv.at[way, step, index], partner[1]
        )

    def line_step(step, index):
        if step == 0 and index == 0:
            own_share.wait()
            for d in range(1, chips):
                share_copy(d).wait_recv()
        if step == 0:
            swap_copy(0, 0, index).start()
        for way in range(2):
            room = replica - step >= 0 if way == 0 else replica + step < replicas
            onward = has_right if way == 0 else has_left
            if step > 0:

                @pl.when(room)
                def _():
                    came(way, step - 1, index).wait_recv()
                    swap_copy(way, step, index).start()

            if step < replicas - 1:

                @pl.when(room & onward)
                def _():
                    line_copy(way, step, index).start()

    line_step(0, 0)
    line_step(0, 1)
    start_rows(*weight_rows)

    for which in range(2):
        for d in range(1, shards):
            small_copy(which, d).wait_recv()
    gain_out[...] = gains[...]
    place_out[...] = places[...]
    for s in range(seqs):
        seg_row_ref[s] = jnp.concatenate([places[k, 0, s : s + 1] for k in range(shards)], 1)
        turned = jnp.concatenate([places[k, 0, s : s + 1] for k in range(shards)], 0).T
        seg_col_ref[s] = jnp.concatenate([turned[:, k : k + 1] for k in range(shards)], 0)

    def gain_row(which):
        return jnp.concatenate([gains[k, which : which + 1] for k in range(shards)], 1)

    take_tokens.wait()
    gain_one = gain_row(0)

    @pl.loop(0, rows // 32)
    def _(i):
        at = pl.ds(pl.multiple_of(i * 32, 32), 32)
        x = tokens[at].astype(f32)
        unit = x * lax.rsqrt(jnp.mean(x * x, -1, keepdims=True) + epsilon)
        normed[at] = (unit * gain_one).astype(bf16)

    keep_normed = pltpu.make_async_copy(normed, normed_out, load_sem.at[0])
    keep_normed.start()
    if relay and replicas > 2:
        pass_rows(*weight_rows, between=lambda index: line_step(1, index))
    else:
        pass_rows(*weight_rows)
        if replicas > 2:
            line_step(1, 0)
            line_step(1, 1)
    own_weight.wait()
    keep_normed.wait()
    start_rows(*output_rows, halves=range(1))
    end_rows(*weight_rows)
    keep_weight = pltpu.make_async_copy(weights, weight_out, self_sem.at[1])
    keep_weight.start()

    lane = lax.broadcasted_iota(jnp.int32, (rows, part), 1)
    lower = lane % HEAD_DIM < HEAD_DIM // 2

    def project(owner):
        at = pl.ds(pl.multiple_of(owner * part, part), part)
        value = dot_nn(normed[...], weights[:, :, at].reshape(width, part))
        swapped = jnp.where(
            lower,
            pltpu.roll(value, part - HEAD_DIM // 2, 1),
            pltpu.roll(value, HEAD_DIM // 2, 1),
        )
        turned = value * cos_ref[...] + swapped * sin_ref[...]
        made[owner] = turned.astype(bf16)

    @pl.loop(0, shards)
    def _(k):
        project(k)

    def at_seq(s):
        return pl.ds(pl.multiple_of(s * span, span), span)

    def qkv_copy(d, s):
        return remote(
            made.at[partner[d], at_seq(s)], qkv_land.at[me, s],
            qkv_send.at[d, s], qkv_recv.at[d, s], partner[d],
        )

    def own_qkv(s):
        return pltpu.make_async_copy(made.at[me, at_seq(s)], qkv_land.at[me, s], load_sem.at[1 + s])

    for s in range(seqs):
        own_qkv(s).start()
        for d in range(shards - 1, 0, -1):
            qkv_copy(d, s).start()
    if replicas > 3:
        line_step(2, 0)

    def attn_copy(d, s):
        return remote(
            attended.at[s, partner[d]],
            attn_land.at[at_seq(s), pl.ds(pl.multiple_of(me * wide, wide), wide)],
            attn_send.at[d, s], attn_recv.at[d, s], partner[d],
        )

    def own_attn(s):
        return pltpu.make_async_copy(
            attended.at[s, me],
            attn_land.at[at_seq(s), pl.ds(pl.multiple_of(me * wide, wide), wide)],
            load_sem.at[1 + s],
        )

    @pl.loop(0, seqs)
    def _(s):
        own_qkv(s).wait()
        for d in range(1, shards):
            qkv_copy(d, s).wait_recv()
        take = pltpu.make_async_copy(qkv_land.at[:, s], qkv, load_sem.at[0])
        take.start()
        take.wait()
        attention_fore(
            heads, 256, qkv, seg_col_ref[s], seg_row_ref[s], attended.at[s], norm_ref.at[s]
        )
        own_attn(s).start()
        for d in range(1, shards):
            attn_copy(d, s).start()

        @pl.when(s == 0)
        def _():
            start_rows(*output_rows, halves=range(1, 2))
            if replicas > 3:
                line_step(2, 1)

    for step in range(2, replicas):
        for index in range(2):
            if (step, index) not in ((2, 0), (2, 1)) and step < replicas - 1:
                line_step(step, index)
    pass_rows(*output_rows)
    for s in range(seqs):
        own_attn(s).wait()
        for d in range(1, shards):
            attn_copy(d, s).wait_recv()
    end_rows(*output_rows)
    own_output.wait()
    keep_weight.wait()
    sent_rows(*weight_rows)
    take_output = pltpu.make_async_copy(
        output_land, weights.at[:, :, pl.ds(0, width)], self_sem.at[1]
    )
    take_attn = pltpu.make_async_copy(attn_land, normed, load_sem.at[0])
    take_output.start()
    take_attn.start()
    line_step(replicas - 1, 0)
    take_output.wait()
    take_attn.wait()

    @pl.loop(0, width // 512)
    def _(j):
        at = pl.ds(pl.multiple_of(j * 512, 512), 512)
        hidden[:, at] = tokens[:, at].astype(f32) + dot_nn(
            normed[...], weights[:, :, at].reshape(width, 512)
        )

    keep_hidden = pltpu.make_async_copy(hidden, hidden_out, self_sem.at[1])
    keep_hidden.start()
    gain_two = gain_row(1)

    @pl.loop(0, rows // 32)
    def _(i):
        at = pl.ds(pl.multiple_of(i * 32, 32), 32)
        x = hidden[at]
        scale = lax.rsqrt(jnp.mean(x * x, -1, keepdims=True) + epsilon)
        scale_ref[at] = scale
        normed[at] = (x * scale * gain_two).astype(bf16)

    keep_second = pltpu.make_async_copy(normed, second_out, load_sem.at[0])
    keep_second.start()
    line_step(replicas - 1, 1)
    keep_hidden.wait()
    keep_second.wait()

    for which in range(2):
        for d in range(1, shards):
            small_copy(which, d).wait_send()
    sent_rows(*output_rows)
    for d in range(1, chips):
        share_copy(d).wait_send()
    for s in range(seqs):
        for d in range(1, shards):
            qkv_copy(d, s).wait_send()
            attn_copy(d, s).wait_send()
    for index in range(2):
        swap_copy(0, 0, index).wait_send()
        swap_copy(0, 0, index).wait_recv()
        for way in range(2):
            for step in range(replicas):
                room = replica - step >= 0 if way == 0 else replica + step < replicas
                onward = has_right if way == 0 else has_left
                if step > 0:

                    @pl.when(room)
                    def _():
                        swap_copy(way, step, index).wait_send()
                        swap_copy(way, step, index).wait_recv()

                if step < replicas - 1:

                    @pl.when(room & onward)
                    def _():
                        line_copy(way, step, index).wait_send()


def head(heads, share, weight, output, tokens, gains, places, cosine, sine):
    chips = share.shape[0]
    shards = 2 * chips
    rows, width = tokens.shape
    _, seqs, span = places.shape
    owned, columns = weight.shape
    part = columns // shards
    wide = heads * HEAD_DIM
    length = shards * span
    replicas = lax.axis_size("replica")
    hbm = pl.BlockSpec(memory_space=pl.ANY)
    vmem = pl.BlockSpec(memory_space=pltpu.VMEM)
    dma = pltpu.SemaphoreType.DMA

    def low(*shape):
        return jax.ShapeDtypeStruct(shape, bf16)

    def high(*shape):
        return jax.ShapeDtypeStruct(shape, f32)

    out_shape = (
        low(2, replicas, *share.shape), low(shards, owned, columns), low(shards, owned, width),
        low(shards, seqs, span, part), low(rows, shards * wide),
        low(rows, width), high(rows, width), low(rows, width),
        high(seqs, heads, length), high(rows, 1), high(shards, *gains.shape),
        high(shards, *places.shape), high(seqs, length, 1), high(seqs, 1, length),
    )
    return pl.pallas_call(
        functools.partial(head_kernel, heads),
        in_specs=[hbm] * 4 + [vmem] * 4,
        out_specs=(hbm,) * 8 + (vmem,) * 6,
        out_shape=out_shape,
        scratch_shapes=[
            pltpu.VMEM((shards, owned, columns), bf16),
            pltpu.VMEM((rows, width), bf16),
            pltpu.VMEM((rows, width), bf16),
            pltpu.VMEM((shards, rows, part), bf16),
            pltpu.VMEM((shards, span, part), bf16),
            pltpu.VMEM((seqs, shards, span, wide), bf16),
            pltpu.VMEM((rows, width), f32),
            pltpu.VMEM((shards, *gains.shape), f32),
            pltpu.VMEM((shards, *places.shape), f32),
            dma((2, shards)), dma((2, shards)),
            dma((chips,)), dma((chips,)), dma((2, replicas, 2)), dma((2, replicas, 2)),
            dma((2, replicas, 2)), dma((2, replicas, 2)),
            dma((chips, 2)), dma((chips, 2)), dma((chips, 2)), dma((chips, 2)),
            dma((chips, 2)), dma((chips, 2)), dma((chips, 2)), dma((chips, 2)),
            dma((shards, seqs)), dma((shards, seqs)), dma((shards, seqs)), dma((shards, seqs)),
            dma((3,)), dma((1 + seqs,)),
        ],
        compiler_params=pltpu.CompilerParams(
            collective_id=2, has_side_effects=True, vmem_limit_bytes=56 * 2**20
        ),
        cost_estimate=pl.CostEstimate(
            flops=4 * seqs * heads * length * length * HEAD_DIM,
            bytes_accessed=2**28,
            transcendentals=seqs * heads * length * length,
        ),
    )(share, weight, output, tokens, gains, places, cosine, sine)


def pieces_of(chips):
    if chips == 4:
        return [[(0, 0), (0, 1)], [(1, 0), (2, 0)], [(1, 1), (2, 1)], [(3, 0), (3, 1)]]
    return [[(d, 0), (d, 1)] for d in range(chips)]


def feed_kernel(
    normed_ref, cot_own_ref, share_ref, down_own_ref, down_other_ref,
    normed_out, cot_ref, partial_ref, late_ref, out_ref, mixed_ref, gate_ref, up_ref,
    weights, normed, cot, inner, sent, out_stage, kept,
    weight_sem, normed_send, normed_recv, far_send, far_recv, cot_sem, inner_sem,
    sum_send, sum_recv, own_sem, late_sem, out_sem, keep_sem,
):
    chips, rows, width = normed.shape
    units = mixed_ref.shape[1]
    half_rows, half_units = rows // 2, units // 2
    _, replicas, _, _, share, _ = share_ref.shape
    me = lax.axis_index("shard")
    replica = lax.axis_index("replica")
    chip, core = me // 2, me % 2
    partner = [chip_at(chip, d) * 2 + core for d in range(chips)]
    steps = pieces_of(chips)
    spot = {piece: (i, at) for i, step in enumerate(steps) for at, piece in enumerate(step)}
    relay = chips == 4

    def remote(source, target, send, recv, shard):
        return pltpu.make_async_remote_copy(
            src_ref=source, dst_ref=target, send_sem=send, recv_sem=recv,
            device_id=(replica, shard), device_id_type=pl.DeviceIdType.MESH,
        )

    barrier = pltpu.get_barrier_semaphore()
    for shard in partner[1:]:
        pl.semaphore_signal(
            barrier, inc=1, device_id=(replica, shard), device_id_type=pl.DeviceIdType.MESH
        )
    pl.semaphore_wait(barrier, chips - 1)

    def half(index):
        return pl.ds(index * half_rows, half_rows)

    def block_copy(which, d, part):
        own, land = ((normed_ref, normed), (cot_own_ref, cot_ref))[which]
        send, recv = ((normed_send, normed_recv), (far_send, far_recv))[which]
        index, at = spot[d, part]
        if relay and d == 3:
            origin, way = (1, 2) if part == 0 else (2, 1)
            from_index, from_at = spot[origin, part]
            source, to = land.at[from_index, half(from_at)], partner[way]
        else:
            source, to = own.at[half(part)], partner[d]
        return remote(source, land.at[index, half(at)], send.at[d, part], recv.at[d, part], to)

    for part in range(2):
        for which in range(2):
            for d in range(1, 3 if relay else chips):
                block_copy(which, d, part).start()
    own_copy = pltpu.make_async_copy(normed_ref, normed.at[0], own_sem.at[0])
    own_copy.start()
    own_cot = pltpu.make_async_copy(cot_own_ref, cot_ref.at[0], own_sem.at[1])
    own_cot.start()

    def cot_copy(index):
        source = cot_own_ref if index == 0 else cot_ref.at[index]
        return pltpu.make_async_copy(source, cot.at[index % 2], cot_sem.at[index % 2])

    cot_copy(0).start()
    owned = share * replicas
    for which in range(2):
        for k in range(chips):
            for z in range(replicas):
                for c in range(2):
                    pltpu.make_async_copy(
                        share_ref.at[c, z, k, which],
                        weights.at[which, pl.ds((2 * k + c) * owned + z * share, share), pl.ds(0, units)],
                        weight_sem.at[which],
                    ).start()
    down_own = pltpu.make_async_copy(
        down_own_ref, weights.at[2, pl.ds(core * half_units, half_units)], weight_sem.at[2]
    )
    down_other = pltpu.make_async_copy(
        down_other_ref, weights.at[2, pl.ds((1 - core) * half_units, half_units)], weight_sem.at[3]
    )
    down_own.start()
    down_other.start()
    own_copy.wait()
    for which in range(2):
        whole = weights.at[which, pl.ds(0, width), pl.ds(0, units)]
        pltpu.make_async_copy(whole, whole, weight_sem.at[which]).wait()
    down_own.wait()
    down_other.wait()

    def inner_copies(index):
        return [
            pltpu.make_async_copy(
                inner.at[which], ref.at[pl.ds(index * rows, rows)], inner_sem.at[which]
            )
            for which, ref in enumerate((mixed_ref, gate_ref, up_ref))
        ]

    def out_copies(index):
        return [
            pltpu.make_async_copy(
                out_stage.at[half(at)], out_ref.at[chip_at(chip, d), half(part)], out_sem.at[at]
            )
            for at, (d, part) in enumerate(steps[index])
        ]

    def sum_copy(index, at):
        d, part = steps[index][at]
        return remote(
            sent.at[index % 2, half(at)], partial_ref.at[d, half(part)],
            sum_send.at[d, part], sum_recv.at[d, part], partner[d],
        )

    own_sum = pltpu.make_async_copy(sent.at[0], partial_ref.at[0], own_sem.at[2])
    late_sum = pltpu.make_async_copy(sent.at[(chips - 1) % 2], late_ref, late_sem)
    keep_normed = pltpu.make_async_copy(normed, normed_out, keep_sem)
    tile = min(512, units)
    for index in range(chips):
        split = index == chips - 1
        for d, part in steps[index]:
            if d > 0:
                block_copy(0, d, part).wait_recv()
                if not split:
                    block_copy(1, d, part).wait_recv()
        if relay and index in (1, 2):
            for which in range(2):
                block_copy(which, 3, index - 1).start()
        if index > 0 and not split:
            cot_copy(index).start()
        if index == chips - 1:
            keep_normed.start()
        if index > 0:
            for copy in inner_copies(index - 1):
                copy.wait()
        if not split:
            cot_copy(index).wait()

        def project_out():
            @pl.loop(0, width // 512)
            def _(j):
                columns = pl.ds(pl.multiple_of(j * 512, 512), 512)
                out_stage[:, columns] = dot_nn(inner[0], weights[2, :units, columns]).astype(bf16)

            for copy in out_copies(index):
                copy.start()

        if split:
            @pl.loop(0, units // tile)
            def _(j):
                columns = pl.ds(pl.multiple_of(j * tile, tile), tile)
                gate = dot_nn(normed[index], weights[0, :width, columns])
                up = dot_nn(normed[index], weights[1, :width, columns])
                kept[0, :, columns] = gate
                kept[1, :, columns] = up
                inner[0, :, columns] = (gate * jax.nn.sigmoid(gate) * up).astype(bf16)

            for copy in out_copies(index - 1):
                copy.wait()
            project_out()
            for d, part in steps[index]:
                block_copy(1, d, part).wait_recv()
            cot_copy(index).start()
            cot_copy(index).wait()

        @pl.loop(0, units // tile)
        def _(j):
            columns = pl.ds(pl.multiple_of(j * tile, tile), tile)
            if split:
                gate, up = kept[0, :, columns], kept[1, :, columns]
            else:
                gate = dot_nn(normed[index], weights[0, :width, columns])
                up = dot_nn(normed[index], weights[1, :width, columns])
            grad = dot_nt(cot[index % 2], weights[2, columns, :])
            sigmoid = jax.nn.sigmoid(gate)
            swish = gate * sigmoid
            if not split:
                inner[0, :, columns] = (swish * up).astype(bf16)
            inner[1, :, columns] = (grad * up * (sigmoid + swish * (1.0 - sigmoid))).astype(bf16)
            inner[2, :, columns] = (grad * swish).astype(bf16)

        for copy in inner_copies(index):
            copy.start()
        if index > 0 and not split:
            for copy in out_copies(index - 1):
                copy.wait()
        if index == 2:
            own_sum.wait()
        if index >= 3:
            for at in range(2):
                sum_copy(index - 2, at).wait_send()

        @pl.loop(0, width // 512)
        def _(j):
            columns = pl.ds(pl.multiple_of(j * 512, 512), 512)
            sent[index % 2, :, columns] = (
                dot_nt(inner[1], weights[0, columns, :units])
                + dot_nt(inner[2], weights[1, columns, :units])
            ).astype(bf16)

        if index == 0:
            own_sum.start()
        elif index == chips - 1:
            late_sum.start()
        else:
            for at in range(2):
                sum_copy(index, at).start()

        if not split:
            project_out()

    for copy in inner_copies(chips - 1):
        copy.wait()
    for copy in out_copies(chips - 1):
        copy.wait()
    late_sum.wait()
    keep_normed.wait()
    own_cot.wait()
    for at in range(2):
        sum_copy(chips - 2, at).wait_send()
    for index in range(1, chips - 1):
        for at in range(2):
            sum_copy(index, at).wait_recv()
    for d in range(1, chips):
        for part in range(2):
            for which in range(2):
                block_copy(which, d, part).wait_send()


def feed_forward(normed, cot, share, down_own, down_other):
    chips = share.shape[2]
    rows, width = normed.shape
    units = down_own.shape[0] * 2
    tokens = chips * rows
    hbm = pl.BlockSpec(memory_space=pl.ANY)
    dma = pltpu.SemaphoreType.DMA

    def low(*shape):
        return jax.ShapeDtypeStruct(shape, bf16)

    out_shape = (
        low(chips, rows, width), low(chips, rows, width), low(chips - 1, rows, width),
        low(rows, width), low(chips, rows, width),
        low(tokens, units), low(tokens, units), low(tokens, units),
    )
    return pl.pallas_call(
        feed_kernel,
        in_specs=[hbm] * 5,
        out_specs=(hbm,) * len(out_shape),
        out_shape=out_shape,
        scratch_shapes=[
            pltpu.VMEM((3, width, width), bf16),
            pltpu.VMEM((chips, rows, width), bf16),
            pltpu.VMEM((2, rows, width), bf16),
            pltpu.VMEM((3, rows, units), bf16),
            pltpu.VMEM((2, rows, width), bf16),
            pltpu.VMEM((rows, width), bf16),
            pltpu.VMEM((2, rows, units), f32),
            dma((4,)), dma((chips, 2)), dma((chips, 2)), dma((chips, 2)), dma((chips, 2)),
            dma((2,)), dma((3,)), dma((chips, 2)), dma((chips, 2)), dma((3,)), dma(()), dma((2,)),
            dma(()),
        ],
        compiler_params=pltpu.CompilerParams(
            collective_id=0, has_side_effects=True, vmem_limit_bytes=63 * 2**20
        ),
        cost_estimate=pl.CostEstimate(
            flops=12 * tokens * units * width, bytes_accessed=2**27, transcendentals=tokens * units
        ),
    )(normed, cot, share, down_own, down_other)


def tail_kernel(
    heads,
    normed_all, cot_all, mixed_ref, gate_ref, up_ref, partial_ref, late_ref, outs_ref,
    hidden_ref, cot_ref, output_ref, weight_ref, qkv_ref, normed_ref, attn_ref,
    scale_ref, gain_ref, norm_ref, seg_col_ref, seg_row_ref, cos_ref, sin_ref,
    down_sum, inner_sum, down_got, inner_got, late_land, hidden_out,
    inner_land, grad_land, turn_land, end_land, mid_land, sum_out, sum_qkv, pass_land, out_land, total,
    one_out, down_result, gate_result, up_result, rest_result,
    branch, grad_made, core_out, core_qkv, relay_out, relay_qkv, mine, theirs, half, whole,
    pair_send, pair_recv, late_send, late_recv,
    inner_send, inner_recv, grad_send, grad_recv, turn_send, turn_recv, core_send, core_recv,
    sum_send, sum_recv, part_send, part_recv, end_send, end_recv, mid_send, mid_recv, out_send,
    out_recv, relay_send, relay_recv, pass_send, pass_recv,
    big_sem, tile_sem, got_sem, self_sem, load_sem, seq_sem, tick_sem, whole_sem, total_sem,
    one_sem,
):
    shards, seqs, span, part = qkv_ref.shape
    rows, width = normed_ref.shape
    _, owned, units = inner_land.shape[1:]
    chips = shards // 2
    tokens = chips * rows
    wide = heads * HEAD_DIM
    chunks = end_land.shape[0]
    qkv_width = shards * part
    full = qkv_width + width
    across = total.shape[0]
    line = lax.axis_size("replica") == 4
    relay = chips == 4
    me, replica = lax.axis_index("shard"), lax.axis_index("replica")
    chip, core = me // 2, me % 2
    partner = [
        chip_at(chip, d // 2) * 2 + (core if d % 2 == 0 else 1 - core) for d in range(shards)
    ]
    is_inner = (replica == 1) | (replica == 2)
    inward = jnp.where(replica < 2, 1, 2)
    outward = jnp.where(replica < 2, 0, 3)

    def partner_at(d):
        if isinstance(d, int):
            return partner[d]
        result, bit = 0, 1
        while bit < shards:
            result = result + bit * (((me // bit) % 2 + (d // bit) % 2) % 2)
            bit *= 2
        return result

    def remote(source, target, send, recv, shard, to=None):
        return pltpu.make_async_remote_copy(
            src_ref=source, dst_ref=target, send_sem=send, recv_sem=recv,
            device_id=(replica if to is None else to, shard),
            device_id_type=pl.DeviceIdType.MESH,
        )

    barrier = pltpu.get_barrier_semaphore()

    def greet(to, shard):
        pl.semaphore_signal(
            barrier, inc=1, device_id=(to, shard), device_id_type=pl.DeviceIdType.MESH
        )

    for d in range(1, shards):
        greet(replica, partner[d])
    if line:

        @pl.when(is_inner)
        def _():
            greet(outward, me)
            greet(3 - replica, me)
            pl.semaphore_wait(barrier, shards + 1)

        @pl.when(jnp.logical_not(is_inner))
        def _():
            greet(inward, me)
            pl.semaphore_wait(barrier, shards)

    else:
        pl.semaphore_wait(barrier, shards - 1)

    half_rows = rows // 2

    def late_copy(index):
        at = pl.ds(index * half_rows, half_rows)
        return remote(
            late_ref.at[at], late_land.at[at], late_send.at[index], late_recv.at[index],
            partner[2 * (chips - 1)],
        )

    late_copy(0).start()
    late_copy(1).start()

    down_across = width // units
    down_chunks = down_sum.shape[0] // owned * down_across
    last_inner = down_chunks + 2 * shards
    up_first = down_chunks + shards
    out_chunks = width // units

    def block(ref, row, column):
        return ref.at[
            pl.ds(pl.multiple_of(row * owned, owned), owned),
            pl.ds(pl.multiple_of(column * units, units), units),
        ]

    def inner_of(c):
        return (c - down_chunks) // shards, (c - down_chunks) % shards

    def source_of(c):
        if isinstance(c, int):
            if c < down_chunks:
                return block(down_sum, c // down_across, c % down_across)
            if c >= last_inner:
                return total.at[c - last_inner]
        which, d = inner_of(c)
        return inner_land.at[which, partner_at(d)]

    def place_of(c):
        if isinstance(c, int):
            if c < down_chunks:
                return block(down_result, c // down_across, c % down_across)
            if c >= last_inner + out_chunks:
                return block(rest_result, 0, c - last_inner - out_chunks)
            if c >= last_inner:
                return block(rest_result, 0, qkv_width // units + c - last_inner)
            which, d = inner_of(c)
            return block((gate_result, up_result)[which], 0, partner[d])
        return block(gate_result, 0, partner_at(inner_of(c)[1]))

    def end_copy(c):
        return remote(source_of(c), end_land.at[c], end_send.at[c], end_recv.at[c], me, inward)

    def mid_copy(c):
        return remote(
            half.at[c % 4], mid_land.at[c], mid_send.at[c], mid_recv.at[c], me, 3 - replica
        )

    def out_copy(c):
        return remote(whole.at[c % 2], place_of(c), out_send.at[c], out_recv.at[c], me, outward)

    def keep_copy(c):
        return pltpu.make_async_copy(whole.at[c % 2], place_of(c), whole_sem.at[c % 2])

    def from_end(c):
        if line:

            @pl.when(jnp.logical_not(is_inner))
            def _():
                end_copy(c).start()

    def take_mine(c):
        return pltpu.make_async_copy(source_of(c), mine, tick_sem.at[0])

    def take_other(c):
        return pltpu.make_async_copy(mid_land.at[c], theirs.at[1], tick_sem.at[2])

    def send_out(c):
        mid_copy(c).wait_recv()
        take_other(c).start()
        if not isinstance(c, int) or c >= 2:
            out_copy(c - 2).wait_send()
            keep_copy(c - 2).wait()
        take_other(c).wait()
        whole[c % 2] = (half[c % 4].astype(f32) + theirs[1].astype(f32)).astype(bf16)
        if isinstance(c, int):
            out_copy(c).start()
            keep_copy(c).start()
            return

        @pl.when(c >= down_chunks)
        def _():
            out_copy(c).start()
            keep_copy(c).start()

        for old in (down_chunks - 2, down_chunks - 1):

            @pl.when(c == old)
            def _():
                out_copy(old).start()
                keep_copy(old).start()

    def middle(c):
        if not line:
            return
        static = isinstance(c, int)

        @pl.when(is_inner)
        def _():
            if static and (c == 0 or c == up_first or c >= last_inner):
                take_mine(c).start()
            end_copy(c).wait_recv()
            two = pltpu.make_async_copy(end_land.at[c], theirs.at[0], tick_sem.at[1])
            two.start()
            if not static or c >= 4:
                mid_copy(c - 4).wait_send()
            take_mine(c).wait()
            two.wait()
            half[c % 4] = (mine[...].astype(f32) + theirs[0].astype(f32)).astype(bf16)
            mid_copy(c).start()
            if not static:

                @pl.when(c + 1 < up_first)
                def _():
                    take_mine(c + 1).start()

            elif c + 1 < last_inner and c + 1 != up_first:
                take_mine(c + 1).start()
            if static and c > last_inner:
                send_out(c - 1)
            elif not static or c >= 2:
                send_out(c - 2)
            if static and c == last_inner:
                send_out(c - 1)

    lead = 3
    position = [0]

    settled = [down_chunks]

    def ticks(count):
        for _ in range(count):
            c = position[0]
            if c >= last_inner:
                return
            position[0] += 1
            ahead = c + lead
            if c >= up_first:
                ahead = min(ahead, up_first + 2 * (c - up_first) + 1)
            while settled[0] <= min(ahead, last_inner - 1):
                settle(settled[0])
                from_end(settled[0])
                settled[0] += 1
            middle(c)

    def later_tick(c):
        @pl.when(c + lead < up_first)
        def _():
            settle(c + lead)
            from_end(c + lead)

        middle(c)

    def inner_copy(which, d):
        at = partner_at(d)
        return remote(
            inner_sum.at[which, pl.ds(pl.multiple_of(at * owned, owned), owned)],
            inner_land.at[which, me],
            inner_send.at[which, d], inner_recv.at[which, d], at,
        )

    def own_inner(which):
        return pltpu.make_async_copy(
            inner_sum.at[which, pl.ds(pl.multiple_of(me * owned, owned), owned)],
            inner_land.at[which, me], self_sem.at[which],
        )

    def start_inner(which):
        own_inner(which).start()
        for d in range(1, shards):
            inner_copy(which, d).start()

    def settle(c):
        which, d = inner_of(c)
        if isinstance(c, int):
            if d == 0:
                own_inner(which).wait()
            else:
                inner_copy(which, d).wait_recv()
            return

        @pl.when(d == 0)
        def _():
            own_inner(which).wait()

        @pl.when(d > 0)
        def _():
            inner_copy(which, d).wait_recv()

    half_units = units
    tiles = width // rows
    per_slot = width // half_units

    def weight_gradients(big, sent_stage, kept_stage):
        got = branch
        def load(ref, slot, columns):
            return pltpu.make_async_copy(
                ref, big.at[slot, pl.ds(0, tokens), pl.ds(0, columns)], big_sem.at[slot]
            )

        def load_blocks(ref, slot):
            return [
                pltpu.make_async_copy(
                    ref.at[k], big.at[slot, pl.ds(k * rows, rows)], big_sem.at[3 + slot * chips + k]
                )
                for k in range(chips)
            ]

        first_loads = load_blocks(cot_all, 1) + [load(mixed_ref, 0, 2 * half_units)]
        normed_loads = load_blocks(normed_all, 2)
        for copy in first_loads + normed_loads:
            copy.start()
        for copy in first_loads:
            copy.wait()

        sums = (down_sum, inner_sum.at[0], inner_sum.at[1])
        gots = (down_got, inner_got.at[0], inner_got.at[1])

        def tile_copies(which, owner, stage):
            result = []
            for t in range(half_units // rows if which == 0 else tiles):
                if which == 0:
                    source = stage.at[t]
                else:
                    source = stage.at[
                        t // per_slot, :, pl.ds((t % per_slot) * half_units, half_units)
                    ]
                place = pl.ds(t * rows, rows)
                if owner == 0:
                    copy = remote(
                        source, gots[which].at[place], pair_send.at[which, t],
                        pair_recv.at[which, t], partner[1],
                    )
                else:
                    copy = pltpu.make_async_copy(
                        source, sums[which].at[place], tile_sem.at[which, t]
                    )
                result.append(copy)
            return result

        pair, made = {}, [0]
        for which in range(3):
            if which == 1:
                later = load(gate_ref, 0, 2 * half_units)
                later.start()
                following = load(up_ref, 1, 2 * half_units)
                following.start()
                for copy in normed_loads:
                    copy.wait()
                later.wait()
            if which == 2:
                following.wait()
            for owner in range(2):
                stage = (sent_stage, kept_stage)[owner]
                first = ((1 - core) if owner == 0 else core) * half_units
                copies = tile_copies(which, owner, stage)
                pair[which, owner] = copies
                if which > 0 and owner == 0:
                    for copy in pair[which - 1, 0]:
                        copy.wait_send()
                for t, copy in enumerate(copies):
                    columns = width if which == 0 else half_units
                    if owner == 1:
                        pair[which, 0][t].wait_recv()
                        take = pltpu.make_async_copy(
                            gots[which].at[pl.ds(t * rows, rows)], got.at[:, pl.ds(0, columns)],
                            got_sem,
                        )
                        take.start()
                    if which == 0:
                        at = pl.ds(pl.multiple_of(first + t * rows, rows), rows)
                        left, right, slot, begin = big[0, :tokens, at], 1, t, 0
                    else:
                        left = big[2, :tokens, t * rows : (t + 1) * rows]
                        right = which - 1
                        slot, begin = t // per_slot, (t % per_slot) * half_units
                    step = min(1024, columns)
                    for j in range(columns // step):
                        if which == 0:
                            at = pl.ds(j * step, step)
                        else:
                            at = pl.ds(pl.multiple_of(first, half_units), half_units)
                        product = outer_sum(left, big[right, :tokens, at])
                        if owner == 1:
                            if j == 0:
                                take.wait()
                            product = product + got[:, j * step : (j + 1) * step].astype(f32)
                        stage[slot, :, begin + j * step : begin + (j + 1) * step] = product.astype(
                            bf16
                        )
                    copy.start()
                    if which == 0 and owner == 1:
                        copy.wait()
                        per_tile = rows // owned * down_across
                        for c in range(t * per_tile, (t + 1) * per_tile):
                            from_end(c)
                    if which > 0:
                        made[0] += 1
                        if made[0] % 3 == 0 and position[0] < down_chunks - lead:
                            ticks(1)
                if owner == 1 and which > 0:
                    for copy in copies:
                        copy.wait()
                    if which == 1:
                        start_inner(0)
        for copy in pair[2, 0]:
            copy.wait_send()

    pl.run_scoped(
        weight_gradients,
        pltpu.VMEM((3, tokens, width), bf16),
        pltpu.VMEM((2, rows, width), bf16),
        pltpu.VMEM((2, rows, width), bf16),
    )

    def grad_copy(d, s):
        at = pl.ds(pl.multiple_of(s * span, span), span)
        return remote(
            grad_made.at[partner[d], at], grad_land.at[me, at],
            grad_send.at[d, s], grad_recv.at[d, s], partner[d],
        )

    own_grad = pltpu.make_async_copy(grad_made.at[me], grad_land.at[me], self_sem.at[2])

    def norm_backward(partials, hidden, cot, output):
        loads = [
            pltpu.make_async_copy(partial_ref, partials.at[pl.ds(0, chips - 1)], load_sem.at[0]),
            pltpu.make_async_copy(hidden_ref, hidden, load_sem.at[1]),
            pltpu.make_async_copy(cot_ref, cot, load_sem.at[2]),
            pltpu.make_async_copy(output_ref, output, load_sem.at[3]),
        ]
        for copy in loads:
            copy.start()
        late_copy(0).wait_recv()
        late_copy(1).wait_recv()
        last = pltpu.make_async_copy(late_land, partials.at[chips - 1], load_sem.at[4])
        last.start()
        ticks(1)
        for copy in loads[:3] + [last]:
            copy.wait()

        @pl.loop(0, rows // 32)
        def _(i):
            at = pl.ds(pl.multiple_of(i * 32, 32), 32)
            grad = partials[0, at].astype(f32)
            for d in range(1, chips):
                grad = grad + partials[d, at].astype(f32)
            scale = scale_ref[at]
            unit = hidden[at] * scale
            scaled = grad * gain_ref[...]
            level = jnp.mean(scaled * unit, -1, keepdims=True)
            result = cot[at].astype(f32) + scale * (scaled - unit * level)
            hidden[at] = result
            branch[at] = result.astype(bf16)

        keep = pltpu.make_async_copy(hidden, hidden_out, load_sem.at[1])
        keep.start()
        ticks(1)
        loads[3].wait()

        @pl.loop(0, shards)
        def _(k):
            grad_made[k] = dot_nt(branch[...], output[k]).astype(bf16)

        own_grad.start()
        for s in range(seqs):
            for d in range(1, shards):
                grad_copy(d, s).start()
        keep.wait()

    pl.run_scoped(
        norm_backward,
        pltpu.VMEM((chips, rows, width), bf16),
        pltpu.VMEM((rows, width), f32),
        pltpu.VMEM((rows, width), bf16),
        pltpu.VMEM((shards, owned, width), bf16),
    )

    def turn_copy(turned, d, s):
        at = pl.ds(pl.multiple_of(s * span, span), span)
        return remote(
            turned.at[s, partner[d]], turn_land.at[me, at],
            turn_send.at[d, s], turn_recv.at[d, s], partner[d],
        )

    def attention(qkv, grads, turned, sums, turned_all, normed, attn, sent, weight, one):
        loads = [
            pltpu.make_async_copy(normed_ref, normed, load_sem.at[0]),
            pltpu.make_async_copy(attn_ref, attn, load_sem.at[1]),
        ]
        for copy in loads:
            copy.start()
        own_grad.wait()
        half_owned = owned // 2

        def part_of(index):
            return pl.ds(index * half_owned, half_owned)

        def scatter_steps(which, product, core_land, relay_land, sum_land):
            wide_of = core_land.shape[2]

            def core_copy(d):
                return remote(
                    sent.at[d, :, pl.ds(0, wide_of)], core_land.at[d],
                    core_send.at[which, d], core_recv.at[which, d], partner[1],
                )

            def sum_copy(d, index):
                return remote(
                    core_land.at[d, part_of(index)], sum_land.at[d, part_of(index)],
                    sum_send.at[which, d, index], sum_recv.at[which, d, index], partner[2 * d],
                )

            def relay_copy(index):
                return remote(
                    core_land.at[3, part_of(index)], relay_land.at[index],
                    relay_send.at[which, index], relay_recv.at[which, index],
                    partner[2 * (index + 1)],
                )

            order = list(range(chips - 1, -1, -1))

            def near():
                for d in order:
                    for place, value in product(chip_at(chip, d) * 2 + 1 - core):
                        sent[d, :, place] = value.astype(bf16)
                    core_copy(d).start()

            def far():
                for d in order:
                    core_copy(d).wait_recv()
                    for place, value in product(chip_at(chip, d) * 2 + core):
                        core_land[d, :, place] = (
                            core_land[d, :, place].astype(f32) + value
                        ).astype(bf16)
                    if relay and d == 3:
                        relay_copy(0).start()
                        relay_copy(1).start()
                    elif d > 0:
                        for index in range(2):
                            if not relay or index != 2 - d:
                                sum_copy(d, index).start()
                for d in range(chips):
                    core_copy(d).wait_send()

            def onward():
                for index in range(2 if relay else 0):
                    relay_copy(index).wait_recv()
                    at = part_of(index)
                    core_land[2 - index, at] = (
                        core_land[2 - index, at].astype(f32) + relay_land[index].astype(f32)
                    ).astype(bf16)
                    sum_copy(2 - index, index).start()

            def arrive(first):
                direct = range(1, 3 if relay else chips)
                for d in direct:
                    for index in range(2):
                        sum_copy(d, index).wait_recv()
                gets = [
                    pltpu.make_async_copy(
                        sum_land.at[d], sent.at[d, :, pl.ds(0, wide_of)], load_sem.at[2 + d]
                    )
                    for d in direct
                ]
                for copy in gets:
                    copy.start()
                for copy in gets:
                    copy.wait()
                count = wide_of // units
                for k in range(count):
                    columns = slice(k * units, (k + 1) * units)
                    value = core_land[0, :, columns].astype(f32)
                    for d in direct:
                        value = value + sent[d, :, columns].astype(f32)
                    sent[0, :, columns] = value.astype(bf16)
                puts = [
                    pltpu.make_async_copy(
                        sent.at[0, :, pl.ds(k * units, units)], total.at[first + k],
                        total_sem.at[first + k],
                    )
                    for k in range(count)
                ]
                for put in puts:
                    put.start()
                for k, put in enumerate(puts):
                    put.wait()
                    from_end(last_inner + first + k)

            def leave():
                for index in range(2 if relay else 0):
                    relay_copy(index).wait_send()
                for d in range(1, 3 if relay else chips):
                    for index in range(2):
                        sum_copy(d, index).wait_send()

            return near, far, onward, arrive, leave

        def rows_for(owner):
            return pl.ds(pl.multiple_of(owner * owned, owned), owned)

        def out_product(owner):
            left = attn[:, rows_for(owner)]
            for k in range(out_chunks):
                at = slice(k * units, (k + 1) * units)
                yield at, outer_sum(left, branch[:, at])

        def qkv_product(owner):
            left = normed[:, rows_for(owner)]
            for k in range(shards):
                value = outer_sum(left, turned_all[k])
                key_at = shards * wide + k * HEAD_DIM
                value_at = key_at + shards * HEAD_DIM
                yield slice(k * wide, (k + 1) * wide), value[:, :wide]
                yield slice(key_at, key_at + HEAD_DIM), value[:, wide : wide + HEAD_DIM]
                yield slice(value_at, value_at + HEAD_DIM), value[:, wide + HEAD_DIM :]

        out_scatter = scatter_steps(0, out_product, core_out, relay_out, sum_out)
        qkv_scatter = scatter_steps(1, qkv_product, core_qkv, relay_qkv, sum_qkv)
        loads[1].wait()
        out_scatter[0]()
        ticks(1)
        out_scatter[1]()
        ticks(down_chunks - position[0])

        def own_turn(s):
            at = pl.ds(pl.multiple_of(s * span, span), span)
            return pltpu.make_async_copy(turned.at[s, me], turn_land.at[me, at], seq_sem.at[2 + s])

        @pl.loop(0, seqs)
        def _(s):
            for d in range(1, shards):
                grad_copy(d, s).wait_recv()
            at = pl.ds(pl.multiple_of(s * span, span), span)
            takes = [
                pltpu.make_async_copy(qkv_ref.at[:, s], qkv, seq_sem.at[0]),
                pltpu.make_async_copy(grad_land.at[:, at], grads, seq_sem.at[1]),
            ]
            for copy in takes:
                copy.start()
            for copy in takes:
                copy.wait()
            attention_back(
                heads, 256, qkv, grads, norm_ref.at[s], seg_col_ref[s], seg_row_ref[s],
                cos_ref.at[s], sin_ref.at[s], turned.at[s], sums,
                between=lambda: later_tick(down_chunks + 2 * s) if line else None,
            )
            own_turn(s).start()
            for d in range(1, shards):
                turn_copy(turned, d, s).start()
            if line:
                later_tick(down_chunks + 1 + 2 * s)

        if line:
            position[0] = down_chunks + 2 * seqs
            settled[0] = up_first
        start_inner(1)
        ticks(1)
        for s in range(seqs):
            own_turn(s).wait()
            for d in range(1, shards):
                turn_copy(turned, d, s).wait_recv()
        take = pltpu.make_async_copy(turn_land, turned_all, load_sem.at[2])
        take.start()
        weight_load(weight, 0).start()
        ticks(1)
        loads[0].wait()
        take.wait()

        qkv_scatter[0]()
        ticks(1)
        qkv_scatter[1]()
        ticks(1)
        out_scatter[2]()
        qkv_scatter[2]()

        def rows_of(index):
            return pl.ds(index * half_rows, half_rows)

        def part_copy(d, index):
            return remote(
                outs_ref.at[chip_at(chip, d), rows_of(index)], out_land.at[d, rows_of(index)],
                part_send.at[d, index], part_recv.at[d, index], partner[2 * d],
            )

        def pass_copy(index):
            return remote(
                outs_ref.at[chip_at(chip, 3), rows_of(index)], pass_land.at[index],
                pass_send.at[index], pass_recv.at[index], partner[2 * (index + 1)],
            )

        if relay:
            pass_copy(0).start()
            pass_copy(1).start()
            part_copy(1, 0).start()
            part_copy(2, 1).start()
        else:
            for d in range(1, chips):
                for index in range(2):
                    part_copy(d, index).start()

        def one_copy(k):
            at = pl.ds(k * owned, owned)
            return pltpu.make_async_copy(one.at[k % 2], one_out.at[:, at], one_sem.at[2 + k % 2])

        for k in range(shards):
            weight_load(weight, k).wait()
            if k + 1 < shards:
                weight_load(weight, k + 1).start()
            if k >= 2:
                one_copy(k - 2).wait()
            value = dot_nt(turned_all[0], weight[k % 2, :, :part])
            for j in range(1, shards):
                value = value + dot_nt(
                    turned_all[j], weight[k % 2, :, j * part : (j + 1) * part]
                )
            one[k % 2] = value
            one_copy(k).start()
            if k % 2 == 1:
                ticks(1)
            if k == 3:
                out_scatter[3](0)
        one_copy(shards - 2).wait()
        one_copy(shards - 1).wait()

        if relay:
            for index in range(2):
                pass_copy(index).wait_recv()
                at = rows_of(index)
                gets = [
                    pltpu.make_async_copy(
                        outs_ref.at[chip_at(chip, 2 - index), at], normed.at[rows_of(0)],
                        load_sem.at[0],
                    ),
                    pltpu.make_async_copy(
                        pass_land.at[index], normed.at[rows_of(1)], load_sem.at[1]
                    ),
                ]
                for copy in gets:
                    copy.start()
                for copy in gets:
                    copy.wait()
                attn[at] = (
                    normed[rows_of(0)].astype(f32) + normed[rows_of(1)].astype(f32)
                ).astype(bf16)
                remote(
                    attn.at[at], out_land.at[2 - index, at],
                    part_send.at[2 - index, index], part_recv.at[2 - index, index],
                    partner[2 * (2 - index)],
                ).start()
                ticks(1)
        ticks(last_inner - 4 - position[0])
        qkv_scatter[3](out_chunks)
        ticks(last_inner)
        for k in range(across):
            middle(last_inner + k)
        if line:

            @pl.when(is_inner)
            def _():
                send_out(chunks - 1)

        for s in range(seqs):
            for d in range(1, shards):
                turn_copy(turned, d, s).wait_send()
        out_scatter[4]()
        qkv_scatter[4]()
        if relay:
            for index in range(2):
                pass_copy(index).wait_send()
        for d in range(1, 3 if relay else chips):
            for index in range(2):
                part_copy(d, index).wait_send()
                part_copy(d, index).wait_recv()

    def weight_load(weight, k):
        return pltpu.make_async_copy(weight_ref.at[k], weight.at[k % 2], one_sem.at[k % 2])

    pl.run_scoped(
        attention,
        pltpu.VMEM((shards, span, part), bf16),
        pltpu.VMEM((shards, span, wide), bf16),
        pltpu.VMEM((seqs, shards, span, part), bf16),
        pltpu.VMEM((2, shards * span, HEAD_DIM), f32),
        pltpu.VMEM((shards, rows, part), bf16),
        pltpu.VMEM((rows, width), bf16),
        pltpu.VMEM((rows, width), bf16),
        pltpu.VMEM((chips, owned, qkv_width), bf16),
        pltpu.VMEM((2, owned, qkv_width), bf16),
        pltpu.VMEM((2, rows, owned), f32),
    )

    late_copy(0).wait_send()
    late_copy(1).wait_send()
    for s in range(seqs):
        for d in range(1, shards):
            grad_copy(d, s).wait_send()
    for which in range(2):
        for d in range(1, shards):
            inner_copy(which, d).wait_send()
    if line:

        @pl.when(is_inner)
        def _():
            for c in range(chunks - 4, chunks):
                mid_copy(c).wait_send()
            for c in (chunks - 2, chunks - 1):
                out_copy(c).wait_send()
                keep_copy(c).wait()

        @pl.when(jnp.logical_not(is_inner))
        def _():
            for c in range(chunks):
                end_copy(c).wait_send()
                out_copy(c).wait_recv()


def tail(
    heads, normed_all, cot_all, mixed, gate, up, partials, late, outs,
    hidden, cot, output, weight, qkv, normed, attn, *tables,
):
    shards, seqs, span, part = qkv.shape
    rows, width = normed.shape
    chips = shards // 2
    units = mixed.shape[1] // 2
    owned = width // shards
    wide = heads * HEAD_DIM
    full = shards * part + width
    across = full // units
    chunks = (units // owned) * (width // units) + 2 * shards + across
    tiles = width // rows
    hbm = pl.BlockSpec(memory_space=pl.ANY)
    vmem = pl.BlockSpec(memory_space=pltpu.VMEM)
    dma = pltpu.SemaphoreType.DMA

    def low(*shape):
        return jax.ShapeDtypeStruct(shape, bf16)

    def high(*shape):
        return jax.ShapeDtypeStruct(shape, f32)

    pieces = low(chunks, owned, units)
    out_shape = (
        low(units, width), low(2, width, units), low(units, width), low(2, width, units),
        low(rows, width), high(rows, width),
        low(2, shards, owned, units), low(shards, rows, wide), low(shards, rows, part),
        pieces, pieces, low(chips, owned, width), low(chips, owned, shards * part),
        low(2, rows // 2, width), low(*outs.shape),
        low(across, owned, units), high(rows, width),
        low(units, width), low(owned, shards * units), low(owned, shards * units), low(owned, full),
    )
    length = shards * span
    return pl.pallas_call(
        functools.partial(tail_kernel, heads),
        in_specs=[hbm] * 15 + [vmem] * 7,
        out_specs=(hbm,) * len(out_shape),
        out_shape=out_shape,
        scratch_shapes=[
            pltpu.VMEM((rows, width), bf16),
            pltpu.VMEM((shards, rows, wide), bf16),
            pltpu.VMEM((chips, owned, width), bf16),
            pltpu.VMEM((chips, owned, shards * part), bf16),
            pltpu.VMEM((2, owned // 2, width), bf16),
            pltpu.VMEM((2, owned // 2, shards * part), bf16),
            pltpu.VMEM((owned, units), bf16),
            pltpu.VMEM((2, owned, units), bf16),
            pltpu.VMEM((4, owned, units), bf16),
            pltpu.VMEM((2, owned, units), bf16),
            dma((3, tiles)), dma((3, tiles)), dma((2,)), dma((2,)),
            dma((2, shards)), dma((2, shards)), dma((shards, seqs)), dma((shards, seqs)),
            dma((shards, seqs)), dma((shards, seqs)), dma((2, chips)), dma((2, chips)),
            dma((2, chips, 2)), dma((2, chips, 2)), dma((chips, 2)), dma((chips, 2)),
            dma((chunks,)), dma((chunks,)), dma((chunks,)), dma((chunks,)), dma((chunks,)),
            dma((chunks,)), dma((2, 2)), dma((2, 2)), dma((2,)), dma((2,)),
            dma((3 + 3 * chips,)), dma((3, tiles)), dma(()), dma((3,)), dma((5 + chips,)),
            dma((2 + seqs,)), dma((3,)), dma((2,)), dma((across,)), dma((4,)),
        ],
        compiler_params=pltpu.CompilerParams(
            collective_id=1, has_side_effects=True, vmem_limit_bytes=63 * 2**20
        ),
        cost_estimate=pl.CostEstimate(
            flops=10 * seqs * heads * length * length * HEAD_DIM + 6 * chips * rows * width * width,
            bytes_accessed=2**29,
            transcendentals=seqs * heads * length * length,
        ),
    )(
        normed_all, cot_all, mixed, gate, up, partials, late, outs,
        hidden, cot, output, weight, qkv, normed, attn, *tables,
    )


def norm_back(grad_normed, unit_rows, scale_rows, gain_rows):
    scaled_grad = grad_normed * gain_rows
    return scale_rows * (
        scaled_grad - unit_rows * jnp.mean(scaled_grad * unit_rows, -1, keepdims=True)
    )


def body(
    tokens,
    segments,
    positions,
    cotangent,
    attention_gain,
    query_weight,
    key_weight,
    value_weight,
    output_weight,
    mlp_gain,
    gate_weight,
    up_weight,
    down_weight,
):
    seqs, span, width = tokens.shape
    shards = lax.axis_size("shard")
    me = lax.axis_index("shard")
    rows = seqs * span
    length = shards * span
    owned = query_weight.shape[0]
    heads = HEADS // shards
    copies = max(1, shards // KV_HEADS)
    wide = heads * HEAD_DIM
    part = wide + 2 * HEAD_DIM
    hidden_share = down_weight.shape[0]

    chips = shards // 2
    replicas = lax.axis_size("replica")
    swap = [(i, i + 1 - 2 * (i % 2)) for i in range(shards)]

    share = owned // replicas
    units = 2 * hidden_share
    share_own = lax.dynamic_slice_in_dim(
        jnp.stack([gate_weight, up_weight]), lax.axis_index("replica") * share, share, 1
    )
    share_own = jnp.transpose(share_own.reshape(2, share, chips, units), (2, 0, 1, 3))
    down_other = lax.ppermute(down_weight, "shard", swap)

    def per_head(weight):
        return jnp.repeat(weight.reshape(owned, KV_HEADS, HEAD_DIM), copies, axis=1)

    qkv_owned = jnp.concatenate(
        [query_weight.reshape(owned, shards, wide), per_head(key_weight), per_head(value_weight)],
        -1,
    ).reshape(owned, shards * part)

    angle = angles(positions).reshape(rows, HEAD_DIM // 2)
    cosine, sine = jnp.cos(angle), jnp.sin(angle)
    still = jnp.ones((rows, HEAD_DIM), f32)
    cos_lanes = jnp.concatenate([cosine] * (2 * heads + 2) + [still], 1)
    sin_lanes = jnp.concatenate([-sine, sine] * (heads + 1) + [still * 0.0], 1)
    small_gains = jnp.stack([attention_gain, mlp_gain]).astype(f32)
    small_places = jnp.stack([segments, positions]).astype(f32)
    (
        shares, qkv_full, output_full, qkv, attn, normed_one, hidden, normed_two,
        norms, scale_two, gains, places, seg_col, seg_row,
    ) = head(
        heads, share_own, qkv_owned, output_weight, tokens.reshape(rows, width), small_gains,
        small_places, cos_lanes, sin_lanes,
    )
    gain_one, gain_two = gains[:, 0].reshape(width), gains[:, 1].reshape(width)
    spots = jnp.swapaxes(places[:, 1], 0, 1).reshape(seqs, length)
    angle_all = jnp.swapaxes(angles(spots), 1, 2)
    cos_all, sin_all = jnp.cos(angle_all), jnp.sin(angle_all)

    x = tokens.reshape(rows, width).astype(f32)
    scale_one = lax.rsqrt(jnp.mean(x * x, -1, keepdims=True) + epsilon)
    unit_one = x * scale_one

    cot_rows = cotangent.reshape(rows, width)
    normed_all, cot_all, partials, late, outs, mixed, gate, up = feed_forward(
        normed_two, cot_rows, shares, down_weight, down_other
    )
    results = tail(
        heads, normed_all, cot_all, mixed, gate, up, partials, late, outs, hidden, cot_rows,
        output_full, qkv_full, qkv, normed_one, attn, scale_two, gain_two[None], norms, seg_col,
        seg_row, cos_all, sin_all,
    )
    down_part, grad_hidden, inner_blocks = results[0], results[5], results[6]
    out_land, total, grad_one, summed = results[14], results[15], results[16], results[17:]
    out_sum = lax.dynamic_index_in_dim(outs, me // 2, 0, keepdims=False).astype(f32)
    arrived = 3 if chips == 4 else chips
    out_sum = out_sum + jnp.sum(out_land[1:arrived].astype(f32), 0)
    block_out = (hidden + out_sum).astype(bf16)

    if replicas != 4:

        def side_by_side(some):
            return jnp.swapaxes(some, 0, 1).reshape(owned, some.shape[0] * hidden_share)

        out_blocks = width // hidden_share
        rest_blocks = jnp.concatenate([total[out_blocks:], total[:out_blocks]])
        summed = lax.psum(
            (
                down_part, side_by_side(inner_blocks[0]), side_by_side(inner_blocks[1]),
                side_by_side(rest_blocks),
            ),
            "replica",
        )
    down_grad, gate_grad, up_grad, rest = [some.astype(f32) for some in summed]
    key_at, value_at = shards * wide, shards * (wide + HEAD_DIM)
    output_grad = rest[:, shards * part :]

    def kv_grad(columns):
        return jnp.sum(columns.reshape(owned, KV_HEADS, copies, HEAD_DIM), 2).reshape(
            owned, KV_HEADS * HEAD_DIM
        )

    query_grad = rest[:, :key_at]
    key_grad = kv_grad(rest[:, key_at:value_at])
    value_grad = kv_grad(rest[:, value_at : shards * part])

    own_one, own_two = attention_gain.astype(f32), mlp_gain.astype(f32)
    gain_one_grad = (
        jnp.sum(query_weight.astype(f32) * query_grad, 1)
        + jnp.sum(key_weight.astype(f32) * key_grad + value_weight.astype(f32) * value_grad, 1)
    ) / own_one
    gain_two_grad = (
        jnp.sum(gate_weight.astype(f32) * gate_grad + up_weight.astype(f32) * up_grad, 1) / own_two
    )
    token_grad = grad_hidden + norm_back(grad_one, unit_one, scale_one, gain_one)
    return (
        block_out.reshape(seqs, span, width),
        token_grad.reshape(seqs, span, width),
        gain_one_grad,
        query_grad,
        key_grad,
        value_grad,
        output_grad,
        gain_two_grad,
        gate_grad,
        up_grad,
        down_grad,
    )


def solution(mesh):
    rows = P("shard", None)
    blocks = P("replica", "shard", None)
    in_specs = (
        blocks, P("replica", "shard"), P("replica", "shard"), blocks, P("shard"),
        rows, rows, rows, rows, P("shard"), rows, rows, rows,
    )
    out_specs = (
        blocks, blocks, P("shard"), rows, rows, rows, rows, P("shard"), rows, rows, rows,
    )
    return jax.shard_map(body, mesh=mesh, in_specs=in_specs, out_specs=out_specs, check_vma=False)
```
